32 devices in a mesh: dp: 8 (over z, x), seq: 4 (over y, core).
Axes of the slice: x: 2, y: 2, z: 4, core: 2. Of those that a mesh axis runs over, the one named last changes fastest.
Arguments:
- tokens: bfloat16 [16, 1024, 1152], P('dp', 'seq'), may hold values from -6 to 6
- conditioning: float32 [16, 1152], P('dp'), may hold values from -6 to 6
- w_mod: bfloat16 [1152, 6912], P('dp'), may hold values from -0.1875 to 0.1875
- b_mod: bfloat16 [6912], P('dp'), may hold values from -3 to 3
- w_qkv: bfloat16 [1152, 3456], P('dp'), may hold values from -0.1875 to 0.1875
- w_proj: bfloat16 [1152, 1152], P('dp'), may hold values from -1 to 1
- w_fc1: bfloat16 [1152, 4608], P('dp'), may hold values from -0.1875 to 0.1875
- b_fc1: bfloat16 [4608], P('dp'), may hold values from -3 to 3
- w_fc2: bfloat16 [4608, 1152], P('dp'), may hold values from -0.09375 to 0.09375
- cotangent: bfloat16 [16, 1024, 1152], P('dp', 'seq'), may hold values from -6 to 6
Outputs:
- output: bfloat16 [16, 1024, 1152], P('dp', 'seq')
- grad_tokens: float32 [16, 1024, 1152], P('dp', 'seq')
- grad_cond: float32 [16, 1152], P('dp')
- grad_w_mod: float32 [1152, 6912], P(None, ('dp', 'seq'))
- grad_b_mod: float32 [6912], P(('dp', 'seq'))
- grad_w_qkv: float32 [1152, 3456], P('dp', 'seq')
- grad_w_proj: float32 [1152, 1152], P('dp', 'seq')
- grad_w_fc1: float32 [1152, 4608], P('dp', 'seq')
- grad_b_fc1: float32 [4608], P(('dp', 'seq'))
- grad_w_fc2: float32 [4608, 1152], P('dp', 'seq')
The draws below stay inside these ranges and needn't reach their ends.
All inputs are finite; a program needn't handle non-finite values.
Results may differ from the reference program's by a relative error of at most 0.02.
The reference program's roundings to bfloat16 on the way count: a program that leaves them out, or rounds other values in their place, can miss the bound.
Values may be sent and summed in bfloat16 or wider, within the bound.
No kernel may reach another device: no remote copies, remote signals or barrier semaphores. Data moves between devices by JAX's collectives and lax.ppermute only.
A program may use at most 256 MiB of HBM per device.

```python
import jax
import jax.numpy as jnp
from jax import lax

D = 1152
HEADS = 16
HEAD_DIM = 72
FF = 4608
SEQ_LEN = 1024
LATENTS = 16


def levels(stream_key, extent, cuts, low, largest):
    factor_of = 1.0
    for position, blocks in cuts:
        steps = jax.random.uniform(jax.random.fold_in(jax.random.fold_in(stream_key, 6), position), (blocks,), jnp.float32, low / len(cuts), largest / len(cuts))
        factor_of = factor_of * jnp.repeat(jnp.exp(steps), extent[position] // blocks).reshape((-1,) + (1,) * (len(extent) - 1 - position))
    return factor_of


def noise(stream_key, shape, scale, reach, pieces=(), dtype=jnp.bfloat16):
    loudness = levels(stream_key, shape, pieces, -0.22, 0.18) if pieces else 1.0
    values = jax.random.normal(stream_key, shape, jnp.float32) * scale * loudness
    return jnp.minimum(jnp.maximum(values, -reach), reach).astype(dtype)


def setup_inputs(seed: int = 0) -> dict:
    arg_keys = jax.random.split(jax.random.key(seed), 11)
    tokens = noise(arg_keys[0], (LATENTS, SEQ_LEN, D), 1.0, 6.0, ((0, 8), (1, 4)))
    conditioning = noise(arg_keys[1], (LATENTS, D), 1.0, 6.0, ((0, 8),), jnp.float32)
    w_mod = noise(arg_keys[2], (D, 6 * D), D ** -0.5, 0.1875, ((0, 8),))
    b_mod = noise(arg_keys[3], (6 * D,), 0.5, 3.0, ((0, 8),))
    w_qkv = noise(arg_keys[4], (D, 3 * D), D ** -0.5, 0.1875, ((0, 8),))
    w_proj = noise(arg_keys[5], (D, D), (D // 32) ** -0.5, 1.0, ((0, 8),))
    w_fc1 = noise(arg_keys[6], (D, FF), D ** -0.5, 0.1875, ((0, 8),))
    b_fc1 = noise(arg_keys[7], (FF,), 0.5, 3.0, ((0, 8),))
    w_fc2 = noise(arg_keys[8], (FF, D), FF ** -0.5, 0.09375, ((0, 8),))
    cotangent = noise(arg_keys[9], (LATENTS, SEQ_LEN, D), 1.0, 6.0, ((0, 8), (1, 4)))
    return {"tokens": tokens, "conditioning": conditioning, "w_mod": w_mod, "b_mod": b_mod, "w_qkv": w_qkv, "w_proj": w_proj, "w_fc1": w_fc1, "b_fc1": b_fc1, "w_fc2": w_fc2, "cotangent": cotangent}


@jax.custom_vjp
def low(v):
    return lax.optimization_barrier(v.astype(jnp.bfloat16)).astype(jnp.float32)

@jax.custom_vjp
def low_back(v):
    return v

def low_keep(v):
    return (low(v), None)

def low_pass(kept, grad):
    return (grad,)

def back_keep(v):
    return (v, None)

def back_low(kept, grad):
    return (low(grad),)
low.defvjp(low_keep, low_pass)
low_back.defvjp(back_keep, back_low)

def matmul_high(left, right):
    return jnp.matmul(left, right, precision=lax.Precision.HIGHEST)

def layer_norm(values):
    row_mean = lax.optimization_barrier(jnp.mean(values, axis=-1, keepdims=True))
    centred = values - row_mean
    row_var = lax.optimization_barrier(jnp.mean(centred * centred, axis=-1, keepdims=True))
    return centred * lax.rsqrt(row_var + 1e-06)

def attend(packed):
    inv_root = HEAD_DIM ** (-0.5)
    parts = packed.reshape(SEQ_LEN, 3, HEADS, HEAD_DIM)
    queries = parts[:, 0]
    key_rows = parts[:, 1]
    values = parts[:, 2]
    scores = low_back(jnp.einsum('qhd,khd->hqk', queries, key_rows, precision=lax.Precision.HIGHEST) * inv_root)
    row_max = lax.optimization_barrier(jnp.max(scores, axis=-1, keepdims=True))
    exponent = jnp.exp(scores - row_max)
    weights = exponent / lax.optimization_barrier(jnp.sum(exponent, axis=-1, keepdims=True))
    mixed = jnp.einsum('hqk,khd->qhd', low(weights), values, precision=lax.Precision.HIGHEST)
    mixed = low(low_back(mixed))
    return mixed.reshape(SEQ_LEN, HEADS * HEAD_DIM)

def block_forward(tokens, conditioning, w_mod, b_mod, w_qkv, w_proj, w_fc1, b_fc1, w_fc2):
    cond_act = low(jax.nn.silu(conditioning))
    modulation = low_back(matmul_high(cond_act, w_mod) + b_mod)
    shift_attn, scale_attn, gate_attn, shift_mlp, scale_mlp, gate_mlp = jnp.split(modulation, 6, axis=-1)
    normed_attn = low(layer_norm(tokens) * (1.0 + scale_attn[:, None]) + shift_attn[:, None])
    packed = low(low_back(matmul_high(normed_attn, w_qkv)))
    attended = lax.map(jax.checkpoint(attend), packed)
    attn_out = low_back(matmul_high(attended, w_proj))
    resid_mid = tokens + gate_attn[:, None] * attn_out
    normed_mlp = low(layer_norm(resid_mid) * (1.0 + scale_mlp[:, None]) + shift_mlp[:, None])
    hidden = low_back(matmul_high(normed_mlp, w_fc1) + b_fc1)
    activated = low(jax.nn.gelu(hidden, approximate=True))
    mlp_out = low_back(matmul_high(activated, w_fc2))
    return resid_mid + gate_mlp[:, None] * mlp_out

def reference(tokens, conditioning, w_mod, b_mod, w_qkv, w_proj, w_fc1, b_fc1, w_fc2, cotangent):
    primals = [element.astype(jnp.float32) for element in (tokens, conditioning, w_mod, b_mod, w_qkv, w_proj, w_fc1, b_fc1, w_fc2)]
    result, pullback = jax.vjp(block_forward, *primals)
    gradients = pullback(cotangent.astype(jnp.float32))
    return (result.astype(jnp.bfloat16), gradients[0], gradients[1], gradients[2], gradients[3], gradients[4], gradients[5], gradients[6], gradients[7], gradients[8])
```

```python
from functools import partial

import jax
import jax.numpy as jnp
from jax import lax
from jax.sharding import PartitionSpec as P

HEADS = 16
HEAD_DIM = 72
BF = jnp.bfloat16
F32 = jnp.float32
GELU_C = 0.7978845608028654
GELU_A = 0.044715


def hop(value, axis, bits):
    count = lax.axis_size(axis)
    return lax.ppermute(value, axis, [(i, i ^ bits) for i in range(count)])


def matmul(left, right):
    return jnp.dot(left, right, preferred_element_type=F32)


def matmul_nt(left, right):
    return lax.dot_general(left, right, (((1,), (1,)), ((), ())), preferred_element_type=F32)


def matmul_tn(left, right):
    return lax.dot_general(left, right, (((0,), (0,)), ((), ())), preferred_element_type=F32)


def ln_parts(values):
    row_mean = jnp.mean(values, axis=-1, keepdims=True)
    centred = values - row_mean
    row_var = jnp.mean(centred * centred, axis=-1, keepdims=True)
    inv_std = lax.rsqrt(row_var + 1e-06)
    return centred * inv_std, inv_std


def ln_backward(grad, normed, inv_std):
    mean_grad = jnp.mean(grad, axis=-1, keepdims=True)
    mean_inner = jnp.mean(grad * normed, axis=-1, keepdims=True)
    return (grad - mean_grad - normed * mean_inner) * inv_std


def seq_gather(mine):
    slots = {0: mine}
    bit = lax.axis_size("seq") // 2
    while bit:
        for j in list(slots):
            slots[j | bit] = hop(slots[j], "seq", bit)
        bit //= 2
    return [slots[j] for j in range(len(slots))]


def seq_reduce(slots):
    slots = dict(enumerate(slots))
    bit = 1
    while len(slots) > 1:
        for j in [j for j in slots if j & bit]:
            slots[j ^ bit] = slots[j ^ bit] + hop(slots.pop(j).astype(BF), "seq", bit).astype(F32)
        bit *= 2
    return slots[0]


def seq_exchange(blocks):
    return [blocks[0]] + [hop(blocks[j], "seq", j) for j in range(1, len(blocks))]


def dp_exchange(value):
    return lax.all_to_all(value, "dp", 0, 0, tiled=True)


GATHER = "sc"
SCATTER = "sc"


def dp_gather(mine):
    if GATHER == "sc":
        return lax.all_gather(mine, "dp", axis=0, tiled=True)
    count = lax.axis_size("dp")
    index = lax.axis_index("dp")
    rows = mine.shape[0]
    slots = {0: mine}
    for j in range(2, count, 2):
        slots[j] = hop(mine, "dp", j)
    for j in range(0, count, 2):
        slots[j + 1] = hop(slots[j], "dp", 1)
    whole = jnp.zeros((count * rows,) + mine.shape[1:], mine.dtype)
    for j in range(count):
        whole = lax.dynamic_update_slice(whole, slots[j], ((index ^ j) * rows, 0))
    return whole


def dp_scatter(terms):
    if SCATTER == "sc":
        return lax.psum_scatter(terms, "dp", scatter_dimension=0, tiled=True).astype(F32)
    count = lax.axis_size("dp")
    index = lax.axis_index("dp")
    rows = terms.shape[0] // count

    def block(j):
        return lax.dynamic_slice(terms, ((index ^ j) * rows, 0), (rows, terms.shape[1]))

    half = {}
    for j in list(range(2, count, 2)) + [0]:
        half[j] = block(j).astype(F32) + hop(block(j + 1), "dp", 1).astype(F32)
    total = half[0]
    for j in range(2, count, 2):
        total = total + hop(half[j].astype(BF), "dp", j).astype(F32)
    return total


def attend_forward(packed):
    inv_root = HEAD_DIM ** (-0.5)
    queries = packed[:, 0]
    key_rows = packed[:, 1]
    values = packed[:, 2]
    scores = (
        jnp.einsum("qhd,khd->hqk", queries, key_rows, preferred_element_type=jnp.float32) * inv_root
    )
    row_max = jnp.max(scores, axis=-1, keepdims=True)
    exponent = jnp.exp(scores - row_max)
    row_sum = jnp.sum(exponent, axis=-1, keepdims=True)
    weights = (exponent / row_sum).astype(jnp.bfloat16)
    mixed = jnp.einsum("hqk,khd->qhd", weights, values, preferred_element_type=jnp.float32)
    seq_len = mixed.shape[0]
    heads_here = mixed.shape[1]
    mixed = mixed.reshape(seq_len, heads_here * HEAD_DIM).astype(jnp.bfloat16)
    return (mixed, (row_max + jnp.log(row_sum))[..., 0])


def attend_backward(group):
    packed, log_sum, d_mixed = group
    inv_root = HEAD_DIM ** (-0.5)
    queries = packed[:, 0]
    key_rows = packed[:, 1]
    values = packed[:, 2]
    scores = (
        jnp.einsum("qhd,khd->hqk", queries, key_rows, preferred_element_type=jnp.float32) * inv_root
    )
    weights = jnp.exp(scores - log_sum[..., None])
    d_values = jnp.einsum(
        "hqk,qhd->khd", weights.astype(jnp.bfloat16), d_mixed, preferred_element_type=jnp.float32
    )
    d_weights = jnp.einsum("qhd,khd->hqk", d_mixed, values, preferred_element_type=jnp.float32)
    row_inner = jnp.sum(weights * d_weights, axis=-1, keepdims=True)
    d_scores = (weights * (d_weights - row_inner)).astype(jnp.bfloat16)
    d_queries = (
        jnp.einsum("hqk,khd->qhd", d_scores, key_rows, preferred_element_type=jnp.float32)
        * inv_root
    )
    d_keys = (
        jnp.einsum("hqk,qhd->khd", d_scores, queries, preferred_element_type=jnp.float32) * inv_root
    )
    stacked = jnp.stack([d_queries, d_keys, d_values], axis=1)
    seq_len = stacked.shape[0]
    heads_here = stacked.shape[2]
    return stacked.reshape(seq_len, 3 * heads_here * HEAD_DIM).astype(jnp.bfloat16)


def attention(packed, heads_here):
    lat, seq_len, _ = packed.shape
    return lax.map(attend_forward, packed.reshape(lat, seq_len, 3, heads_here, HEAD_DIM))


def attention_grad(packed, mixed, log_sums, d_mixed, heads_here):
    lat, seq_len, _ = packed.shape
    return lax.map(
        attend_backward,
        (
            packed.reshape(lat, seq_len, 3, heads_here, HEAD_DIM),
            log_sums,
            d_mixed.reshape(lat, seq_len, heads_here, HEAD_DIM),
        ),
    )


def on_device(tokens, conditioning, w_mod, b_mod, w_qkv, w_proj, w_fc1, b_fc1, w_fc2, cotangent):
    lat, tok, width = tokens.shape
    seq_n = lax.axis_size("seq")
    dp_n = lax.axis_size("dp")
    seq = lax.axis_index("seq")
    dp = lax.axis_index("dp")
    core = seq % 2
    heads_here = HEADS // seq_n
    cols = heads_here * HEAD_DIM
    seq_len = tok * seq_n
    rows = w_qkv.shape[0]
    hid_here = w_fc2.shape[0] // 2
    hid = hid_here * dp_n
    own = lat * tok
    every = ("dp", "seq")
    n_all = dp_n * seq_n

    tok_slots = seq_gather(tokens)

    cond_silu, silu_back = jax.vjp(jax.nn.silu, conditioning)
    cond_act = cond_silu.astype(BF)
    bias_half = lax.dynamic_slice(b_fc1, (core * hid_here,), (hid_here,))
    small = jnp.concatenate(
        [
            cond_act.reshape(lat, dp_n, rows).transpose(1, 0, 2).reshape(dp_n, lat * rows),
            jnp.broadcast_to(bias_half[None], (dp_n, hid_here)),
        ],
        axis=1,
    )
    small = dp_exchange(small)
    cond_rows = small[:, : lat * rows].reshape(dp_n * lat, rows)
    fc1_bias = small[:, lat * rows :].reshape(hid).astype(F32)
    mod_terms = matmul(cond_rows, w_mod)
    piece = b_mod.shape[0]
    mod_terms = lax.dynamic_update_slice(
        mod_terms,
        lax.dynamic_slice(mod_terms, (0, dp * piece), (dp_n * lat, piece))
        + b_mod.astype(F32)[None],
        (0, dp * piece),
    )
    modulation = jnp.sum(dp_exchange(mod_terms.reshape(dp_n, lat, 6 * width)), axis=0)
    shift_attn, scale_attn, gate_attn, shift_mlp, scale_mlp, gate_mlp = [
        modulation[:, None, i * width : (i + 1) * width] for i in range(6)
    ]

    qkv_here = lax.dynamic_index_in_dim(
        w_qkv.reshape(rows, 3, seq_n, cols), seq, axis=2, keepdims=False
    ).reshape(rows, 3 * cols)
    qkv = dp_gather(qkv_here)
    proj_half = dp_gather(lax.dynamic_slice(w_proj, (0, core * (width // 2)), (rows, width // 2)))
    fc1_here = lax.dynamic_index_in_dim(
        w_fc1.reshape(rows, dp_n, 2, hid_here), core, axis=2, keepdims=False
    ).reshape(rows, hid)
    fc1 = dp_gather(fc1_here)
    fc2 = dp_gather(lax.dynamic_slice(w_fc2, (core * hid_here, 0), (hid_here, width)))
    proj_other = hop(proj_half, "seq", 1)
    proj = jnp.where(
        core == 0,
        jnp.concatenate([proj_half, proj_other], axis=1),
        jnp.concatenate([proj_other, proj_half], axis=1),
    )
    proj = jnp.concatenate(
        [lax.dynamic_slice(proj, ((seq ^ j) * cols, 0), (cols, width)) for j in range(seq_n)]
    )

    tok_all = jnp.concatenate(tok_slots, axis=1).astype(F32)
    normed_all = (ln_parts(tok_all)[0] * (1.0 + scale_attn) + shift_attn).astype(BF)
    normed_all = normed_all.reshape(lat * seq_len, width)
    packed = matmul(normed_all, qkv).astype(BF).reshape(lat, seq_len, 3 * cols)
    mixed, log_sums = attention(packed, heads_here)
    mixed_slots = mixed.reshape(lat, seq_n, tok, cols)
    attended = jnp.concatenate(
        seq_exchange([mixed_slots[:, j] for j in range(seq_n)]), axis=2
    ).reshape(own, width)

    attn_out = matmul(attended, proj).reshape(lat, tok, width)
    token_values = tokens.astype(F32)
    resid_mid = token_values + gate_attn * attn_out
    normed_mid, std_mid = ln_parts(resid_mid)
    normed_mlp = (normed_mid * (1.0 + scale_mlp) + shift_mlp).astype(BF).reshape(own, width)
    upstream = cotangent.astype(F32)
    d_mlp = (gate_mlp * upstream).astype(BF).reshape(own, width)
    d_mlp_pair = jnp.concatenate([d_mlp, hop(d_mlp, "seq", 1)])

    normed_pair = jnp.concatenate([normed_mlp, hop(normed_mlp, "seq", 1)])
    hidden = matmul(normed_pair, fc1) + fc1_bias
    tanh = jnp.tanh(GELU_C * (hidden + GELU_A * hidden * hidden * hidden))
    activated = (0.5 * hidden * (1.0 + tanh)).astype(BF)
    gelu_slope = 0.5 * (1.0 + tanh) + 0.5 * hidden * (1.0 - tanh * tanh) * GELU_C * (
        1.0 + 3.0 * GELU_A * hidden * hidden
    )
    d_hidden = (matmul_nt(d_mlp_pair, fc2) * gelu_slope).astype(BF)
    d_norm_part = matmul_nt(d_hidden, fc1)
    d_norm = d_norm_part[:own] + hop(d_norm_part[own:].astype(BF), "seq", 1).astype(F32)
    d_norm = d_norm.reshape(lat, tok, width)
    grad_fc2 = matmul_tn(activated, d_mlp_pair).astype(BF)
    grad_fc1 = matmul_tn(normed_pair, d_hidden).astype(BF)
    grad_bias1 = jnp.sum(d_hidden.astype(F32), axis=0)
    mlp_part = matmul(activated, fc2)
    mlp_out = mlp_part[:own] + hop(mlp_part[own:].astype(BF), "seq", 1).astype(F32)
    mlp_out = mlp_out.reshape(lat, tok, width)
    output = (resid_mid + gate_mlp * mlp_out).astype(BF)
    d_gate_mlp = jnp.sum(upstream * mlp_out, axis=1)

    d_shift_mlp = jnp.sum(d_norm, axis=1)
    d_scale_mlp = jnp.sum(d_norm * normed_mid, axis=1)
    d_resid = upstream + ln_backward(d_norm * (1.0 + scale_mlp), normed_mid, std_mid)
    d_gate_attn = jnp.sum(d_resid * attn_out, axis=1)
    d_attn = (gate_attn * d_resid).astype(BF).reshape(own, width)
    grad_proj = matmul_tn(attended, d_attn).astype(BF)
    d_attended = matmul_nt(d_attn, proj).astype(BF).reshape(lat, tok, width)
    d_mixed = jnp.concatenate(
        seq_exchange([d_attended[:, :, j * cols : (j + 1) * cols] for j in range(seq_n)]), axis=1
    )
    d_packed = attention_grad(packed, mixed, log_sums, d_mixed, heads_here)
    d_packed = d_packed.reshape(lat * seq_len, 3 * cols)
    grad_qkv = matmul_tn(normed_all, d_packed).astype(BF)
    first_parts = matmul_nt(d_packed, qkv).reshape(lat, seq_n, tok, width)
    d_first = seq_reduce([first_parts[:, j] for j in range(seq_n)])
    normed_tok, std_tok = ln_parts(token_values)
    d_shift_attn = jnp.sum(d_first, axis=1)
    d_scale_attn = jnp.sum(d_first * normed_tok, axis=1)
    grad_tokens = d_resid + ln_backward(d_first * (1.0 + scale_attn), normed_tok, std_tok)

    mod_part = jnp.concatenate(
        [d_shift_attn, d_scale_attn, d_gate_attn, d_shift_mlp, d_scale_mlp, d_gate_mlp], axis=1
    )
    share = 6 * width // n_all
    mod_cols = lax.all_to_all(
        mod_part.reshape(lat, n_all, share).transpose(1, 0, 2), every, 0, 0, tiled=True
    )
    d_mod = jnp.sum(mod_cols.reshape(dp_n, seq_n, lat, share), axis=1).reshape(dp_n * lat, share)
    d_mod = d_mod.astype(BF)
    cond_all = lax.all_to_all(
        jnp.broadcast_to(cond_act[None], (dp_n, lat, width)), "dp", 0, 0, tiled=True
    ).reshape(dp_n * lat, width)
    grad_wmod = matmul_tn(cond_all, d_mod)
    grad_bmod = jnp.sum(d_mod.astype(F32), axis=0)
    mod_rows = lax.all_to_all(
        jnp.broadcast_to(d_mod[None], (dp_n, dp_n * lat, share)), "dp", 0, 0, tiled=True
    )
    mod_here = mod_rows.transpose(1, 0, 2).reshape(dp_n * lat, dp_n * share)
    w_mod_here = lax.dynamic_index_in_dim(
        w_mod.reshape(rows, dp_n, seq_n, share), seq, axis=2, keepdims=False
    ).reshape(rows, dp_n * share)
    cond_terms = matmul_nt(mod_here, w_mod_here)
    cond_terms = jnp.broadcast_to(
        cond_terms.reshape(dp_n, 1, lat, rows), (dp_n, seq_n, lat, rows)
    ).reshape(n_all, lat, rows)
    cond_back = lax.all_to_all(cond_terms, every, 0, 0, tiled=True)
    d_cond = jnp.sum(cond_back.reshape(dp_n, seq_n, lat, rows), axis=1)
    (grad_cond,) = silu_back(d_cond.transpose(1, 0, 2).reshape(lat, width))

    spread = jnp.zeros((dp_n, 2, hid_here), F32)
    spread = lax.dynamic_update_slice(spread, grad_bias1.reshape(dp_n, 1, hid_here), (0, core, 0))
    bias_cols = lax.all_to_all(
        spread.reshape(n_all, 2 * hid_here // seq_n), every, 0, 0, tiled=True
    )
    bias_out = jnp.sum(bias_cols, axis=0)

    sum_fc2 = dp_scatter(grad_fc2).astype(BF)
    sum_fc1 = dp_scatter(grad_fc1).astype(BF)
    grad_proj = jnp.concatenate(
        [
            lax.dynamic_slice(grad_proj, ((seq ^ j) * cols, 0), (cols, width))
            for j in range(seq_n)
        ]
    )
    sum_proj = dp_scatter(grad_proj).astype(BF)
    sum_qkv = dp_scatter(grad_qkv).astype(BF)

    def to_owner(blocks):
        return lax.all_to_all(blocks, "seq", 0, 0, tiled=True).astype(F32)

    def pair_sum(received):
        return jnp.sum(received.reshape((seq_n // 2, 2) + received.shape[1:]), axis=0)

    fc2_cols = width // seq_n
    out_fc2 = pair_sum(to_owner(sum_fc2.reshape(hid_here, seq_n, fc2_cols).transpose(1, 0, 2)))
    out_fc2 = out_fc2.reshape(2 * hid_here, fc2_cols)
    per = dp_n * 2 // seq_n
    if per >= 2:
        blocks = sum_fc1.reshape(rows, seq_n, dp_n // seq_n, hid_here).transpose(1, 0, 2, 3)
        out_fc1 = pair_sum(to_owner(blocks)).transpose(1, 2, 0, 3)
    else:
        parts = to_owner(
            jnp.broadcast_to(sum_fc1.reshape(1, rows, hid), (seq_n, rows, hid))
        )
        parts = pair_sum(parts).reshape(2, rows, dp_n, hid_here).transpose(1, 2, 0, 3)
        out_fc1 = lax.dynamic_slice(
            parts.reshape(rows, 2 * hid), (0, seq * (2 * hid // seq_n)), (rows, 2 * hid // seq_n)
        )
    out_fc1 = out_fc1.reshape(rows, 2 * hid // seq_n)
    out_proj = jnp.sum(
        to_owner(sum_proj.reshape(rows, seq_n, width // seq_n).transpose(1, 0, 2)), axis=0
    )
    qkv_slots = seq_gather(sum_qkv)
    qkv_whole = jnp.zeros((rows, 3, seq_n, cols), BF)
    for j in range(seq_n):
        qkv_whole = lax.dynamic_update_slice(
            qkv_whole, qkv_slots[j].reshape(rows, 3, 1, cols), (0, 0, seq ^ j, 0)
        )
    out_qkv = lax.dynamic_slice(
        qkv_whole.reshape(rows, 3 * width), (0, seq * 3 * cols), (rows, 3 * cols)
    ).astype(F32)
    return (
        output,
        grad_tokens,
        grad_cond,
        grad_wmod,
        grad_bmod,
        out_qkv,
        out_proj,
        out_fc1,
        bias_out,
        out_fc2,
    )


def solution(mesh):
    placed = (
        P("dp", "seq", None),
        P("dp", None),
        P("dp", None),
        P("dp"),
        P("dp", None),
        P("dp", None),
        P("dp", None),
        P("dp"),
        P("dp", None),
        P("dp", "seq", None),
    )
    return jax.shard_map(
        on_device,
        mesh=mesh,
        in_specs=placed,
        out_specs=(
            P("dp", "seq", None),
            P("dp", "seq", None),
            P("dp", None),
            P(None, ("dp", "seq")),
            P(("dp", "seq")),
            P("dp", "seq"),
            P("dp", "seq"),
            P("dp", "seq"),
            P(("dp", "seq")),
            P("dp", "seq"),
        ),
        check_vma=False,
    )
```

```python
import math
from functools import partial

import jax
import jax.numpy as jnp
from jax import lax
from jax.experimental import pallas as pl
from jax.experimental.pallas import tpu as pltpu
from jax.sharding import PartitionSpec as P

HEADS = 16
HEAD_DIM = 72
BF = jnp.bfloat16
F32 = jnp.float32
GELU_C = 0.7978845608028654
GELU_A = 0.044715
EXP2_SCALE = HEAD_DIM ** (-0.5) * math.log2(math.e)


def hop(value, axis, bits):
    count = lax.axis_size(axis)
    return lax.ppermute(value, axis, [(i, i ^ bits) for i in range(count)])


def matmul(left, right):
    return jnp.dot(left, right, preferred_element_type=F32)


def matmul_nt(left, right):
    return lax.dot_general(left, right, (((1,), (1,)), ((), ())), preferred_element_type=F32)


def matmul_tn(left, right):
    return lax.dot_general(left, right, (((0,), (0,)), ((), ())), preferred_element_type=F32)


def ln_parts(values):
    row_mean = jnp.mean(values, axis=-1, keepdims=True)
    centred = values - row_mean
    row_var = jnp.mean(centred * centred, axis=-1, keepdims=True)
    inv_std = lax.rsqrt(row_var + 1e-06)
    return centred * inv_std, inv_std


def ln_backward(grad, normed, inv_std):
    mean_grad = jnp.mean(grad, axis=-1, keepdims=True)
    mean_inner = jnp.mean(grad * normed, axis=-1, keepdims=True)
    return (grad - mean_grad - normed * mean_inner) * inv_std


def seq_gather(mine):
    slots = {0: mine}
    bit = lax.axis_size("seq") // 2
    while bit:
        for j in list(slots):
            slots[j | bit] = hop(slots[j], "seq", bit)
        bit //= 2
    return [slots[j] for j in range(len(slots))]


def seq_reduce(slots):
    slots = dict(enumerate(slots))
    bit = 1
    while len(slots) > 1:
        for j in [j for j in slots if j & bit]:
            slots[j ^ bit] = slots[j ^ bit] + hop(slots.pop(j).astype(BF), "seq", bit).astype(F32)
        bit *= 2
    return slots[0]


def seq_exchange(blocks):
    return [blocks[0]] + [hop(blocks[j], "seq", j) for j in range(1, len(blocks))]


def dp_exchange(value):
    return lax.all_to_all(value, "dp", 0, 0, tiled=True)


def dp_gather(mine, place):
    count = lax.axis_size("dp")
    index = lax.axis_index("dp")
    slots = {0: mine}
    for j in range(2, count, 2):
        slots[j] = hop(mine, "dp", j)
    for j in range(0, count, 2):
        slots[j + 1] = hop(slots[j], "dp", 1)
    whole = jnp.zeros((count,) + mine.shape, mine.dtype)
    for j in range(count):
        whole = lax.dynamic_update_index_in_dim(whole, slots[j], place(index ^ j), 0)
    return whole


def dp_scatter(terms, place):
    count = lax.axis_size("dp")
    index = lax.axis_index("dp")

    def block(j):
        return lax.dynamic_index_in_dim(terms, place(index ^ j), 0, keepdims=False)

    half = {}
    for j in list(range(2, count, 2)) + [0]:
        half[j] = block(j).astype(F32) + hop(block(j + 1), "dp", 1).astype(F32)
    total = half[0]
    for j in range(2, count, 2):
        total = total + hop(half[j].astype(BF), "dp", j).astype(F32)
    return total


def attend_kernel(heads, block, packed, mixed, log_sum, mixed_t):
    seq_len = packed.shape[1]
    cols = heads * HEAD_DIM
    for h in range(heads):
        at = h * HEAD_DIM
        keys = packed[0, :, cols + at : cols + at + HEAD_DIM]
        values_t = packed[0, :, 2 * cols + at : 2 * cols + at + HEAD_DIM].astype(F32).T.astype(BF)
        for start in range(0, seq_len, block):
            queries = packed[0, start : start + block, at : at + HEAD_DIM]
            scores = matmul_nt(keys, queries)
            top = jnp.max(scores, axis=0, keepdims=True)
            exponent = jnp.exp2((scores - top) * EXP2_SCALE)
            total = jnp.sum(exponent, axis=0, keepdims=True)
            part = matmul(values_t, exponent.astype(BF)) / total
            mixed_t[at : at + HEAD_DIM, start : start + block] = part
            log_sum[0, h : h + 1, start : start + block] = top * EXP2_SCALE + jnp.log2(total)
    mixed[0] = mixed_t[...].T.astype(BF)


def attend_grad_kernel(heads, block, packed, mixed, log_sum, d_mixed, d_packed, d_queries_t):
    seq_len = packed.shape[1]
    cols = heads * HEAD_DIM
    inv_root = HEAD_DIM ** (-0.5)
    for h in range(heads):
        at = h * HEAD_DIM
        keys = packed[0, :, cols + at : cols + at + HEAD_DIM]
        values = packed[0, :, 2 * cols + at : 2 * cols + at + HEAD_DIM]
        keys_t = keys.astype(F32).T.astype(BF)
        d_keys = d_values = None
        for start in range(0, seq_len, block):
            queries = packed[0, start : start + block, at : at + HEAD_DIM]
            grads = d_mixed[0, start : start + block, at : at + HEAD_DIM]
            outs = mixed[0, start : start + block, at : at + HEAD_DIM]
            inner = jnp.sum(grads.astype(F32) * outs.astype(F32), axis=1, keepdims=True)
            inner = jnp.broadcast_to(inner, (block, 128)).T[0:1]
            scores = matmul_nt(keys, queries)
            probs = jnp.exp2(scores * EXP2_SCALE - log_sum[0, h : h + 1, start : start + block])
            d_probs = matmul_nt(values, grads)
            d_scores = (probs * (d_probs - inner)).astype(BF)
            d_v = matmul(probs.astype(BF), grads)
            d_k = matmul(d_scores, queries)
            d_values = d_v if d_values is None else d_values + d_v
            d_keys = d_k if d_keys is None else d_keys + d_k
            d_queries_t[at : at + HEAD_DIM, start : start + block] = matmul(keys_t, d_scores) * inv_root
        d_packed[0, :, cols + at : cols + at + HEAD_DIM] = (d_keys * inv_root).astype(BF)
        d_packed[0, :, 2 * cols + at : 2 * cols + at + HEAD_DIM] = d_values.astype(BF)
    d_packed[0, :, 0:cols] = d_queries_t[...].T.astype(BF)


def row_spec(*shape):
    return pl.BlockSpec((1,) + shape, lambda i: (i, 0, 0))


def attention(packed, heads, block=512):
    lat, seq_len, _ = packed.shape
    cols = heads * HEAD_DIM
    return pl.pallas_call(
        partial(attend_kernel, heads, block),
        grid=(lat,),
        in_specs=[row_spec(seq_len, 3 * cols)],
        out_specs=[row_spec(seq_len, cols), row_spec(heads, seq_len)],
        out_shape=[
            jax.ShapeDtypeStruct((lat, seq_len, cols), BF),
            jax.ShapeDtypeStruct((lat, heads, seq_len), F32),
        ],
        scratch_shapes=[pltpu.VMEM((cols, seq_len), F32)],
        compiler_params=pltpu.CompilerParams(vmem_limit_bytes=48 * 2**20),
        name="attend",
    )(packed)


def attention_grad(packed, mixed, log_sum, d_mixed, heads, block=512):
    lat, seq_len, _ = packed.shape
    cols = heads * HEAD_DIM
    return pl.pallas_call(
        partial(attend_grad_kernel, heads, block),
        grid=(lat,),
        in_specs=[
            row_spec(seq_len, 3 * cols),
            row_spec(seq_len, cols),
            row_spec(heads, seq_len),
            row_spec(seq_len, cols),
        ],
        out_specs=row_spec(seq_len, 3 * cols),
        out_shape=jax.ShapeDtypeStruct((lat, seq_len, 3 * cols), BF),
        scratch_shapes=[pltpu.VMEM((cols, seq_len), F32)],
        compiler_params=pltpu.CompilerParams(vmem_limit_bytes=48 * 2**20),
        name="attend_grad",
    )(packed, mixed, log_sum, d_mixed)


def on_device(tokens, conditioning, w_mod, b_mod, w_qkv, w_proj, w_fc1, b_fc1, w_fc2, cotangent):
    lat, tok, width = tokens.shape
    seq_n = lax.axis_size("seq")
    dp_n = lax.axis_size("dp")
    seq = lax.axis_index("seq")
    dp = lax.axis_index("dp")
    core = seq % 2
    heads_here = HEADS // seq_n
    cols = heads_here * HEAD_DIM
    seq_len = tok * seq_n
    rows = w_qkv.shape[0]
    hid_here = w_fc2.shape[0] // 2
    hid = hid_here * dp_n
    every = ("dp", "seq")
    n_all = dp_n * seq_n
    groups = 2
    per = lat // groups
    own = per * tok

    cond_silu, silu_back = jax.vjp(jax.nn.silu, conditioning)
    cond_act = cond_silu.astype(BF)
    bias_half = lax.dynamic_slice(b_fc1, (core * hid_here,), (hid_here,))
    small = jnp.concatenate(
        [
            cond_act.reshape(lat, dp_n, rows).transpose(1, 0, 2).reshape(dp_n, lat * rows),
            jnp.broadcast_to(bias_half[None], (dp_n, hid_here)),
        ],
        axis=1,
    )
    small = dp_exchange(small)
    cond_rows = small[:, : lat * rows].reshape(dp_n * lat, rows)
    fc1_bias = small[:, lat * rows :].reshape(hid).astype(F32)
    mod_terms = matmul(cond_rows, w_mod)
    piece = b_mod.shape[0]
    mod_terms = lax.dynamic_update_slice(
        mod_terms,
        lax.dynamic_slice(mod_terms, (0, dp * piece), (dp_n * lat, piece))
        + b_mod.astype(F32)[None],
        (0, dp * piece),
    )
    modulation = jnp.sum(dp_exchange(mod_terms.reshape(dp_n, lat, 6 * width)), axis=0)

    tok_slots = seq_gather(tokens)

    qkv_here = lax.dynamic_index_in_dim(
        w_qkv.reshape(rows, 3, seq_n, cols), seq, axis=2, keepdims=False
    ).reshape(rows, 3 * cols)
    qkv = dp_gather(qkv_here, lambda d: d).reshape(width, 3 * cols)
    fc1_here = lax.dynamic_index_in_dim(
        w_fc1.reshape(rows, dp_n, 2, hid_here), core, axis=2, keepdims=False
    ).reshape(rows, hid)
    fc1 = lax.all_gather(fc1_here, "dp", axis=0, tiled=True)
    fc2 = lax.all_gather(
        lax.dynamic_slice(w_fc2, (core * hid_here, 0), (hid_here, width)), "dp", axis=0, tiled=True
    )
    ratio = cols // rows
    half = rows // 2

    def proj_place(d):
        return ((d // ratio) ^ seq) * ratio + d % ratio

    def flip(halves):
        return halves.reshape(seq_n // 2, 2, ratio * half, width)[:, ::-1].reshape(
            dp_n, half, width
        )

    proj_mine = dp_gather(lax.dynamic_slice(w_proj, (core * half, 0), (half, width)), proj_place)
    proj_other = flip(hop(proj_mine, "seq", 1))
    proj = jnp.where(
        core == 0,
        jnp.stack([proj_mine, proj_other], axis=1),
        jnp.stack([proj_other, proj_mine], axis=1),
    ).reshape(width, width)

    def part(g):
        return slice(g * per, (g + 1) * per)

    shift_attn, scale_attn, gate_attn, shift_mlp, scale_mlp, gate_mlp = [
        [modulation[part(g), None, i * width : (i + 1) * width] for g in range(groups)]
        for i in range(6)
    ]
    token_values = [tokens[part(g)].astype(F32) for g in range(groups)]
    normed_all, packed, mixed, log_sums, attended = [], [], [], [], []
    for g in range(groups):
        tok_all = jnp.concatenate([slot[part(g)] for slot in tok_slots], axis=1).astype(F32)
        normed = (ln_parts(tok_all)[0] * (1.0 + scale_attn[g]) + shift_attn[g]).astype(BF)
        normed_all.append(normed.reshape(per * seq_len, width))
        packed.append(matmul(normed_all[g], qkv).astype(BF).reshape(per, seq_len, 3 * cols))
        out, log_sum = attention(packed[g], heads_here)
        mixed.append(out)
        log_sums.append(log_sum)
        out = out.reshape(per, seq_n, tok, cols)
        attended.append(
            jnp.concatenate(seq_exchange([out[:, j] for j in range(seq_n)]), axis=2).reshape(
                own, width
            )
        )

    attn_out, resid_mid, normed_mid, std_mid, normed_mlp, upstream, d_mlp = ([] for _ in range(7))
    for g in range(groups):
        attn_out.append(matmul(attended[g], proj).reshape(per, tok, width))
        resid_mid.append(token_values[g] + gate_attn[g] * attn_out[g])
        normed, inv_std = ln_parts(resid_mid[g])
        normed_mid.append(normed)
        std_mid.append(inv_std)
        normed_mlp.append(
            (normed * (1.0 + scale_mlp[g]) + shift_mlp[g]).astype(BF).reshape(own, width)
        )
        upstream.append(cotangent[part(g)].astype(F32))
        d_mlp.append((gate_mlp[g] * upstream[g]).astype(BF).reshape(own, width))
    d_mlp_pair = jnp.concatenate(d_mlp + [hop(v, "seq", 1) for v in d_mlp])
    normed_pair = jnp.concatenate(normed_mlp + [hop(v, "seq", 1) for v in normed_mlp])

    hidden = matmul(normed_pair, fc1) + fc1_bias
    tanh = jnp.tanh(GELU_C * (hidden + GELU_A * hidden * hidden * hidden))
    activated = (0.5 * hidden * (1.0 + tanh)).astype(BF)
    gelu_slope = 0.5 * (1.0 + tanh) + 0.5 * hidden * (1.0 - tanh * tanh) * GELU_C * (
        1.0 + 3.0 * GELU_A * hidden * hidden
    )
    d_hidden = (matmul_nt(d_mlp_pair, fc2) * gelu_slope).astype(BF)
    grad_fc2 = matmul_tn(activated, d_mlp_pair).astype(BF)
    sum_fc2 = lax.psum_scatter(grad_fc2, "dp", scatter_dimension=0, tiled=True)
    d_norm_part = matmul_nt(d_hidden, fc1)
    d_norm_sent = [
        hop(d_norm_part[(groups + g) * own : (groups + g + 1) * own].astype(BF), "seq", 1)
        for g in range(groups)
    ]
    grad_fc1 = matmul_tn(normed_pair, d_hidden).astype(BF)
    sum_fc1 = lax.psum_scatter(grad_fc1, "dp", scatter_dimension=0, tiled=True)
    grad_bias1 = jnp.sum(d_hidden.astype(F32), axis=0)
    mlp_part = matmul(activated, fc2)
    mlp_sent = hop(mlp_part[groups * own :].astype(BF), "seq", 1)
    mlp_out = mlp_part[: groups * own] + mlp_sent.astype(F32)
    mlp_out = mlp_out.reshape(groups, per, tok, width)
    output = jnp.concatenate(
        [(resid_mid[g] + gate_mlp[g] * mlp_out[g]).astype(BF) for g in range(groups)]
    )

    def stacked(terms):
        return jnp.concatenate(terms)

    d_gate_mlp = stacked([jnp.sum(upstream[g] * mlp_out[g], axis=1) for g in range(groups)])
    d_shift_mlp, d_scale_mlp, d_gate_attn, d_resid, d_attn = ([] for _ in range(5))
    d_mixed = []
    for g in range(groups):
        d_norm = d_norm_part[g * own : (g + 1) * own] + d_norm_sent[g].astype(F32)
        d_norm = d_norm.reshape(per, tok, width)
        d_shift_mlp.append(jnp.sum(d_norm, axis=1))
        d_scale_mlp.append(jnp.sum(d_norm * normed_mid[g], axis=1))
        d_resid.append(
            upstream[g] + ln_backward(d_norm * (1.0 + scale_mlp[g]), normed_mid[g], std_mid[g])
        )
        d_gate_attn.append(jnp.sum(d_resid[g] * attn_out[g], axis=1))
        d_attn.append((gate_attn[g] * d_resid[g]).astype(BF).reshape(own, width))
        d_attended = matmul_nt(d_attn[g], proj).astype(BF).reshape(per, tok, width)
        d_mixed.append(
            jnp.concatenate(
                seq_exchange([d_attended[:, :, j * cols : (j + 1) * cols] for j in range(seq_n)]),
                axis=1,
            )
        )
    grad_proj = matmul_tn(stacked(attended), stacked(d_attn)).astype(BF)
    grad_proj = grad_proj.reshape(dp_n, 2, half, width)
    proj_sent = hop(
        lax.dynamic_index_in_dim(grad_proj, 1 - core, axis=1, keepdims=False), "seq", 1
    )
    proj_terms = lax.dynamic_index_in_dim(grad_proj, core, axis=1, keepdims=False).astype(F32)
    proj_terms = (proj_terms + flip(proj_sent).astype(F32)).astype(BF)
    sum_proj = dp_scatter(proj_terms, proj_place).astype(BF)

    d_packed, d_first = [], []
    for g in range(groups):
        d_packed.append(
            attention_grad(packed[g], mixed[g], log_sums[g], d_mixed[g], heads_here).reshape(
                per * seq_len, 3 * cols
            )
        )
        parts = matmul_nt(d_packed[g], qkv).reshape(per, seq_n, tok, width)
        d_first.append(seq_reduce([parts[:, j] for j in range(seq_n)]))
    grad_qkv = matmul_tn(stacked(normed_all), stacked(d_packed)).astype(BF)
    sum_qkv = dp_scatter(grad_qkv.reshape(dp_n, rows, 3 * cols), lambda d: d).astype(BF)
    d_shift_attn, d_scale_attn, grad_tokens = [], [], []
    for g in range(groups):
        normed_tok, std_tok = ln_parts(token_values[g])
        d_shift_attn.append(jnp.sum(d_first[g], axis=1))
        d_scale_attn.append(jnp.sum(d_first[g] * normed_tok, axis=1))
        grad_tokens.append(
            d_resid[g] + ln_backward(d_first[g] * (1.0 + scale_attn[g]), normed_tok, std_tok)
        )

    mod_part = jnp.concatenate(
        [stacked(d_shift_attn), stacked(d_scale_attn), stacked(d_gate_attn)]
        + [stacked(d_shift_mlp), stacked(d_scale_mlp), d_gate_mlp],
        axis=1,
    )
    share = 6 * width // n_all
    mod_cols = lax.all_to_all(
        mod_part.reshape(lat, n_all, share).transpose(1, 0, 2), every, 0, 0, tiled=True
    )
    d_mod = jnp.sum(mod_cols.reshape(dp_n, seq_n, lat, share), axis=1).reshape(dp_n * lat, share)
    d_mod = d_mod.astype(BF)
    cond_all = lax.all_to_all(
        jnp.broadcast_to(cond_act[None], (dp_n, lat, width)), "dp", 0, 0, tiled=True
    ).reshape(dp_n * lat, width)
    grad_wmod = matmul_tn(cond_all, d_mod)
    grad_bmod = jnp.sum(d_mod.astype(F32), axis=0)
    mod_rows = lax.all_to_all(
        jnp.broadcast_to(d_mod[None], (dp_n, dp_n * lat, share)), "dp", 0, 0, tiled=True
    )
    mod_here = mod_rows.transpose(1, 0, 2).reshape(dp_n * lat, dp_n * share)
    w_mod_here = lax.dynamic_index_in_dim(
        w_mod.reshape(rows, dp_n, seq_n, share), seq, axis=2, keepdims=False
    ).reshape(rows, dp_n * share)
    cond_terms = matmul_nt(mod_here, w_mod_here)
    cond_terms = jnp.broadcast_to(
        cond_terms.reshape(dp_n, 1, lat, rows), (dp_n, seq_n, lat, rows)
    ).reshape(n_all, lat, rows)
    cond_back = lax.all_to_all(cond_terms, every, 0, 0, tiled=True)
    d_cond = jnp.sum(cond_back.reshape(dp_n, seq_n, lat, rows), axis=1)
    (grad_cond,) = silu_back(d_cond.transpose(1, 0, 2).reshape(lat, width))

    spread = jnp.zeros((dp_n, 2, hid_here), F32)
    spread = lax.dynamic_update_slice(spread, grad_bias1.reshape(dp_n, 1, hid_here), (0, core, 0))
    bias_cols = lax.all_to_all(
        spread.reshape(n_all, 2 * hid_here // seq_n), every, 0, 0, tiled=True
    )
    bias_out = jnp.sum(bias_cols, axis=0)

    def to_owner(blocks):
        received = lax.all_to_all(blocks, "seq", 0, 0, tiled=True).astype(F32)
        return jnp.sum(received.reshape((seq_n // 2, 2) + received.shape[1:]), axis=0)

    share = width // seq_n
    out_fc2 = to_owner(sum_fc2.reshape(hid_here, seq_n, share).transpose(1, 0, 2))
    out_fc2 = out_fc2.reshape(2 * hid_here, share)
    out_proj = to_owner(sum_proj.reshape(half, seq_n, share).transpose(1, 0, 2))
    out_proj = out_proj.reshape(rows, share)
    blocks = sum_fc1.reshape(rows, seq_n, dp_n // seq_n, hid_here).transpose(1, 0, 2, 3)
    out_fc1 = to_owner(blocks).transpose(1, 2, 0, 3).reshape(rows, 2 * hid // seq_n)
    qkv_slots = jnp.stack(
        seq_gather(sum_qkv.reshape(rows, 3, cols).transpose(1, 0, 2))
    ).reshape(3 * seq_n, rows, cols)
    out_qkv = []
    for i in range(3):
        block = 3 * seq + i
        at = ((block % seq_n) ^ seq) * 3 + block // seq_n
        out_qkv.append(lax.dynamic_index_in_dim(qkv_slots, at, 0, keepdims=False))
    out_qkv = jnp.concatenate(out_qkv, axis=1).astype(F32)
    return (
        output,
        stacked(grad_tokens),
        grad_cond,
        grad_wmod,
        grad_bmod,
        out_qkv,
        out_proj,
        out_fc1,
        bias_out,
        out_fc2,
    )


def solution(mesh):
    placed = (
        P("dp", "seq", None),
        P("dp", None),
        P("dp", None),
        P("dp"),
        P("dp", None),
        P("dp", None),
        P("dp", None),
        P("dp"),
        P("dp", None),
        P("dp", "seq", None),
    )
    return jax.shard_map(
        on_device,
        mesh=mesh,
        in_specs=placed,
        out_specs=(
            P("dp", "seq", None),
            P("dp", "seq", None),
            P("dp", None),
            P(None, ("dp", "seq")),
            P(("dp", "seq")),
            P("dp", "seq"),
            P("dp", "seq"),
            P("dp", "seq"),
            P(("dp", "seq")),
            P("dp", "seq"),
        ),
        check_vma=False,
    )
```

```python
import math
from functools import partial

import jax
import jax.numpy as jnp
from jax import lax
from jax.experimental import pallas as pl
from jax.experimental.pallas import tpu as pltpu
from jax.sharding import PartitionSpec as P

HEADS = 16
HEAD_DIM = 72
BF = jnp.bfloat16
F32 = jnp.float32
GELU_C = 0.7978845608028654
GELU_A = 0.044715
EXP2_SCALE = HEAD_DIM ** (-0.5) * math.log2(math.e)


def hop(value, axis, bits):
    count = lax.axis_size(axis)
    return lax.ppermute(value, axis, [(i, i ^ bits) for i in range(count)])


def matmul(left, right):
    return jnp.dot(left, right, preferred_element_type=F32)


def matmul_nt(left, right):
    return lax.dot_general(left, right, (((1,), (1,)), ((), ())), preferred_element_type=F32)


def matmul_tn(left, right):
    return lax.dot_general(left, right, (((0,), (0,)), ((), ())), preferred_element_type=F32)


def ln_parts(values):
    row_mean = jnp.mean(values, axis=-1, keepdims=True)
    centred = values - row_mean
    row_var = jnp.mean(centred * centred, axis=-1, keepdims=True)
    inv_std = lax.rsqrt(row_var + 1e-06)
    return centred * inv_std, inv_std


def ln_backward(grad, normed, inv_std):
    mean_grad = jnp.mean(grad, axis=-1, keepdims=True)
    mean_inner = jnp.mean(grad * normed, axis=-1, keepdims=True)
    return (grad - mean_grad - normed * mean_inner) * inv_std


def seq_gather(mine):
    slots = {0: mine}
    bit = lax.axis_size("seq") // 2
    while bit:
        for j in list(slots):
            slots[j | bit] = hop(slots[j], "seq", bit)
        bit //= 2
    return [slots[j] for j in range(len(slots))]


def seq_reduce(slots):
    slots = dict(enumerate(slots))
    bit = 1
    while len(slots) > 1:
        for j in [j for j in slots if j & bit]:
            slots[j ^ bit] = slots[j ^ bit] + hop(slots.pop(j).astype(BF), "seq", bit).astype(F32)
        bit *= 2
    return slots[0]


def seq_exchange(blocks):
    return [blocks[0]] + [hop(blocks[j], "seq", j) for j in range(1, len(blocks))]


def dp_exchange(value):
    return lax.all_to_all(value, "dp", 0, 0, tiled=True)


def dp_gather(mine, place):
    count = lax.axis_size("dp")
    index = lax.axis_index("dp")
    slots = {0: mine}
    for j in range(2, count, 2):
        slots[j] = hop(mine, "dp", j)
    for j in range(0, count, 2):
        slots[j + 1] = hop(slots[j], "dp", 1)
    whole = jnp.zeros((count,) + mine.shape, mine.dtype)
    for j in range(count):
        whole = lax.dynamic_update_index_in_dim(whole, slots[j], place(index ^ j), 0)
    return whole


def dp_scatter(terms, place):
    count = lax.axis_size("dp")
    index = lax.axis_index("dp")

    def block(j):
        return lax.dynamic_index_in_dim(terms, place(index ^ j), 0, keepdims=False)

    half = {}
    for j in list(range(2, count, 2)) + [0]:
        half[j] = block(j).astype(F32) + hop(block(j + 1), "dp", 1).astype(F32)
    total = half[0]
    for j in range(2, count, 2):
        total = total + hop(half[j].astype(BF), "dp", j).astype(F32)
    return total


def attend_kernel(heads, block, packed, mixed, log_sum, mixed_t):
    seq_len = packed.shape[1]
    cols = heads * HEAD_DIM
    for h in range(heads):
        at = h * HEAD_DIM
        keys = packed[0, :, cols + at : cols + at + HEAD_DIM]
        values_t = packed[0, :, 2 * cols + at : 2 * cols + at + HEAD_DIM].astype(F32).T.astype(BF)
        for start in range(0, seq_len, block):
            queries = packed[0, start : start + block, at : at + HEAD_DIM]
            scores = matmul_nt(keys, queries)
            top = jnp.max(scores, axis=0, keepdims=True)
            exponent = jnp.exp2((scores - top) * EXP2_SCALE)
            total = jnp.sum(exponent, axis=0, keepdims=True)
            part = matmul(values_t, exponent.astype(BF)) / total
            mixed_t[at : at + HEAD_DIM, start : start + block] = part
            log_sum[0, h : h + 1, start : start + block] = top * EXP2_SCALE + jnp.log2(total)
    mixed[0] = mixed_t[...].T.astype(BF)


def attend_grad_kernel(
    heads, block, packed, mixed, log_sum, d_mixed, after, d_packed, d_queries_t
):
    seq_len = packed.shape[1]
    cols = heads * HEAD_DIM
    inv_root = HEAD_DIM ** (-0.5)
    for h in range(heads):
        at = h * HEAD_DIM
        keys = packed[0, :, cols + at : cols + at + HEAD_DIM]
        values = packed[0, :, 2 * cols + at : 2 * cols + at + HEAD_DIM]
        keys_t = keys.astype(F32).T.astype(BF)
        d_keys = d_values = None
        for start in range(0, seq_len, block):
            queries = packed[0, start : start + block, at : at + HEAD_DIM]
            grads = d_mixed[0, start : start + block, at : at + HEAD_DIM]
            outs = mixed[0, start : start + block, at : at + HEAD_DIM]
            inner = jnp.sum(grads.astype(F32) * outs.astype(F32), axis=1, keepdims=True)
            inner = jnp.broadcast_to(inner, (block, 128)).T[0:1]
            scores = matmul_nt(keys, queries)
            probs = jnp.exp2(scores * EXP2_SCALE - log_sum[0, h : h + 1, start : start + block])
            d_probs = matmul_nt(values, grads)
            d_scores = (probs * (d_probs - inner)).astype(BF)
            d_v = matmul(probs.astype(BF), grads)
            d_k = matmul(d_scores, queries)
            d_values = d_v if d_values is None else d_values + d_v
            d_keys = d_k if d_keys is None else d_keys + d_k
            d_queries_t[at : at + HEAD_DIM, start : start + block] = matmul(keys_t, d_scores) * inv_root
        d_packed[0, :, cols + at : cols + at + HEAD_DIM] = (d_keys * inv_root).astype(BF)
        d_packed[0, :, 2 * cols + at : 2 * cols + at + HEAD_DIM] = d_values.astype(BF)
    d_packed[0, :, 0:cols] = d_queries_t[...].T.astype(BF)


def row_spec(*shape):
    return pl.BlockSpec((1,) + shape, lambda i: (i, 0, 0))


def attention(packed, heads, block=1024):
    lat, seq_len, _ = packed.shape
    cols = heads * HEAD_DIM
    return pl.pallas_call(
        partial(attend_kernel, heads, block),
        grid=(lat,),
        in_specs=[row_spec(seq_len, 3 * cols)],
        out_specs=[row_spec(seq_len, cols), row_spec(heads, seq_len)],
        out_shape=[
            jax.ShapeDtypeStruct((lat, seq_len, cols), BF),
            jax.ShapeDtypeStruct((lat, heads, seq_len), F32),
        ],
        scratch_shapes=[pltpu.VMEM((cols, seq_len), F32)],
        compiler_params=pltpu.CompilerParams(vmem_limit_bytes=48 * 2**20),
        name="attend",
    )(packed)


def attention_grad(packed, mixed, log_sum, d_mixed, after, heads, block=512):
    lat, seq_len, _ = packed.shape
    cols = heads * HEAD_DIM
    return pl.pallas_call(
        partial(attend_grad_kernel, heads, block),
        grid=(lat,),
        in_specs=[
            row_spec(seq_len, 3 * cols),
            row_spec(seq_len, cols),
            row_spec(heads, seq_len),
            row_spec(seq_len, cols),
            pl.BlockSpec(memory_space=pl.ANY),
        ],
        out_specs=row_spec(seq_len, 3 * cols),
        out_shape=jax.ShapeDtypeStruct((lat, seq_len, 3 * cols), BF),
        scratch_shapes=[pltpu.VMEM((cols, seq_len), F32)],
        compiler_params=pltpu.CompilerParams(vmem_limit_bytes=48 * 2**20),
        name="attend_grad",
    )(packed, mixed, log_sum, d_mixed, after)


def on_device(tokens, conditioning, w_mod, b_mod, w_qkv, w_proj, w_fc1, b_fc1, w_fc2, cotangent):
    lat, tok, width = tokens.shape
    seq_n = lax.axis_size("seq")
    dp_n = lax.axis_size("dp")
    seq = lax.axis_index("seq")
    dp = lax.axis_index("dp")
    core = seq % 2
    heads_here = HEADS // seq_n
    cols = heads_here * HEAD_DIM
    seq_len = tok * seq_n
    rows = w_qkv.shape[0]
    hid_here = w_fc2.shape[0] // seq_n
    hid = hid_here * dp_n
    groups = 2
    per = lat // groups
    own = per * tok

    cond_silu, silu_back = jax.vjp(jax.nn.silu, conditioning)
    cond_act = cond_silu.astype(BF)
    bias_here = lax.dynamic_slice(b_fc1, (seq * hid_here,), (hid_here,))
    small = jnp.concatenate([cond_act.reshape(lat * width), bias_here])
    small = dp_exchange(jnp.broadcast_to(small[None], (dp_n, lat * width + hid_here)))
    cond_all = small[:, : lat * width].reshape(dp_n * lat, width)
    fc1_bias = small[:, lat * width :].reshape(hid).astype(F32)
    cond_rows = lax.dynamic_slice(cond_all, (0, dp * rows), (dp_n * lat, rows))
    mod_terms = matmul(cond_rows, w_mod)
    piece = b_mod.shape[0]
    mod_terms = lax.dynamic_update_slice(
        mod_terms,
        lax.dynamic_slice(mod_terms, (0, dp * piece), (dp_n * lat, piece))
        + b_mod.astype(F32)[None],
        (0, dp * piece),
    )
    modulation = jnp.sum(dp_exchange(mod_terms.reshape(dp_n, lat, 6 * width)), axis=0)

    tok_slots = seq_gather(tokens)

    qkv_here = jnp.concatenate(
        [lax.dynamic_slice(w_qkv, (0, t * width + seq * cols), (rows, cols)) for t in range(3)],
        axis=1,
    )
    qkv = dp_gather(qkv_here, lambda d: d).reshape(width, 3 * cols)
    half = rows // 2
    proj_mine = lax.all_gather(
        lax.dynamic_slice(w_proj, (core * half, 0), (half, width)), "dp", axis=0
    )
    fc1_here = jnp.concatenate(
        [
            lax.dynamic_slice(w_fc1, (0, (d * seq_n + seq) * hid_here), (rows, hid_here))
            for d in range(dp_n)
        ],
        axis=1,
    )
    fc1 = lax.all_gather(fc1_here, "dp", axis=0, tiled=True)
    fc2 = lax.all_gather(
        lax.dynamic_slice(w_fc2, (seq * hid_here, 0), (hid_here, width)), "dp", axis=0, tiled=True
    )
    proj_other = hop(proj_mine, "seq", 1)
    proj = jnp.where(
        core == 0,
        jnp.stack([proj_mine, proj_other], axis=1),
        jnp.stack([proj_other, proj_mine], axis=1),
    ).reshape(seq_n, cols, width)

    def by_place(blocks):
        return jnp.concatenate(
            [lax.dynamic_index_in_dim(blocks, seq ^ j, 0, keepdims=False) for j in range(seq_n)]
        )

    proj = by_place(proj)

    def part(g):
        return slice(g * per, (g + 1) * per)

    shift_attn, scale_attn, gate_attn, shift_mlp, scale_mlp, gate_mlp = [
        [modulation[part(g), None, i * width : (i + 1) * width] for g in range(groups)]
        for i in range(6)
    ]
    token_values = [tokens[part(g)].astype(F32) for g in range(groups)]
    normed_all, packed, mixed, log_sums, attended = [], [], [], [], []
    for g in range(groups):
        tok_all = jnp.concatenate([slot[part(g)] for slot in tok_slots], axis=1).astype(F32)
        normed = (ln_parts(tok_all)[0] * (1.0 + scale_attn[g]) + shift_attn[g]).astype(BF)
        normed_all.append(normed.reshape(per * seq_len, width))
        packed.append(matmul(normed_all[g], qkv).astype(BF).reshape(per, seq_len, 3 * cols))
        out, log_sum = attention(packed[g], heads_here)
        mixed.append(out)
        log_sums.append(log_sum)
        out = out.reshape(per, seq_n, tok, cols)
        attended.append(
            jnp.concatenate(seq_exchange([out[:, j] for j in range(seq_n)]), axis=2).reshape(
                own, width
            )
        )

    attn_out, resid_mid, normed_mid, std_mid, normed_mlp, upstream, d_mlp = ([] for _ in range(7))
    for g in range(groups):
        attn_out.append(matmul(attended[g], proj).reshape(per, tok, width))
        resid_mid.append(token_values[g] + gate_attn[g] * attn_out[g])
        normed, inv_std = ln_parts(resid_mid[g])
        normed_mid.append(normed)
        std_mid.append(inv_std)
        normed_mlp.append(
            (normed * (1.0 + scale_mlp[g]) + shift_mlp[g]).astype(BF).reshape(own, width)
        )
        upstream.append(cotangent[part(g)].astype(F32))
        d_mlp.append((gate_mlp[g] * upstream[g]).astype(BF).reshape(own, width))
    d_mlp_all = [jnp.concatenate(seq_gather(v)) for v in d_mlp]
    normed_mlp_all = [jnp.concatenate(seq_gather(v)) for v in normed_mlp]

    grad_fc1 = grad_fc2 = grad_bias1 = 0.0
    d_norm, mlp_out = [], []
    for g in range(groups):
        hidden = matmul(normed_mlp_all[g], fc1) + fc1_bias
        tanh = jnp.tanh(GELU_C * (hidden + GELU_A * hidden * hidden * hidden))
        activated = (0.5 * hidden * (1.0 + tanh)).astype(BF)
        gelu_slope = 0.5 * (1.0 + tanh) + 0.5 * hidden * (1.0 - tanh * tanh) * GELU_C * (
            1.0 + 3.0 * GELU_A * hidden * hidden
        )
        d_hidden = (matmul_nt(d_mlp_all[g], fc2) * gelu_slope).astype(BF)
        terms = matmul_nt(d_hidden, fc1).reshape(seq_n, own, width)
        d_norm.append(seq_reduce([terms[j] for j in range(seq_n)]).reshape(per, tok, width))
        grad_fc2 = grad_fc2 + matmul_tn(activated, d_mlp_all[g])
        grad_fc1 = grad_fc1 + matmul_tn(normed_mlp_all[g], d_hidden)
        grad_bias1 = grad_bias1 + jnp.sum(d_hidden.astype(F32), axis=0)
        terms = matmul(activated, fc2).reshape(seq_n, own, width)
        mlp_out.append(seq_reduce([terms[j] for j in range(seq_n)]).reshape(per, tok, width))
    sum_fc2 = lax.psum_scatter(grad_fc2.astype(BF), "dp", scatter_dimension=0, tiled=True)
    sum_fc1 = lax.psum_scatter(grad_fc1.astype(BF), "dp", scatter_dimension=0, tiled=True)
    output = jnp.concatenate(
        [(resid_mid[g] + gate_mlp[g] * mlp_out[g]).astype(BF) for g in range(groups)]
    )

    def stacked(terms):
        return jnp.concatenate(terms)

    d_gate_mlp = stacked([jnp.sum(upstream[g] * mlp_out[g], axis=1) for g in range(groups)])
    d_shift_mlp, d_scale_mlp, d_gate_attn, d_resid, d_attn = ([] for _ in range(5))
    d_mixed, d_attended = [], []
    for g in range(groups):
        d_shift_mlp.append(jnp.sum(d_norm[g], axis=1))
        d_scale_mlp.append(jnp.sum(d_norm[g] * normed_mid[g], axis=1))
        d_resid.append(
            upstream[g] + ln_backward(d_norm[g] * (1.0 + scale_mlp[g]), normed_mid[g], std_mid[g])
        )
        d_gate_attn.append(jnp.sum(d_resid[g] * attn_out[g], axis=1))
        d_attn.append((gate_attn[g] * d_resid[g]).astype(BF).reshape(own, width))
        d_attended.append(matmul_nt(d_attn[g], proj).astype(BF).reshape(per, tok, width))
        d_mixed.append(
            jnp.concatenate(
                seq_exchange([d_attended[g][:, :, j * cols : (j + 1) * cols] for j in range(seq_n)]),
                axis=1,
            )
        )
    grad_proj = by_place(
        matmul_tn(stacked(attended), stacked(d_attn)).astype(BF).reshape(seq_n, cols, width)
    ).reshape(dp_n, 2, half, width)
    proj_sent = hop(
        lax.dynamic_index_in_dim(grad_proj, 1 - core, axis=1, keepdims=False), "seq", 1
    )
    proj_terms = lax.dynamic_index_in_dim(grad_proj, core, axis=1, keepdims=False).astype(F32)
    proj_terms = (proj_terms + proj_sent.astype(F32)).astype(BF)
    sum_proj = lax.psum_scatter(
        proj_terms.reshape(dp_n * half, width), "dp", scatter_dimension=0, tiled=True
    )

    d_packed, d_first = [], []
    for g in range(groups):
        d_packed.append(
            attention_grad(
                packed[g], mixed[g], log_sums[g], d_mixed[g], d_attended[-1], heads_here
            ).reshape(
                per * seq_len, 3 * cols
            )
        )
        parts = matmul_nt(d_packed[g], qkv).reshape(per, seq_n, tok, width)
        d_first.append(seq_reduce([parts[:, j] for j in range(seq_n)]))
    grad_qkv = matmul_tn(stacked(normed_all), stacked(d_packed)).astype(BF)
    sum_qkv = dp_scatter(grad_qkv.reshape(dp_n, rows, 3 * cols), lambda d: d).astype(BF)
    d_shift_attn, d_scale_attn, grad_tokens = [], [], []
    for g in range(groups):
        normed_tok, std_tok = ln_parts(token_values[g])
        d_shift_attn.append(jnp.sum(d_first[g], axis=1))
        d_scale_attn.append(jnp.sum(d_first[g] * normed_tok, axis=1))
        grad_tokens.append(
            d_resid[g] + ln_backward(d_first[g] * (1.0 + scale_attn[g]), normed_tok, std_tok)
        )

    mod_part = jnp.concatenate(
        [stacked(d_shift_attn), stacked(d_scale_attn), stacked(d_gate_attn)]
        + [stacked(d_shift_mlp), stacked(d_scale_mlp), d_gate_mlp],
        axis=1,
    )
    bit = 1
    while bit < seq_n:
        mod_part = mod_part + hop(mod_part, "seq", bit)
        bit *= 2
    d_mod = dp_exchange(jnp.broadcast_to(mod_part.astype(BF)[None], (dp_n, lat, 6 * width)))
    d_mod = d_mod.reshape(dp_n * lat, 6 * width)
    share = 6 * width // (dp_n * seq_n)
    mod_cols = lax.dynamic_slice(d_mod, (0, (dp * seq_n + seq) * share), (dp_n * lat, share))
    grad_wmod = matmul_tn(cond_all, mod_cols)
    grad_bmod = jnp.sum(mod_cols.astype(F32), axis=0)
    d_cond = dp_exchange(matmul_nt(d_mod, w_mod).reshape(dp_n, lat, rows))
    (grad_cond,) = silu_back(d_cond.transpose(1, 0, 2).reshape(lat, width))

    bias_out = jnp.sum(dp_exchange(grad_bias1.reshape(dp_n, hid_here)), axis=0)

    def to_owner(blocks):
        return lax.all_to_all(blocks, "seq", 0, 0, tiled=True).astype(F32)

    share = width // seq_n
    out_fc2 = to_owner(sum_fc2.reshape(hid_here, seq_n, share).transpose(1, 0, 2))
    out_fc2 = out_fc2.reshape(seq_n * hid_here, share)
    out_proj = to_owner(sum_proj.reshape(half, seq_n, share).transpose(1, 0, 2))
    out_proj = jnp.sum(out_proj.reshape(seq_n // 2, rows, share), axis=0)
    blocks = sum_fc1.reshape(rows, seq_n, dp_n // seq_n, hid_here).transpose(1, 0, 2, 3)
    out_fc1 = to_owner(blocks).transpose(1, 2, 0, 3).reshape(rows, hid)
    qkv_slots = jnp.stack(
        seq_gather(sum_qkv.reshape(rows, 3, cols).transpose(1, 0, 2))
    ).reshape(3 * seq_n, rows, cols)
    out_qkv = []
    for i in range(3):
        block = 3 * seq + i
        at = ((block % seq_n) ^ seq) * 3 + block // seq_n
        out_qkv.append(lax.dynamic_index_in_dim(qkv_slots, at, 0, keepdims=False))
    out_qkv = jnp.concatenate(out_qkv, axis=1).astype(F32)
    return (
        output,
        stacked(grad_tokens),
        grad_cond,
        grad_wmod,
        grad_bmod,
        out_qkv,
        out_proj,
        out_fc1,
        bias_out,
        out_fc2,
    )


def solution(mesh):
    placed = (
        P("dp", "seq", None),
        P("dp", None),
        P("dp", None),
        P("dp"),
        P("dp", None),
        P("dp", None),
        P("dp", None),
        P("dp"),
        P("dp", None),
        P("dp", "seq", None),
    )
    return jax.shard_map(
        on_device,
        mesh=mesh,
        in_specs=placed,
        out_specs=(
            P("dp", "seq", None),
            P("dp", "seq", None),
            P("dp", None),
            P(None, ("dp", "seq")),
            P(("dp", "seq")),
            P("dp", "seq"),
            P("dp", "seq"),
            P("dp", "seq"),
            P(("dp", "seq")),
            P("dp", "seq"),
        ),
        check_vma=False,
    )
```

```python
import math
from functools import partial

import jax
import jax.numpy as jnp
from jax import lax
from jax.experimental import pallas as pl
from jax.experimental.pallas import tpu as pltpu
from jax.sharding import PartitionSpec as P

HEADS = 16
HEAD_DIM = 72
BF = jnp.bfloat16
F32 = jnp.float32
GELU_C = 0.7978845608028654
GELU_A = 0.044715
EXP2_SCALE = HEAD_DIM ** (-0.5) * math.log2(math.e)


def hop(value, axis, bits):
    count = lax.axis_size(axis)
    return lax.ppermute(value, axis, [(i, i ^ bits) for i in range(count)])


def matmul(left, right):
    return jnp.dot(left, right, preferred_element_type=F32)


def matmul_nt(left, right):
    return lax.dot_general(left, right, (((1,), (1,)), ((), ())), preferred_element_type=F32)


def matmul_tn(left, right):
    return lax.dot_general(left, right, (((0,), (0,)), ((), ())), preferred_element_type=F32)


def ln_parts(values):
    row_mean = jnp.mean(values, axis=-1, keepdims=True)
    centred = values - row_mean
    row_var = jnp.mean(centred * centred, axis=-1, keepdims=True)
    inv_std = lax.rsqrt(row_var + 1e-06)
    return centred * inv_std, inv_std


def ln_backward(grad, normed, inv_std):
    mean_grad = jnp.mean(grad, axis=-1, keepdims=True)
    mean_inner = jnp.mean(grad * normed, axis=-1, keepdims=True)
    return (grad - mean_grad - normed * mean_inner) * inv_std


def seq_gather(mine):
    slots = {0: mine}
    bit = lax.axis_size("seq") // 2
    while bit:
        for j in list(slots):
            slots[j | bit] = hop(slots[j], "seq", bit)
        bit //= 2
    return [slots[j] for j in range(len(slots))]


def seq_reduce(slots):
    slots = dict(enumerate(slots))
    bit = 1
    while len(slots) > 1:
        for j in [j for j in slots if j & bit]:
            slots[j ^ bit] = slots[j ^ bit] + hop(slots.pop(j).astype(BF), "seq", bit).astype(F32)
        bit *= 2
    return slots[0]


def seq_exchange(blocks):
    return [blocks[0]] + [hop(blocks[j], "seq", j) for j in range(1, len(blocks))]


def dp_exchange(value):
    return lax.all_to_all(value, "dp", 0, 0, tiled=True)


def dp_gather(mine, place):
    count = lax.axis_size("dp")
    index = lax.axis_index("dp")
    slots = {0: mine}
    for j in range(2, count, 2):
        slots[j] = hop(mine, "dp", j)
    for j in range(0, count, 2):
        slots[j + 1] = hop(slots[j], "dp", 1)
    whole = jnp.zeros((count,) + mine.shape, mine.dtype)
    for j in range(count):
        whole = lax.dynamic_update_index_in_dim(whole, slots[j], place(index ^ j), 0)
    return whole


def dp_scatter(terms, place):
    count = lax.axis_size("dp")
    index = lax.axis_index("dp")

    def block(j):
        return lax.dynamic_index_in_dim(terms, place(index ^ j), 0, keepdims=False)

    half = {}
    for j in list(range(2, count, 2)) + [0]:
        half[j] = block(j).astype(F32) + hop(block(j + 1), "dp", 1).astype(F32)
    total = half[0]
    for j in range(2, count, 2):
        total = total + hop(half[j].astype(BF), "dp", j).astype(F32)
    return total


def attend_kernel(heads, block, packed, after, mixed, log_sum, mixed_t):
    seq_len = packed.shape[1]
    cols = heads * HEAD_DIM
    for h in range(heads):
        at = h * HEAD_DIM
        keys = packed[0, :, cols + at : cols + at + HEAD_DIM]
        values_t = packed[0, :, 2 * cols + at : 2 * cols + at + HEAD_DIM].astype(F32).T.astype(BF)
        for start in range(0, seq_len, block):
            queries = packed[0, start : start + block, at : at + HEAD_DIM]
            scores = matmul_nt(keys, queries)
            top = jnp.max(scores, axis=0, keepdims=True)
            exponent = jnp.exp2((scores - top) * EXP2_SCALE)
            total = jnp.sum(exponent, axis=0, keepdims=True)
            part = matmul(values_t, exponent.astype(BF)) / total
            mixed_t[at : at + HEAD_DIM, start : start + block] = part
            log_sum[0, h : h + 1, start : start + block] = top * EXP2_SCALE + jnp.log2(total)
    mixed[0] = mixed_t[...].T.astype(BF)


def attend_grad_kernel(
    heads, block, packed, mixed, log_sum, d_mixed, after, d_packed, d_queries_t
):
    seq_len = packed.shape[1]
    cols = heads * HEAD_DIM
    inv_root = HEAD_DIM ** (-0.5)
    for h in range(heads):
        at = h * HEAD_DIM
        keys = packed[0, :, cols + at : cols + at + HEAD_DIM]
        values = packed[0, :, 2 * cols + at : 2 * cols + at + HEAD_DIM]
        keys_t = keys.astype(F32).T.astype(BF)
        d_keys = d_values = None
        for start in range(0, seq_len, block):
            queries = packed[0, start : start + block, at : at + HEAD_DIM]
            grads = d_mixed[0, start : start + block, at : at + HEAD_DIM]
            outs = mixed[0, start : start + block, at : at + HEAD_DIM]
            inner = jnp.sum(grads.astype(F32) * outs.astype(F32), axis=1, keepdims=True)
            inner = jnp.broadcast_to(inner, (block, 128)).T[0:1]
            scores = matmul_nt(keys, queries)
            probs = jnp.exp2(scores * EXP2_SCALE - log_sum[0, h : h + 1, start : start + block])
            d_probs = matmul_nt(values, grads)
            d_scores = (probs * (d_probs - inner)).astype(BF)
            d_v = matmul(probs.astype(BF), grads)
            d_k = matmul(d_scores, queries)
            d_values = d_v if d_values is None else d_values + d_v
            d_keys = d_k if d_keys is None else d_keys + d_k
            d_queries_t[at : at + HEAD_DIM, start : start + block] = matmul(keys_t, d_scores) * inv_root
        d_packed[0, :, cols + at : cols + at + HEAD_DIM] = (d_keys * inv_root).astype(BF)
        d_packed[0, :, 2 * cols + at : 2 * cols + at + HEAD_DIM] = d_values.astype(BF)
    d_packed[0, :, 0:cols] = d_queries_t[...].T.astype(BF)


def row_spec(*shape):
    return pl.BlockSpec((1,) + shape, lambda i: (i, 0, 0))


def attention(packed, after, heads, block=1024):
    lat, seq_len, _ = packed.shape
    cols = heads * HEAD_DIM
    return pl.pallas_call(
        partial(attend_kernel, heads, block),
        grid=(lat,),
        in_specs=[row_spec(seq_len, 3 * cols), pl.BlockSpec(memory_space=pl.ANY)],
        out_specs=[row_spec(seq_len, cols), row_spec(heads, seq_len)],
        out_shape=[
            jax.ShapeDtypeStruct((lat, seq_len, cols), BF),
            jax.ShapeDtypeStruct((lat, heads, seq_len), F32),
        ],
        scratch_shapes=[pltpu.VMEM((cols, seq_len), F32)],
        compiler_params=pltpu.CompilerParams(vmem_limit_bytes=48 * 2**20),
        name="attend",
    )(packed, after)


def attention_grad(packed, mixed, log_sum, d_mixed, after, heads, block=512):
    lat, seq_len, _ = packed.shape
    cols = heads * HEAD_DIM
    return pl.pallas_call(
        partial(attend_grad_kernel, heads, block),
        grid=(lat,),
        in_specs=[
            row_spec(seq_len, 3 * cols),
            row_spec(seq_len, cols),
            row_spec(heads, seq_len),
            row_spec(seq_len, cols),
            pl.BlockSpec(memory_space=pl.ANY),
        ],
        out_specs=row_spec(seq_len, 3 * cols),
        out_shape=jax.ShapeDtypeStruct((lat, seq_len, 3 * cols), BF),
        scratch_shapes=[pltpu.VMEM((cols, seq_len), F32)],
        compiler_params=pltpu.CompilerParams(vmem_limit_bytes=48 * 2**20),
        name="attend_grad",
    )(packed, mixed, log_sum, d_mixed, after)


def qkv_kernel(count, *refs):
    slots, (shift, scale, qkv, normed, packed) = refs[:count], refs[count:]
    chunk, width = slots[0].shape[1:]
    for j in range(count):
        value = ln_parts(slots[j][0].astype(F32))[0] * (1.0 + scale[0]) + shift[0]
        normed[0, j] = value.astype(BF)
    rows = normed[0].reshape(count * chunk, width)
    packed[0] = matmul(rows, qkv[...]).astype(BF).reshape(count, chunk, packed.shape[3])


def qkv_forward(slots, group, per, shift, scale, qkv):
    count = len(slots)
    _, tok, width = slots[0].shape
    chunk = max(16, 256 // count)
    row = pl.BlockSpec((1, 1, width), lambda i, c: (i, 0, 0))
    cols = qkv.shape[1]
    return pl.pallas_call(
        partial(qkv_kernel, count),
        grid=(per, tok // chunk),
        in_specs=[pl.BlockSpec((1, chunk, width), lambda i, c: (group * per + i, c, 0))] * count
        + [row, row, pl.BlockSpec((width, cols), lambda i, c: (0, 0))],
        out_specs=[
            pl.BlockSpec((1, count, chunk, width), lambda i, c: (i, 0, c, 0)),
            pl.BlockSpec((1, count, chunk, cols), lambda i, c: (i, 0, c, 0)),
        ],
        out_shape=[
            jax.ShapeDtypeStruct((per, count, tok, width), BF),
            jax.ShapeDtypeStruct((per, count, tok, cols), BF),
        ],
        compiler_params=pltpu.CompilerParams(vmem_limit_bytes=48 * 2**20),
        name="qkv_forward",
    )(*slots, shift, scale, qkv)


def mlp_kernel(count, *refs):
    inputs, grads = refs[:count], refs[count : 2 * count]
    gate, fc1, bias, fc2, x_all, g_all, activated, d_hidden, d_norm, d_bias = refs[2 * count :]
    chunk, width = inputs[0].shape[1:]
    hid = fc1.shape[1]
    for j in range(count):
        x_all[0, j] = inputs[j][0]
        g_all[0, j] = (gate[0] * grads[j][0].astype(F32)).astype(BF)
    x = x_all[0].reshape(count * chunk, width)
    g = g_all[0].reshape(count * chunk, width)
    hidden = matmul(x, fc1[...]) + bias[...]
    square = hidden * hidden
    tanh = jnp.tanh(GELU_C * (hidden + GELU_A * hidden * square))
    half = 0.5 * (1.0 + tanh)
    activated[0] = (hidden * half).astype(BF).reshape(count, chunk, hid)
    slope = half + (0.5 * GELU_C) * hidden * (1.0 - tanh * tanh) * (1.0 + 3.0 * GELU_A * square)
    d_h = (matmul_nt(g, fc2[...]) * slope).astype(BF)
    d_hidden[0] = d_h.reshape(count, chunk, hid)
    d_norm[0] = matmul_nt(d_h, fc1[...]).astype(BF).reshape(count, chunk, width)

    @pl.when((pl.program_id(0) == 0) & (pl.program_id(1) == 0))
    def _():
        d_bias[...] = jnp.zeros_like(d_bias)

    d_bias[...] += jnp.sum(d_h.astype(F32), axis=0, keepdims=True)


def mlp(inputs, grads, group, gate, fc1, bias, fc2):
    count = len(inputs)
    per, tok, width = inputs[0].shape
    hid = fc1.shape[1]
    chunk = max(16, 256 // count)
    slot = pl.BlockSpec((1, chunk, width), lambda i, c: (i, c, 0))
    late = pl.BlockSpec((1, chunk, width), lambda i, c: (group * per + i, c, 0))

    def whole(rows, cols):
        return pl.BlockSpec((rows, cols), lambda i, c: (0, 0))

    wide = pl.BlockSpec((1, count, chunk, width), lambda i, c: (i, 0, c, 0))
    inner = pl.BlockSpec((1, count, chunk, hid), lambda i, c: (i, 0, c, 0))
    shape_wide = jax.ShapeDtypeStruct((per, count, tok, width), BF)
    shape_inner = jax.ShapeDtypeStruct((per, count, tok, hid), BF)
    return pl.pallas_call(
        partial(mlp_kernel, count),
        grid=(per, tok // chunk),
        in_specs=[slot] * count
        + [late] * count
        + [pl.BlockSpec((1, 1, width), lambda i, c: (i, 0, 0))]
        + [whole(width, hid), whole(1, hid), whole(hid, width)],
        out_specs=[wide, wide, inner, inner, wide, whole(1, hid)],
        out_shape=[shape_wide, shape_wide, shape_inner, shape_inner, shape_wide]
        + [jax.ShapeDtypeStruct((1, hid), F32)],
        compiler_params=pltpu.CompilerParams(vmem_limit_bytes=56 * 2**20),
        name="mlp",
    )(*inputs, *grads, gate, fc1, bias, fc2)


def mlp_out_kernel(activated, fc2, after, out):
    count, chunk, hid = activated.shape[1:]
    rows = activated[0].reshape(count * chunk, hid)
    out[0] = matmul(rows, fc2[...]).astype(BF).reshape(count, chunk, out.shape[3])


def mlp_out_terms(activated, fc2, after):
    per, count, tok, hid = activated.shape
    width = fc2.shape[1]
    chunk = max(16, 256 // count)
    return pl.pallas_call(
        mlp_out_kernel,
        grid=(per, tok // chunk),
        in_specs=[
            pl.BlockSpec((1, count, chunk, hid), lambda i, c: (i, 0, c, 0)),
            pl.BlockSpec((hid, width), lambda i, c: (0, 0)),
            pl.BlockSpec(memory_space=pl.ANY),
        ],
        out_specs=pl.BlockSpec((1, count, chunk, width), lambda i, c: (i, 0, c, 0)),
        out_shape=jax.ShapeDtypeStruct((per, count, tok, width), BF),
        compiler_params=pltpu.CompilerParams(vmem_limit_bytes=48 * 2**20),
        name="mlp_out_terms",
    )(activated, fc2, after)


def resid_grad_kernel(count, *refs):
    d_norm, resid_mid, attn_out, cotangent, scale, gate, proj, after = refs[:8]
    d_resid, d_attn, d_shift, d_scale, d_gate = refs[8:13]
    d_attended = refs[13:]
    normed, inv_std = ln_parts(resid_mid[0])
    grad = d_norm[0]
    total = cotangent[0].astype(F32) + ln_backward(grad * (1.0 + scale[0]), normed, inv_std)
    d_resid[0] = total
    d_a = (gate[0] * total).astype(BF)
    d_attn[0] = d_a
    back = matmul_nt(d_a, proj[...]).astype(BF)
    cols = back.shape[1] // count
    for j in range(count):
        d_attended[j][0] = back[:, j * cols : (j + 1) * cols]

    @pl.when(pl.program_id(1) == 0)
    def _():
        d_shift[...] = jnp.zeros_like(d_shift)
        d_scale[...] = jnp.zeros_like(d_scale)
        d_gate[...] = jnp.zeros_like(d_gate)

    d_shift[0] += jnp.sum(grad, axis=0, keepdims=True)
    d_scale[0] += jnp.sum(grad * normed, axis=0, keepdims=True)
    d_gate[0] += jnp.sum(total * attn_out[0], axis=0, keepdims=True)


def resid_grad(d_norm, resid_mid, attn_out, cotangent, group, scale, gate, proj, after, count):
    per, tok, width = d_norm.shape
    chunk = min(tok, 128)
    block = pl.BlockSpec((1, chunk, width), lambda i, c: (i, c, 0))
    row = pl.BlockSpec((1, 1, width), lambda i, c: (i, 0, 0))
    part = pl.BlockSpec((1, chunk, width // count), lambda i, c: (i, c, 0))
    row_shape = jax.ShapeDtypeStruct((per, 1, width), F32)
    return pl.pallas_call(
        partial(resid_grad_kernel, count),
        grid=(per, tok // chunk),
        in_specs=[
            block,
            block,
            block,
            pl.BlockSpec((1, chunk, width), lambda i, c: (group * per + i, c, 0)),
            row,
            row,
            pl.BlockSpec((width, width), lambda i, c: (0, 0)),
            pl.BlockSpec(memory_space=pl.ANY),
        ],
        out_specs=[block, block, row, row, row] + [part] * count,
        out_shape=[
            jax.ShapeDtypeStruct((per, tok, width), F32),
            jax.ShapeDtypeStruct((per, tok, width), BF),
            row_shape,
            row_shape,
            row_shape,
        ]
        + [jax.ShapeDtypeStruct((per, tok, width // count), BF)] * count,
        compiler_params=pltpu.CompilerParams(vmem_limit_bytes=48 * 2**20),
        name="resid_grad",
    )(d_norm, resid_mid, attn_out, cotangent, scale, gate, proj, after)


def unpack_kernel(joined, after, *parts):
    start = 0
    for part in parts:
        part[0] = joined[0, start : start + part.shape[1]]
        start += part.shape[1]


def unpack(joined, after, row_counts):
    count, rows, width = joined.shape
    return pl.pallas_call(
        unpack_kernel,
        grid=(count,),
        in_specs=[
            pl.BlockSpec((1, rows, width), lambda i: (i, 0, 0)),
            pl.BlockSpec(memory_space=pl.ANY),
        ],
        out_specs=[pl.BlockSpec((1, n, width), lambda i: (i, 0, 0)) for n in row_counts],
        out_shape=[jax.ShapeDtypeStruct((count, n, width), joined.dtype) for n in row_counts],
        compiler_params=pltpu.CompilerParams(vmem_limit_bytes=32 * 2**20),
        name="unpack",
    )(joined, after)


def on_device(tokens, conditioning, w_mod, b_mod, w_qkv, w_proj, w_fc1, b_fc1, w_fc2, cotangent):
    lat, tok, width = tokens.shape
    seq_n = lax.axis_size("seq")
    dp_n = lax.axis_size("dp")
    seq = lax.axis_index("seq")
    dp = lax.axis_index("dp")
    core = seq % 2
    heads_here = HEADS // seq_n
    cols = heads_here * HEAD_DIM
    seq_len = tok * seq_n
    rows = w_qkv.shape[0]
    hid_here = w_fc2.shape[0] // seq_n
    hid = hid_here * dp_n
    groups = 2
    per = lat // groups
    own = per * tok

    cond_silu, silu_back = jax.vjp(jax.nn.silu, conditioning)
    cond_act = cond_silu.astype(BF)
    bias_here = lax.dynamic_slice(b_fc1, (seq * hid_here,), (hid_here,))
    small = jnp.concatenate([cond_act.reshape(lat * width), bias_here])
    small = dp_exchange(jnp.broadcast_to(small[None], (dp_n, lat * width + hid_here)))
    cond_all = small[:, : lat * width].reshape(dp_n * lat, width)
    fc1_bias = small[:, lat * width :].reshape(hid).astype(F32)
    cond_rows = lax.dynamic_slice(cond_all, (0, dp * rows), (dp_n * lat, rows))
    mod_terms = matmul(cond_rows, w_mod)
    piece = b_mod.shape[0]
    mod_terms = lax.dynamic_update_slice(
        mod_terms,
        lax.dynamic_slice(mod_terms, (0, dp * piece), (dp_n * lat, piece))
        + b_mod.astype(F32)[None],
        (0, dp * piece),
    )
    modulation = jnp.sum(dp_exchange(mod_terms.reshape(dp_n, lat, 6 * width)), axis=0)

    tok_slots = seq_gather(tokens)
    cot_slots = seq_gather(cotangent)

    qkv_here = jnp.concatenate(
        [lax.dynamic_slice(w_qkv, (0, t * width + seq * cols), (rows, cols)) for t in range(3)],
        axis=1,
    )
    qkv = dp_gather(qkv_here, lambda d: d).reshape(width, 3 * cols)
    half = rows // 2
    fc1_here = jnp.concatenate(
        [
            lax.dynamic_slice(w_fc1, (0, (d * seq_n + seq) * hid_here), (rows, hid_here))
            for d in range(dp_n)
        ],
        axis=1,
    )
    fc2_here = lax.dynamic_slice(w_fc2, (seq * hid_here, 0), (hid_here, width))
    proj_here = lax.dynamic_slice(w_proj, (core * half, 0), (half, width))
    together = hid == width
    if together:
        joined = lax.all_gather(jnp.concatenate([fc1_here, fc2_here, proj_here]), "dp", axis=0)
    else:
        proj_mine = lax.all_gather(proj_here, "dp", axis=0)
        fc1 = lax.all_gather(fc1_here, "dp", axis=0, tiled=True)
        fc2 = lax.all_gather(fc2_here, "dp", axis=0, tiled=True)
    def part(g):
        return slice(g * per, (g + 1) * per)

    shift_attn, scale_attn, gate_attn, shift_mlp, scale_mlp, gate_mlp = [
        [modulation[part(g), None, i * width : (i + 1) * width] for g in range(groups)]
        for i in range(6)
    ]
    token_values = [tokens[part(g)].astype(F32) for g in range(groups)]
    normed_all, packed, mixed, log_sums, attended = [], [], [], [], []
    for g in range(groups):
        normed, rows_packed = qkv_forward(tok_slots, g, per, shift_attn[g], scale_attn[g], qkv)
        normed_all.append(normed.reshape(per * seq_len, width))
        packed.append(rows_packed.reshape(per, seq_len, 3 * cols))
        out, log_sum = attention(packed[g], tokens if g == 0 else cot_slots[-1], heads_here)
        mixed.append(out)
        log_sums.append(log_sum)
        out = out.reshape(per, seq_n, tok, cols)
        attended.append(
            jnp.concatenate(seq_exchange([out[:, j] for j in range(seq_n)]), axis=2).reshape(
                own, width
            )
        )

    if together:
        fc1, fc2, proj_mine = unpack(joined, mixed[-1], [rows, hid_here, half])
        fc1, fc2 = fc1.reshape(width, hid), fc2.reshape(hid, width)
    proj_other = hop(proj_mine, "seq", 1)
    proj = jnp.where(
        core == 0,
        jnp.stack([proj_mine, proj_other], axis=1),
        jnp.stack([proj_other, proj_mine], axis=1),
    ).reshape(seq_n, cols, width)

    def by_place(blocks):
        return jnp.concatenate(
            [lax.dynamic_index_in_dim(blocks, seq ^ j, 0, keepdims=False) for j in range(seq_n)]
        )

    proj = by_place(proj)

    attn_out, resid_mid, normed_mlp, upstream = [], [], [], []
    for g in range(groups):
        attn_out.append(matmul(attended[g], proj).reshape(per, tok, width))
        resid_mid.append(token_values[g] + gate_attn[g] * attn_out[g])
        normed_mlp.append(
            (ln_parts(resid_mid[g])[0] * (1.0 + scale_mlp[g]) + shift_mlp[g]).astype(BF)
        )
        upstream.append(cotangent[part(g)].astype(F32))

    grad_fc1 = grad_fc2 = grad_bias1 = 0.0
    d_norm, activated = [], []
    for g in range(groups):
        x_all, d_mlp, active, d_hidden, terms, d_bias = mlp(
            seq_gather(normed_mlp[g]), cot_slots, g, gate_mlp[g], fc1, fc1_bias[None], fc2
        )
        d_norm.append(seq_reduce([terms[:, j].astype(F32) for j in range(seq_n)]))
        activated.append(active)
        flat = per * seq_len
        grad_fc2 = grad_fc2 + matmul_tn(active.reshape(flat, hid), d_mlp.reshape(flat, width))
        grad_fc1 = grad_fc1 + matmul_tn(x_all.reshape(flat, width), d_hidden.reshape(flat, hid))
        grad_bias1 = grad_bias1 + d_bias[0]
    grad_fc1 = grad_fc1.astype(BF).reshape(dp_n, rows, hid)
    grad_fc2 = grad_fc2.astype(BF).reshape(dp_n, hid_here, width)
    if together:
        grad_fc = jnp.concatenate([grad_fc1, grad_fc2], axis=1)
        sum_fc = lax.psum_scatter(grad_fc, "dp", scatter_dimension=0)
        sum_fc1, sum_fc2 = sum_fc[:rows], sum_fc[rows:]
    else:
        grad_fc = grad_fc1
        sum_fc1 = lax.psum_scatter(grad_fc1, "dp", scatter_dimension=0)
        sum_fc2 = lax.psum_scatter(grad_fc2, "dp", scatter_dimension=0)

    def stacked(terms):
        return jnp.concatenate(terms)

    d_shift_mlp, d_scale_mlp, d_gate_attn, d_resid, d_attn, d_attended = ([] for _ in range(6))
    d_mixed = []
    for g in range(groups):
        outs = resid_grad(
            d_norm[g], resid_mid[g], attn_out[g], cotangent, g, scale_mlp[g], gate_attn[g], proj,
            grad_fc, seq_n,
        )
        d_resid.append(outs[0])
        d_attn.append(outs[1].reshape(own, width))
        d_shift_mlp.append(outs[2][:, 0])
        d_scale_mlp.append(outs[3][:, 0])
        d_gate_attn.append(outs[4][:, 0])
        d_attended.append(outs[5])
        d_mixed.append(jnp.concatenate(seq_exchange(outs[5:]), axis=1))
    mlp_out = []
    for g in range(groups):
        terms = mlp_out_terms(activated[g], fc2, d_attended[-1])
        mlp_out.append(seq_reduce([terms[:, j].astype(F32) for j in range(seq_n)]))
    output = jnp.concatenate(
        [(resid_mid[g] + gate_mlp[g] * mlp_out[g]).astype(BF) for g in range(groups)]
    )
    d_gate_mlp = stacked([jnp.sum(upstream[g] * mlp_out[g], axis=1) for g in range(groups)])
    grad_proj = by_place(
        matmul_tn(stacked(attended), stacked(d_attn)).astype(BF).reshape(seq_n, cols, width)
    ).reshape(dp_n, rows, 2, width // 2)
    proj_sent = hop(
        lax.dynamic_index_in_dim(grad_proj, 1 - core, axis=2, keepdims=False), "seq", 1
    )
    proj_terms = lax.dynamic_index_in_dim(grad_proj, core, axis=2, keepdims=False).astype(F32)
    proj_terms = (proj_terms + proj_sent.astype(F32)).astype(BF)

    d_packed, d_first = [], []
    for g in range(groups):
        d_packed.append(
            attention_grad(
                packed[g], mixed[g], log_sums[g], d_mixed[g], d_attended[-1], heads_here
            ).reshape(
                per * seq_len, 3 * cols
            )
        )
        parts = matmul_nt(d_packed[g], qkv).reshape(per, seq_n, tok, width)
        d_first.append(seq_reduce([parts[:, j] for j in range(seq_n)]))
    grad_qkv = matmul_tn(stacked(normed_all), stacked(d_packed)).astype(BF)
    sum_last = lax.psum_scatter(
        jnp.concatenate([proj_terms, grad_qkv.reshape(dp_n, rows, 3 * cols)], axis=2),
        "dp",
        scatter_dimension=0,
    )
    sum_proj, sum_qkv = sum_last[:, : width // 2], sum_last[:, width // 2 :]
    d_shift_attn, d_scale_attn, grad_tokens = [], [], []
    for g in range(groups):
        normed_tok, std_tok = ln_parts(token_values[g])
        d_shift_attn.append(jnp.sum(d_first[g], axis=1))
        d_scale_attn.append(jnp.sum(d_first[g] * normed_tok, axis=1))
        grad_tokens.append(
            d_resid[g] + ln_backward(d_first[g] * (1.0 + scale_attn[g]), normed_tok, std_tok)
        )

    mod_part = jnp.concatenate(
        [stacked(d_shift_attn), stacked(d_scale_attn), stacked(d_gate_attn)]
        + [stacked(d_shift_mlp), stacked(d_scale_mlp), d_gate_mlp],
        axis=1,
    )
    bit = 1
    while bit < seq_n:
        mod_part = mod_part + hop(mod_part, "seq", bit)
        bit *= 2
    d_mod = dp_exchange(jnp.broadcast_to(mod_part.astype(BF)[None], (dp_n, lat, 6 * width)))
    d_mod = d_mod.reshape(dp_n * lat, 6 * width)
    share = 6 * width // (dp_n * seq_n)
    mod_cols = lax.dynamic_slice(d_mod, (0, (dp * seq_n + seq) * share), (dp_n * lat, share))
    grad_wmod = matmul_tn(cond_all, mod_cols)
    grad_bmod = jnp.sum(mod_cols.astype(F32), axis=0)
    d_cond = dp_exchange(matmul_nt(d_mod, w_mod).reshape(dp_n, lat, rows))
    (grad_cond,) = silu_back(d_cond.transpose(1, 0, 2).reshape(lat, width))

    bias_out = jnp.sum(dp_exchange(grad_bias1.reshape(dp_n, hid_here)), axis=0)

    def to_owner(blocks):
        return lax.all_to_all(blocks, "seq", 0, 0, tiled=True).astype(F32)

    share = width // seq_n
    fc2_blocks = sum_fc2.reshape(hid_here, seq_n, share).transpose(1, 0, 2)
    fc1_blocks = sum_fc1.reshape(rows, seq_n, hid // seq_n).transpose(1, 0, 2)
    if together:
        received = to_owner(jnp.concatenate([fc1_blocks, fc2_blocks], axis=1))
        out_fc1, out_fc2 = received[:, :rows], received[:, rows:]
    else:
        out_fc1, out_fc2 = to_owner(fc1_blocks), to_owner(fc2_blocks)
    out_fc2 = out_fc2.reshape(seq_n * hid_here, share)
    out_fc1 = out_fc1.reshape(seq_n, rows, dp_n // seq_n, hid_here).transpose(1, 2, 0, 3)
    out_fc1 = out_fc1.reshape(rows, hid)
    owners = jnp.arange(seq_n)
    proj_blocks = jnp.where(
        (owners // (seq_n // 2) == core)[:, None, None],
        jnp.tile(sum_proj.reshape(rows, seq_n // 2, share).transpose(1, 0, 2), (2, 1, 1)),
        0,
    )
    qkv_thirds = sum_qkv.reshape(rows, 3, cols).transpose(1, 0, 2)
    qkv_blocks = jnp.stack(
        [
            lax.dynamic_index_in_dim(
                qkv_thirds, jnp.minimum((3 * to - seq + seq_n - 1) // seq_n, 2), 0, keepdims=False
            )
            for to in range(seq_n)
        ]
    )
    received = to_owner(jnp.concatenate([proj_blocks, qkv_blocks], axis=1))
    out_proj = jnp.sum(received[:, :rows], axis=0)
    out_qkv = jnp.concatenate(
        [
            lax.dynamic_index_in_dim(received, (3 * seq + i) % seq_n, 0, keepdims=False)[rows:]
            for i in range(3)
        ],
        axis=1,
    )
    return (
        output,
        stacked(grad_tokens),
        grad_cond,
        grad_wmod,
        grad_bmod,
        out_qkv,
        out_proj,
        out_fc1,
        bias_out,
        out_fc2,
    )


def solution(mesh):
    placed = (
        P("dp", "seq", None),
        P("dp", None),
        P("dp", None),
        P("dp"),
        P("dp", None),
        P("dp", None),
        P("dp", None),
        P("dp"),
        P("dp", None),
        P("dp", "seq", None),
    )
    return jax.shard_map(
        on_device,
        mesh=mesh,
        in_specs=placed,
        out_specs=(
            P("dp", "seq", None),
            P("dp", "seq", None),
            P("dp", None),
            P(None, ("dp", "seq")),
            P(("dp", "seq")),
            P("dp", "seq"),
            P("dp", "seq"),
            P("dp", "seq"),
            P(("dp", "seq")),
            P("dp", "seq"),
        ),
        check_vma=False,
    )
```

```python
import math
from functools import partial

import jax
import jax.numpy as jnp
from jax import lax
from jax.experimental import pallas as pl
from jax.experimental.pallas import tpu as pltpu
from jax.sharding import PartitionSpec as P

HEADS = 16
HEAD_DIM = 72
BF = jnp.bfloat16
F32 = jnp.float32
GELU_C = 0.7978845608028654
GELU_A = 0.044715
VMEM_LIMIT = 60 * 2**20
EXP2_SCALE = HEAD_DIM ** (-0.5) * math.log2(math.e)


def hop(value, axis, bits):
    count = lax.axis_size(axis)
    return lax.ppermute(value, axis, [(i, i ^ bits) for i in range(count)])


def matmul(left, right):
    return jnp.dot(left, right, preferred_element_type=F32)


def matmul_nt(left, right):
    return lax.dot_general(left, right, (((1,), (1,)), ((), ())), preferred_element_type=F32)


def matmul_tn(left, right):
    return lax.dot_general(left, right, (((0,), (0,)), ((), ())), preferred_element_type=F32)


def ln_parts(values):
    row_mean = jnp.mean(values, axis=-1, keepdims=True)
    centred = values - row_mean
    row_var = jnp.mean(centred * centred, axis=-1, keepdims=True)
    inv_std = lax.rsqrt(row_var + 1e-06)
    return centred * inv_std, inv_std


def ln_backward(grad, normed, inv_std):
    mean_grad = jnp.mean(grad, axis=-1, keepdims=True)
    mean_inner = jnp.mean(grad * normed, axis=-1, keepdims=True)
    return (grad - mean_grad - normed * mean_inner) * inv_std


def seq_gather(mine):
    slots = {0: mine}
    bit = lax.axis_size("seq") // 2
    while bit:
        for j in list(slots):
            slots[j | bit] = hop(slots[j], "seq", bit)
        bit //= 2
    return [slots[j] for j in range(len(slots))]


def seq_reduce(slots):
    slots = dict(enumerate(slots))
    bit = 1
    while len(slots) > 1:
        for j in [j for j in slots if j & bit]:
            slots[j ^ bit] = slots[j ^ bit] + hop(slots.pop(j).astype(BF), "seq", bit).astype(F32)
        bit *= 2
    return slots[0]


def seq_exchange(blocks):
    return [blocks[0]] + [hop(blocks[j], "seq", j) for j in range(1, len(blocks))]


def dp_exchange(value):
    return lax.all_to_all(value, "dp", 0, 0, tiled=True)


def dp_gather(mine, place):
    count = lax.axis_size("dp")
    index = lax.axis_index("dp")
    slots = {0: mine}
    for j in range(2, count, 2):
        slots[j] = hop(mine, "dp", j)
    for j in range(0, count, 2):
        slots[j + 1] = hop(slots[j], "dp", 1)
    whole = jnp.zeros((count,) + mine.shape, mine.dtype)
    for j in range(count):
        whole = lax.dynamic_update_index_in_dim(whole, slots[j], place(index ^ j), 0)
    return whole


def dp_scatter(terms, place):
    count = lax.axis_size("dp")
    index = lax.axis_index("dp")

    def block(j):
        return lax.dynamic_index_in_dim(terms, place(index ^ j), 0, keepdims=False)

    half = {}
    for j in list(range(2, count, 2)) + [0]:
        half[j] = block(j).astype(F32) + hop(block(j + 1), "dp", 1).astype(F32)
    total = half[0]
    for j in range(2, count, 2):
        total = total + hop(half[j].astype(BF), "dp", j).astype(F32)
    return total


def attend_kernel(heads, block, packed, *refs):
    mixed, log_sum, mixed_t = refs[-3:]
    seq_len = packed.shape[1]
    cols = heads * HEAD_DIM
    for h in range(heads):
        at = h * HEAD_DIM
        keys = packed[0, :, cols + at : cols + at + HEAD_DIM]
        values_t = packed[0, :, 2 * cols + at : 2 * cols + at + HEAD_DIM].astype(F32).T.astype(BF)
        for start in range(0, seq_len, block):
            queries = packed[0, start : start + block, at : at + HEAD_DIM]
            scores = matmul_nt(keys, queries)
            top = jnp.max(scores, axis=0, keepdims=True)
            exponent = jnp.exp2((scores - top) * EXP2_SCALE)
            total = jnp.sum(exponent, axis=0, keepdims=True)
            part = matmul(values_t, exponent.astype(BF)) / total
            mixed_t[at : at + HEAD_DIM, start : start + block] = part
            log_sum[0, h : h + 1, start : start + block] = top * EXP2_SCALE + jnp.log2(total)
    mixed[0] = mixed_t[...].T.astype(BF)


def attend_grad_kernel(heads, block, packed, mixed, log_sum, d_mixed, qkv, *refs):
    d_packed, terms, d_queries_t = refs[-3:]
    seq_len = packed.shape[1]
    cols = heads * HEAD_DIM
    inv_root = HEAD_DIM ** (-0.5)
    for h in range(heads):
        at = h * HEAD_DIM
        keys = packed[0, :, cols + at : cols + at + HEAD_DIM]
        values = packed[0, :, 2 * cols + at : 2 * cols + at + HEAD_DIM]
        keys_t = keys.astype(F32).T.astype(BF)
        d_keys = d_values = None
        for start in range(0, seq_len, block):
            queries = packed[0, start : start + block, at : at + HEAD_DIM]
            grads = d_mixed[0, start : start + block, at : at + HEAD_DIM]
            outs = mixed[0, start : start + block, at : at + HEAD_DIM]
            inner = jnp.sum(grads.astype(F32) * outs.astype(F32), axis=1, keepdims=True)
            inner = jnp.broadcast_to(inner, (block, 128)).T[0:1]
            scores = matmul_nt(keys, queries)
            probs = jnp.exp2(scores * EXP2_SCALE - log_sum[0, h : h + 1, start : start + block])
            d_probs = matmul_nt(values, grads)
            d_scores = (probs * (d_probs - inner)).astype(BF)
            d_v = matmul(probs.astype(BF), grads)
            d_k = matmul(d_scores, queries)
            d_values = d_v if d_values is None else d_values + d_v
            d_keys = d_k if d_keys is None else d_keys + d_k
            d_queries_t[at : at + HEAD_DIM, start : start + block] = matmul(keys_t, d_scores) * inv_root
        d_packed[0, :, cols + at : cols + at + HEAD_DIM] = (d_keys * inv_root).astype(BF)
        d_packed[0, :, 2 * cols + at : 2 * cols + at + HEAD_DIM] = d_values.astype(BF)
    d_packed[0, :, 0:cols] = d_queries_t[...].T.astype(BF)
    for start in range(0, seq_len, block):
        rows = d_packed[0, start : start + block]
        terms[0, start : start + block] = matmul_nt(rows, qkv[...]).astype(BF)


def row_spec(*shape):
    return pl.BlockSpec((1,) + shape, lambda i: (i, 0, 0))


def attention(packed, after, heads, block=1024):
    lat, seq_len, _ = packed.shape
    cols = heads * HEAD_DIM
    return pl.pallas_call(
        partial(attend_kernel, heads, block),
        grid=(lat,),
        in_specs=[row_spec(seq_len, 3 * cols)] + [pl.BlockSpec(memory_space=pl.ANY)] * len(after),
        out_specs=[row_spec(seq_len, cols), row_spec(heads, seq_len)],
        out_shape=[
            jax.ShapeDtypeStruct((lat, seq_len, cols), BF),
            jax.ShapeDtypeStruct((lat, heads, seq_len), F32),
        ],
        scratch_shapes=[pltpu.VMEM((cols, seq_len), F32)],
        compiler_params=pltpu.CompilerParams(vmem_limit_bytes=VMEM_LIMIT),
        name="attend",
    )(packed, *after)


def attention_grad(packed, mixed, log_sum, d_mixed, qkv, after, heads, block=512):
    lat, seq_len, _ = packed.shape
    cols = heads * HEAD_DIM
    return pl.pallas_call(
        partial(attend_grad_kernel, heads, block),
        grid=(lat,),
        in_specs=[
            row_spec(seq_len, 3 * cols),
            row_spec(seq_len, cols),
            row_spec(heads, seq_len),
            row_spec(seq_len, cols),
            pl.BlockSpec(qkv.shape, lambda i: (0, 0)),
        ]
        + [pl.BlockSpec(memory_space=pl.ANY)] * len(after),
        out_specs=[row_spec(seq_len, 3 * cols), row_spec(seq_len, qkv.shape[0])],
        out_shape=[
            jax.ShapeDtypeStruct((lat, seq_len, 3 * cols), BF),
            jax.ShapeDtypeStruct((lat, seq_len, qkv.shape[0]), BF),
        ],
        scratch_shapes=[pltpu.VMEM((cols, seq_len), F32)],
        compiler_params=pltpu.CompilerParams(vmem_limit_bytes=VMEM_LIMIT),
        name="attend_grad",
    )(packed, mixed, log_sum, d_mixed, qkv, *after)


def qkv_kernel(count, *refs):
    slots, (shift, scale, qkv, normed, packed) = refs[:count], refs[count:]
    chunk, width = slots[0].shape[1:]
    for j in range(count):
        value = ln_parts(slots[j][0].astype(F32))[0] * (1.0 + scale[0]) + shift[0]
        normed[0, j] = value.astype(BF)
    rows = normed[0].reshape(count * chunk, width)
    packed[0] = matmul(rows, qkv[...]).astype(BF).reshape(count, chunk, packed.shape[3])


def qkv_forward(slots, group, per, shift, scale, qkv):
    count = len(slots)
    _, tok, width = slots[0].shape
    chunk = max(16, 256 // count)
    row = pl.BlockSpec((1, 1, width), lambda i, c: (i, 0, 0))
    cols = qkv.shape[1]
    return pl.pallas_call(
        partial(qkv_kernel, count),
        grid=(per, tok // chunk),
        in_specs=[pl.BlockSpec((1, chunk, width), lambda i, c: (group * per + i, c, 0))] * count
        + [row, row, pl.BlockSpec((width, cols), lambda i, c: (0, 0))],
        out_specs=[
            pl.BlockSpec((1, count, chunk, width), lambda i, c: (i, 0, c, 0)),
            pl.BlockSpec((1, count, chunk, cols), lambda i, c: (i, 0, c, 0)),
        ],
        out_shape=[
            jax.ShapeDtypeStruct((per, count, tok, width), BF),
            jax.ShapeDtypeStruct((per, count, tok, cols), BF),
        ],
        compiler_params=pltpu.CompilerParams(vmem_limit_bytes=VMEM_LIMIT),
        name="qkv_forward",
    )(*slots, shift, scale, qkv)


def mlp_kernel(count, *refs):
    inputs, grads = refs[:count], refs[count : 2 * count]
    gate, fc1, bias, fc2, x_all, g_all, activated, d_hidden, d_norm, d_bias = refs[2 * count :]
    chunk, width = inputs[0].shape[1:]
    hid = fc1.shape[1]
    for j in range(count):
        x_all[0, j] = inputs[j][0]
        g_all[0, j] = (gate[0] * grads[j][0].astype(F32)).astype(BF)
    x = x_all[0].reshape(count * chunk, width)
    g = g_all[0].reshape(count * chunk, width)
    hidden = matmul(x, fc1[...]) + bias[...]
    square = hidden * hidden
    tanh = jnp.tanh(GELU_C * (hidden + GELU_A * hidden * square))
    half = 0.5 * (1.0 + tanh)
    activated[0] = (hidden * half).astype(BF).reshape(count, chunk, hid)
    slope = half + (0.5 * GELU_C) * hidden * (1.0 - tanh * tanh) * (1.0 + 3.0 * GELU_A * square)
    d_h = (matmul_nt(g, fc2[...]) * slope).astype(BF)
    d_hidden[0] = d_h.reshape(count, chunk, hid)
    d_norm[0] = matmul_nt(d_h, fc1[...]).astype(BF).reshape(count, chunk, width)

    @pl.when((pl.program_id(0) == 0) & (pl.program_id(1) == 0))
    def _():
        d_bias[...] = jnp.zeros_like(d_bias)

    d_bias[...] += jnp.sum(d_h.astype(F32), axis=0, keepdims=True)


def mlp(inputs, grads, group, gate, fc1, bias, fc2):
    count = len(inputs)
    per, tok, width = inputs[0].shape
    hid = fc1.shape[1]
    chunk = max(16, 256 // count)
    slot = pl.BlockSpec((1, chunk, width), lambda i, c: (i, c, 0))
    late = pl.BlockSpec((1, chunk, width), lambda i, c: (group * per + i, c, 0))

    def whole(rows, cols):
        return pl.BlockSpec((rows, cols), lambda i, c: (0, 0))

    wide = pl.BlockSpec((1, count, chunk, width), lambda i, c: (i, 0, c, 0))
    inner = pl.BlockSpec((1, count, chunk, hid), lambda i, c: (i, 0, c, 0))
    shape_wide = jax.ShapeDtypeStruct((per, count, tok, width), BF)
    shape_inner = jax.ShapeDtypeStruct((per, count, tok, hid), BF)
    return pl.pallas_call(
        partial(mlp_kernel, count),
        grid=(per, tok // chunk),
        in_specs=[slot] * count
        + [late] * count
        + [pl.BlockSpec((1, 1, width), lambda i, c: (i, 0, 0))]
        + [whole(width, hid), whole(1, hid), whole(hid, width)],
        out_specs=[wide, wide, inner, inner, wide, whole(1, hid)],
        out_shape=[shape_wide, shape_wide, shape_inner, shape_inner, shape_wide]
        + [jax.ShapeDtypeStruct((1, hid), F32)],
        compiler_params=pltpu.CompilerParams(vmem_limit_bytes=VMEM_LIMIT),
        name="mlp",
    )(*inputs, *grads, gate, fc1, bias, fc2)


def mlp_out_kernel(activated, fc2, after, out):
    count, chunk, hid = activated.shape[1:]
    rows = activated[0].reshape(count * chunk, hid)
    out[0] = matmul(rows, fc2[...]).astype(BF).reshape(count, chunk, out.shape[3])


def mlp_out_terms(activated, fc2, after):
    per, count, tok, hid = activated.shape
    width = fc2.shape[1]
    chunk = max(16, 256 // count)
    return pl.pallas_call(
        mlp_out_kernel,
        grid=(per, tok // chunk),
        in_specs=[
            pl.BlockSpec((1, count, chunk, hid), lambda i, c: (i, 0, c, 0)),
            pl.BlockSpec((hid, width), lambda i, c: (0, 0)),
            pl.BlockSpec(memory_space=pl.ANY),
        ],
        out_specs=pl.BlockSpec((1, count, chunk, width), lambda i, c: (i, 0, c, 0)),
        out_shape=jax.ShapeDtypeStruct((per, count, tok, width), BF),
        compiler_params=pltpu.CompilerParams(vmem_limit_bytes=VMEM_LIMIT),
        name="mlp_out_terms",
    )(activated, fc2, after)


def resid_grad_kernel(count, *refs):
    d_norm, resid_mid, attn_out, cotangent, scale, gate, proj, after = refs[:8]
    d_resid, d_attn, d_shift, d_scale, d_gate = refs[8:13]
    d_attended = refs[13:]
    normed, inv_std = ln_parts(resid_mid[0])
    grad = d_norm[0]
    total = cotangent[0].astype(F32) + ln_backward(grad * (1.0 + scale[0]), normed, inv_std)
    d_resid[0] = total
    d_a = (gate[0] * total).astype(BF)
    d_attn[0] = d_a
    back = matmul_nt(d_a, proj[...]).astype(BF)
    cols = back.shape[1] // count
    for j in range(count):
        d_attended[j][0] = back[:, j * cols : (j + 1) * cols]

    @pl.when(pl.program_id(1) == 0)
    def _():
        d_shift[...] = jnp.zeros_like(d_shift)
        d_scale[...] = jnp.zeros_like(d_scale)
        d_gate[...] = jnp.zeros_like(d_gate)

    d_shift[0] += jnp.sum(grad, axis=0, keepdims=True)
    d_scale[0] += jnp.sum(grad * normed, axis=0, keepdims=True)
    d_gate[0] += jnp.sum(total * attn_out[0], axis=0, keepdims=True)


def resid_grad(d_norm, resid_mid, attn_out, cotangent, group, scale, gate, proj, after, count):
    per, tok, width = d_norm.shape
    chunk = min(tok, 128)
    block = pl.BlockSpec((1, chunk, width), lambda i, c: (i, c, 0))
    row = pl.BlockSpec((1, 1, width), lambda i, c: (i, 0, 0))
    part = pl.BlockSpec((1, chunk, width // count), lambda i, c: (i, c, 0))
    row_shape = jax.ShapeDtypeStruct((per, 1, width), F32)
    return pl.pallas_call(
        partial(resid_grad_kernel, count),
        grid=(per, tok // chunk),
        in_specs=[
            block,
            block,
            block,
            pl.BlockSpec((1, chunk, width), lambda i, c: (group * per + i, c, 0)),
            row,
            row,
            pl.BlockSpec((width, width), lambda i, c: (0, 0)),
            pl.BlockSpec(memory_space=pl.ANY),
        ],
        out_specs=[block, block, row, row, row] + [part] * count,
        out_shape=[
            jax.ShapeDtypeStruct((per, tok, width), F32),
            jax.ShapeDtypeStruct((per, tok, width), BF),
            row_shape,
            row_shape,
            row_shape,
        ]
        + [jax.ShapeDtypeStruct((per, tok, width // count), BF)] * count,
        compiler_params=pltpu.CompilerParams(vmem_limit_bytes=VMEM_LIMIT),
        name="resid_grad",
    )(d_norm, resid_mid, attn_out, cotangent, scale, gate, proj, after)


def pack_kernel(first, second, after, out):
    rows = first.shape[1]
    out[0, :rows] = first[0]
    out[0, rows:] = second[0]


def pack(first, second, after):
    count, rows, width = first.shape
    more = second.shape[1]
    return pl.pallas_call(
        pack_kernel,
        grid=(count,),
        in_specs=[
            pl.BlockSpec((1, rows, width), lambda i: (i, 0, 0)),
            pl.BlockSpec((1, more, width), lambda i: (i, 0, 0)),
            pl.BlockSpec(memory_space=pl.ANY),
        ],
        out_specs=pl.BlockSpec((1, rows + more, width), lambda i: (i, 0, 0)),
        out_shape=jax.ShapeDtypeStruct((count, rows + more, width), first.dtype),
        compiler_params=pltpu.CompilerParams(vmem_limit_bytes=VMEM_LIMIT),
        name="pack",
    )(first, second, after)


def pack_last_kernel(proj_terms, qkv_terms, after, out):
    half = proj_terms.shape[2] // 2
    folded = jnp.concatenate([proj_terms[0, :, :half], proj_terms[0, :, half:]], axis=0)
    out[0] = jnp.concatenate([folded, qkv_terms[0].astype(F32)], axis=1).astype(BF)


def pack_last(proj_terms, qkv_terms, after):
    count, half, width = proj_terms.shape
    _, rows, cols = qkv_terms.shape
    return pl.pallas_call(
        pack_last_kernel,
        grid=(count,),
        in_specs=[
            pl.BlockSpec((1, half, width), lambda i: (i, 0, 0)),
            pl.BlockSpec((1, rows, cols), lambda i: (i, 0, 0)),
            pl.BlockSpec(memory_space=pl.ANY),
        ],
        out_specs=pl.BlockSpec((1, rows, width // 2 + cols), lambda i: (i, 0, 0)),
        out_shape=jax.ShapeDtypeStruct((count, rows, width // 2 + cols), BF),
        compiler_params=pltpu.CompilerParams(vmem_limit_bytes=VMEM_LIMIT),
        name="pack_last",
    )(proj_terms, qkv_terms, after)


def unpack_kernel(joined, after, *parts):
    start = 0
    for part in parts:
        part[0] = joined[0, start : start + part.shape[1]]
        start += part.shape[1]


def unpack(joined, after, row_counts):
    count, rows, width = joined.shape
    return pl.pallas_call(
        unpack_kernel,
        grid=(count,),
        in_specs=[
            pl.BlockSpec((1, rows, width), lambda i: (i, 0, 0)),
            pl.BlockSpec(memory_space=pl.ANY),
        ],
        out_specs=[pl.BlockSpec((1, n, width), lambda i: (i, 0, 0)) for n in row_counts],
        out_shape=[jax.ShapeDtypeStruct((count, n, width), joined.dtype) for n in row_counts],
        compiler_params=pltpu.CompilerParams(vmem_limit_bytes=VMEM_LIMIT),
        name="unpack",
    )(joined, after)


def on_device(tokens, conditioning, w_mod, b_mod, w_qkv, w_proj, w_fc1, b_fc1, w_fc2, cotangent):
    lat, tok, width = tokens.shape
    seq_n = lax.axis_size("seq")
    dp_n = lax.axis_size("dp")
    seq = lax.axis_index("seq")
    dp = lax.axis_index("dp")
    core = seq % 2
    heads_here = HEADS // seq_n
    cols = heads_here * HEAD_DIM
    seq_len = tok * seq_n
    rows = w_qkv.shape[0]
    hid_here = w_fc2.shape[0] // seq_n
    hid = hid_here * dp_n
    groups = 2
    per = lat // groups
    own = per * tok

    cond_silu, silu_back = jax.vjp(jax.nn.silu, conditioning)
    cond_act = cond_silu.astype(BF)
    bias_here = lax.dynamic_slice(b_fc1, (seq * hid_here,), (hid_here,))
    small = jnp.concatenate([cond_act.reshape(lat * width), bias_here])
    small = dp_exchange(jnp.broadcast_to(small[None], (dp_n, lat * width + hid_here)))
    cond_all = small[:, : lat * width].reshape(dp_n * lat, width)
    fc1_bias = small[:, lat * width :].reshape(hid).astype(F32)
    cond_rows = lax.dynamic_slice(cond_all, (0, dp * rows), (dp_n * lat, rows))
    mod_terms = matmul(cond_rows, w_mod)
    piece = b_mod.shape[0]
    mod_terms = lax.dynamic_update_slice(
        mod_terms,
        lax.dynamic_slice(mod_terms, (0, dp * piece), (dp_n * lat, piece))
        + b_mod.astype(F32)[None],
        (0, dp * piece),
    )
    modulation = jnp.sum(dp_exchange(mod_terms.reshape(dp_n, lat, 6 * width)), axis=0)

    tok_slots = seq_gather(tokens)
    cot_slots = seq_gather(cotangent)

    qkv_here = jnp.concatenate(
        [lax.dynamic_slice(w_qkv, (0, t * width + seq * cols), (rows, cols)) for t in range(3)],
        axis=1,
    )
    qkv = dp_gather(qkv_here, lambda d: d).reshape(width, 3 * cols)
    half = rows // 2
    fc1_here = jnp.concatenate(
        [
            lax.dynamic_slice(w_fc1, (0, (d * seq_n + seq) * hid_here), (rows, hid_here))
            for d in range(dp_n)
        ],
        axis=1,
    )
    fc2_here = lax.dynamic_slice(w_fc2, (seq * hid_here, 0), (hid_here, width))
    proj_here = lax.dynamic_slice(w_proj, (core * half, 0), (half, width))
    together = hid == width
    proj_mine = lax.all_gather(proj_here, "dp", axis=0)
    if together:
        joined = lax.all_gather(pack(fc1_here[None], fc2_here[None], proj_mine)[0], "dp", axis=0)
    else:
        fc1 = lax.all_gather(fc1_here, "dp", axis=0, tiled=True)
        fc2 = lax.all_gather(fc2_here, "dp", axis=0, tiled=True)

    def part(g):
        return slice(g * per, (g + 1) * per)

    shift_attn, scale_attn, gate_attn, shift_mlp, scale_mlp, gate_mlp = [
        [modulation[part(g), None, i * width : (i + 1) * width] for g in range(groups)]
        for i in range(6)
    ]
    token_values = [tokens[part(g)].astype(F32) for g in range(groups)]
    normed_all, packed, mixed, log_sums, attended = [], [], [], [], []
    for g in range(groups):
        normed, rows_packed = qkv_forward(tok_slots, g, per, shift_attn[g], scale_attn[g], qkv)
        normed_all.append(normed.reshape(per * seq_len, width))
        packed.append(rows_packed.reshape(per, seq_len, 3 * cols))
        out, log_sum = attention(
            packed[g], mixed + cot_slots[-1:] if g else [], heads_here
        )
        mixed.append(out)
        log_sums.append(log_sum)
        out = out.reshape(per, seq_n, tok, cols)
        attended.append(
            jnp.concatenate(seq_exchange([out[:, j] for j in range(seq_n)]), axis=2).reshape(
                own, width
            )
        )

    proj_other = hop(proj_mine, "seq", 1)
    proj = jnp.where(
        core == 0,
        jnp.stack([proj_mine, proj_other], axis=1),
        jnp.stack([proj_other, proj_mine], axis=1),
    ).reshape(seq_n, cols, width)

    def by_place(blocks):
        return jnp.concatenate(
            [lax.dynamic_index_in_dim(blocks, seq ^ j, 0, keepdims=False) for j in range(seq_n)]
        )

    proj = by_place(proj)

    attn_out, resid_mid, normed_mlp, upstream = [], [], [], []
    for g in range(groups):
        attn_out.append(matmul(attended[g], proj).reshape(per, tok, width))
        resid_mid.append(token_values[g] + gate_attn[g] * attn_out[g])
        normed_mlp.append(
            (ln_parts(resid_mid[g])[0] * (1.0 + scale_mlp[g]) + shift_mlp[g]).astype(BF)
        )
        upstream.append(cotangent[part(g)].astype(F32))
    if together:
        fc1, fc2 = unpack(joined, normed_mlp[0], [rows, hid_here])
        fc1, fc2 = fc1.reshape(width, hid), fc2.reshape(hid, width)

    grad_fc1 = grad_fc2 = grad_bias1 = 0.0
    d_norm, activated = [], []
    for g in range(groups):
        x_all, d_mlp, active, d_hidden, terms, d_bias = mlp(
            seq_gather(normed_mlp[g]), cot_slots, g, gate_mlp[g], fc1, fc1_bias[None], fc2
        )
        d_norm.append(seq_reduce([terms[:, j].astype(F32) for j in range(seq_n)]))
        activated.append(active)
        flat = per * seq_len
        grad_fc2 = grad_fc2 + matmul_tn(active.reshape(flat, hid), d_mlp.reshape(flat, width))
        grad_fc1 = grad_fc1 + matmul_tn(x_all.reshape(flat, width), d_hidden.reshape(flat, hid))
        grad_bias1 = grad_bias1 + d_bias[0]
    grad_fc1 = grad_fc1.astype(BF).reshape(dp_n, rows, hid)
    grad_fc2 = grad_fc2.astype(BF).reshape(dp_n, hid_here, width)
    if together:
        grad_fc = pack(grad_fc1, grad_fc2, grad_bias1)
        sum_fc = lax.psum_scatter(grad_fc, "dp", scatter_dimension=0)
        sum_fc1, sum_fc2 = sum_fc[:rows], sum_fc[rows:]
    else:
        grad_fc = grad_fc1
        sum_fc1 = lax.psum_scatter(grad_fc1, "dp", scatter_dimension=0)
        sum_fc = sum_fc2 = lax.psum_scatter(grad_fc2, "dp", scatter_dimension=0)

    def stacked(terms):
        return jnp.concatenate(terms)

    d_shift_mlp, d_scale_mlp, d_gate_attn, d_resid, d_attn, d_attended = ([] for _ in range(6))
    d_mixed = []
    for g in range(groups):
        outs = resid_grad(
            d_norm[g], resid_mid[g], attn_out[g], cotangent, g, scale_mlp[g], gate_attn[g], proj,
            grad_fc, seq_n,
        )
        d_resid.append(outs[0])
        d_attn.append(outs[1].reshape(own, width))
        d_shift_mlp.append(outs[2][:, 0])
        d_scale_mlp.append(outs[3][:, 0])
        d_gate_attn.append(outs[4][:, 0])
        d_attended.append(outs[5])
        d_mixed.append(jnp.concatenate(seq_exchange(outs[5:]), axis=1))
    mlp_out, mlp_terms = [], []
    for g in range(groups):
        terms = mlp_out_terms(activated[g], fc2, d_attended[-1])
        mlp_terms.append(terms)
        mlp_out.append(seq_reduce([terms[:, j].astype(F32) for j in range(seq_n)]))
    output = jnp.concatenate(
        [(resid_mid[g] + gate_mlp[g] * mlp_out[g]).astype(BF) for g in range(groups)]
    )
    d_gate_mlp = stacked([jnp.sum(upstream[g] * mlp_out[g], axis=1) for g in range(groups)])
    grad_proj = by_place(
        matmul_tn(stacked(attended), stacked(d_attn)).astype(BF).reshape(seq_n, cols, width)
    ).reshape(dp_n, 2, half, width)
    proj_sent = hop(
        lax.dynamic_index_in_dim(grad_proj, 1 - core, axis=1, keepdims=False), "seq", 1
    )
    proj_terms = lax.dynamic_index_in_dim(grad_proj, core, axis=1, keepdims=False).astype(F32)
    proj_terms = proj_terms + proj_sent.astype(F32)

    d_packed, d_first, first_terms = [], [], []
    for g in range(groups):
        grads, terms = attention_grad(
            packed[g], mixed[g], log_sums[g], d_mixed[g], qkv,
            first_terms if g else [d_attended[-1]] + mlp_terms, heads_here,
        )
        d_packed.append(grads.reshape(per * seq_len, 3 * cols))
        first_terms.append(terms)
        terms = terms.reshape(per, seq_n, tok, width)
        d_first.append(seq_reduce([terms[:, j].astype(F32) for j in range(seq_n)]))
    grad_qkv = matmul_tn(stacked(normed_all), stacked(d_packed)).astype(BF)
    sum_last = lax.psum_scatter(
        pack_last(proj_terms, grad_qkv.reshape(dp_n, rows, 3 * cols), sum_fc),
        "dp",
        scatter_dimension=0,
    )
    sum_proj, sum_qkv = sum_last[:, : width // 2], sum_last[:, width // 2 :]
    d_shift_attn, d_scale_attn, grad_tokens = [], [], []
    for g in range(groups):
        normed_tok, std_tok = ln_parts(token_values[g])
        d_shift_attn.append(jnp.sum(d_first[g], axis=1))
        d_scale_attn.append(jnp.sum(d_first[g] * normed_tok, axis=1))
        grad_tokens.append(
            d_resid[g] + ln_backward(d_first[g] * (1.0 + scale_attn[g]), normed_tok, std_tok)
        )

    mod_part = jnp.concatenate(
        [stacked(d_shift_attn), stacked(d_scale_attn), stacked(d_gate_attn)]
        + [stacked(d_shift_mlp), stacked(d_scale_mlp), d_gate_mlp],
        axis=1,
    )
    bit = 1
    while bit < seq_n:
        mod_part = mod_part + hop(mod_part, "seq", bit)
        bit *= 2
    d_mod = dp_exchange(jnp.broadcast_to(mod_part.astype(BF)[None], (dp_n, lat, 6 * width)))
    d_mod = d_mod.reshape(dp_n * lat, 6 * width)
    share = 6 * width // (dp_n * seq_n)
    mod_cols = lax.dynamic_slice(d_mod, (0, (dp * seq_n + seq) * share), (dp_n * lat, share))
    grad_wmod = matmul_tn(cond_all, mod_cols)
    grad_bmod = jnp.sum(mod_cols.astype(F32), axis=0)
    back = jnp.concatenate(
        [
            matmul_nt(d_mod, w_mod).reshape(dp_n, lat * rows),
            grad_bias1.reshape(dp_n, hid_here),
        ],
        axis=1,
    )
    back = dp_exchange(back)
    d_cond = back[:, : lat * rows].reshape(dp_n, lat, rows)
    (grad_cond,) = silu_back(d_cond.transpose(1, 0, 2).reshape(lat, width))
    bias_out = jnp.sum(back[:, lat * rows :], axis=0)

    def to_owner(blocks):
        return lax.all_to_all(blocks, "seq", 0, 0, tiled=True).astype(F32)

    share = width // seq_n
    fc2_blocks = sum_fc2.reshape(hid_here, seq_n, share).transpose(1, 0, 2)
    fc1_blocks = sum_fc1.reshape(rows, seq_n, hid // seq_n).transpose(1, 0, 2)
    if together:
        received = to_owner(jnp.concatenate([fc1_blocks, fc2_blocks], axis=1))
        out_fc1, out_fc2 = received[:, :rows], received[:, rows:]
    else:
        out_fc1, out_fc2 = to_owner(fc1_blocks), to_owner(fc2_blocks)
    out_fc2 = out_fc2.reshape(seq_n * hid_here, share)
    out_fc1 = out_fc1.reshape(seq_n, rows, dp_n // seq_n, hid_here).transpose(1, 2, 0, 3)
    out_fc1 = out_fc1.reshape(rows, hid)
    proj_blocks = sum_proj.reshape(2, half, seq_n // 2, share).transpose(0, 2, 1, 3)
    proj_blocks = proj_blocks.reshape(seq_n, half, share)
    qkv_thirds = sum_qkv.reshape(rows, 3, cols).transpose(1, 0, 2)
    qkv_blocks = jnp.stack(
        [
            lax.dynamic_index_in_dim(
                qkv_thirds, jnp.minimum((3 * to - seq + seq_n - 1) // seq_n, 2), 0, keepdims=False
            )
            for to in range(seq_n)
        ]
    )
    received = to_owner(jnp.concatenate([proj_blocks, qkv_blocks], axis=1))
    out_proj = jnp.sum(received[:, :half].reshape(seq_n // 2, 2, half, share), axis=0)
    out_proj = out_proj.reshape(rows, share)
    out_qkv = jnp.concatenate(
        [
            lax.dynamic_index_in_dim(received, (3 * seq + i) % seq_n, 0, keepdims=False)[half:]
            for i in range(3)
        ],
        axis=1,
    )
    return (
        output,
        stacked(grad_tokens),
        grad_cond,
        grad_wmod,
        grad_bmod,
        out_qkv,
        out_proj,
        out_fc1,
        bias_out,
        out_fc2,
    )


def solution(mesh):
    placed = (
        P("dp", "seq", None),
        P("dp", None),
        P("dp", None),
        P("dp"),
        P("dp", None),
        P("dp", None),
        P("dp", None),
        P("dp"),
        P("dp", None),
        P("dp", "seq", None),
    )
    return jax.shard_map(
        on_device,
        mesh=mesh,
        in_specs=placed,
        out_specs=(
            P("dp", "seq", None),
            P("dp", "seq", None),
            P("dp", None),
            P(None, ("dp", "seq")),
            P(("dp", "seq")),
            P("dp", "seq"),
            P("dp", "seq"),
            P("dp", "seq"),
            P(("dp", "seq")),
            P("dp", "seq"),
        ),
        check_vma=False,
    )
```

```python
import math
from functools import partial

import jax
import jax.numpy as jnp
from jax import lax
from jax.experimental import pallas as pl
from jax.experimental.pallas import tpu as pltpu
from jax.sharding import PartitionSpec as P

HEADS = 16
HEAD_DIM = 72
BF = jnp.bfloat16
F32 = jnp.float32
GELU_C = 0.7978845608028654
GELU_A = 0.044715
VMEM_LIMIT = 60 * 2**20
EXP2_SCALE = HEAD_DIM ** (-0.5) * math.log2(math.e)


def hop(value, axis, bits):
    count = lax.axis_size(axis)
    return lax.ppermute(value, axis, [(i, i ^ bits) for i in range(count)])


def matmul(left, right):
    return jnp.dot(left, right, preferred_element_type=F32)


def matmul_nt(left, right):
    return lax.dot_general(left, right, (((1,), (1,)), ((), ())), preferred_element_type=F32)


def matmul_tn(left, right):
    return lax.dot_general(left, right, (((0,), (0,)), ((), ())), preferred_element_type=F32)


def ln_parts(values):
    row_mean = jnp.mean(values, axis=-1, keepdims=True)
    centred = values - row_mean
    row_var = jnp.mean(centred * centred, axis=-1, keepdims=True)
    inv_std = lax.rsqrt(row_var + 1e-06)
    return centred * inv_std, inv_std


def ln_backward(grad, normed, inv_std):
    mean_grad = jnp.mean(grad, axis=-1, keepdims=True)
    mean_inner = jnp.mean(grad * normed, axis=-1, keepdims=True)
    return (grad - mean_grad - normed * mean_inner) * inv_std


def seq_gather(mine):
    slots = {0: mine}
    bit = lax.axis_size("seq") // 2
    while bit:
        for j in list(slots):
            slots[j | bit] = hop(slots[j], "seq", bit)
        bit //= 2
    return [slots[j] for j in range(len(slots))]


def seq_step(slots, bit):
    kept = {j: v for j, v in slots.items() if not j & bit}
    for j in slots:
        if j & bit:
            kept[j ^ bit] = kept[j ^ bit] + hop(slots[j].astype(BF), "seq", bit).astype(F32)
    return kept


def seq_near(slots):
    slots = dict(enumerate(slots))
    bit = 1
    while len(slots) > 2:
        slots = seq_step(slots, bit)
        bit *= 2
    return slots[0], slots[bit].astype(BF)


def seq_far(kept, sent):
    return kept + hop(sent, "seq", lax.axis_size("seq") // 2).astype(F32)


def seq_reduce(slots):
    return seq_far(*seq_near(slots))


def seq_exchange(blocks):
    return [blocks[0]] + [hop(blocks[j], "seq", j) for j in range(1, len(blocks))]


def dp_exchange(value):
    return lax.all_to_all(value, "dp", 0, 0, tiled=True)


def dp_gather(mine, place):
    count = lax.axis_size("dp")
    index = lax.axis_index("dp")
    slots = {0: mine}
    for j in range(2, count, 2):
        slots[j] = hop(mine, "dp", j)
    for j in range(0, count, 2):
        slots[j + 1] = hop(slots[j], "dp", 1)
    whole = jnp.zeros((count,) + mine.shape, mine.dtype)
    for j in range(count):
        whole = lax.dynamic_update_index_in_dim(whole, slots[j], place(index ^ j), 0)
    return whole


def dp_scatter(terms, place):
    count = lax.axis_size("dp")
    index = lax.axis_index("dp")

    def block(j):
        return lax.dynamic_index_in_dim(terms, place(index ^ j), 0, keepdims=False)

    half = {}
    for j in list(range(2, count, 2)) + [0]:
        half[j] = block(j).astype(F32) + hop(block(j + 1), "dp", 1).astype(F32)
    total = half[0]
    for j in range(2, count, 2):
        total = total + hop(half[j].astype(BF), "dp", j).astype(F32)
    return total


def attend_kernel(heads, block, packed, *refs):
    mixed, log_sum, mixed_t = refs[-3:]
    seq_len = packed.shape[1]
    cols = heads * HEAD_DIM
    for h in range(heads):
        at = h * HEAD_DIM
        keys = packed[0, :, cols + at : cols + at + HEAD_DIM]
        values_t = packed[0, :, 2 * cols + at : 2 * cols + at + HEAD_DIM].astype(F32).T.astype(BF)
        for start in range(0, seq_len, block):
            queries = packed[0, start : start + block, at : at + HEAD_DIM]
            scores = matmul_nt(keys, queries)
            top = jnp.max(scores, axis=0, keepdims=True)
            exponent = jnp.exp2((scores - top) * EXP2_SCALE)
            total = jnp.sum(exponent, axis=0, keepdims=True)
            part = matmul(values_t, exponent.astype(BF)) / total
            mixed_t[at : at + HEAD_DIM, start : start + block] = part
            log_sum[0, h : h + 1, start : start + block] = top * EXP2_SCALE + jnp.log2(total)
    mixed[0] = mixed_t[...].T.astype(BF)


def attend_grad_kernel(heads, block, packed, mixed, log_sum, d_mixed, qkv, *refs):
    d_packed, terms, d_queries_t = refs[-3:]
    seq_len = packed.shape[1]
    cols = heads * HEAD_DIM
    inv_root = HEAD_DIM ** (-0.5)
    for h in range(heads):
        at = h * HEAD_DIM
        keys = packed[0, :, cols + at : cols + at + HEAD_DIM]
        values = packed[0, :, 2 * cols + at : 2 * cols + at + HEAD_DIM]
        keys_t = keys.astype(F32).T.astype(BF)
        d_keys = d_values = None
        for start in range(0, seq_len, block):
            queries = packed[0, start : start + block, at : at + HEAD_DIM]
            grads = d_mixed[0, start : start + block, at : at + HEAD_DIM]
            outs = mixed[0, start : start + block, at : at + HEAD_DIM]
            inner = jnp.sum(grads.astype(F32) * outs.astype(F32), axis=1, keepdims=True)
            inner = jnp.broadcast_to(inner, (block, 128)).T[0:1]
            scores = matmul_nt(keys, queries)
            probs = jnp.exp2(scores * EXP2_SCALE - log_sum[0, h : h + 1, start : start + block])
            d_probs = matmul_nt(values, grads)
            d_scores = (probs * (d_probs - inner)).astype(BF)
            d_v = matmul(probs.astype(BF), grads)
            d_k = matmul(d_scores, queries)
            d_values = d_v if d_values is None else d_values + d_v
            d_keys = d_k if d_keys is None else d_keys + d_k
            d_queries_t[at : at + HEAD_DIM, start : start + block] = matmul(keys_t, d_scores) * inv_root
        d_packed[0, :, cols + at : cols + at + HEAD_DIM] = (d_keys * inv_root).astype(BF)
        d_packed[0, :, 2 * cols + at : 2 * cols + at + HEAD_DIM] = d_values.astype(BF)
    d_packed[0, :, 0:cols] = d_queries_t[...].T.astype(BF)
    for start in range(0, seq_len, block):
        rows = d_packed[0, start : start + block]
        terms[0, start : start + block] = matmul_nt(rows, qkv[...]).astype(BF)


def row_spec(*shape):
    return pl.BlockSpec((1,) + shape, lambda i: (i, 0, 0))


def attention(packed, after, heads, block=1024):
    lat, seq_len, _ = packed.shape
    cols = heads * HEAD_DIM
    return pl.pallas_call(
        partial(attend_kernel, heads, block),
        grid=(lat,),
        in_specs=[row_spec(seq_len, 3 * cols)] + [pl.BlockSpec(memory_space=pl.ANY)] * len(after),
        out_specs=[row_spec(seq_len, cols), row_spec(heads, seq_len)],
        out_shape=[
            jax.ShapeDtypeStruct((lat, seq_len, cols), BF),
            jax.ShapeDtypeStruct((lat, heads, seq_len), F32),
        ],
        scratch_shapes=[pltpu.VMEM((cols, seq_len), F32)],
        compiler_params=pltpu.CompilerParams(vmem_limit_bytes=VMEM_LIMIT),
        name="attend",
    )(packed, *after)


def attention_grad(packed, mixed, log_sum, d_mixed, qkv, after, heads, block=512):
    lat, seq_len, _ = packed.shape
    cols = heads * HEAD_DIM
    return pl.pallas_call(
        partial(attend_grad_kernel, heads, block),
        grid=(lat,),
        in_specs=[
            row_spec(seq_len, 3 * cols),
            row_spec(seq_len, cols),
            row_spec(heads, seq_len),
            row_spec(seq_len, cols),
            pl.BlockSpec(qkv.shape, lambda i: (0, 0)),
        ]
        + [pl.BlockSpec(memory_space=pl.ANY)] * len(after),
        out_specs=[row_spec(seq_len, 3 * cols), row_spec(seq_len, qkv.shape[0])],
        out_shape=[
            jax.ShapeDtypeStruct((lat, seq_len, 3 * cols), BF),
            jax.ShapeDtypeStruct((lat, seq_len, qkv.shape[0]), BF),
        ],
        scratch_shapes=[pltpu.VMEM((cols, seq_len), F32)],
        compiler_params=pltpu.CompilerParams(vmem_limit_bytes=VMEM_LIMIT),
        name="attend_grad",
    )(packed, mixed, log_sum, d_mixed, qkv, *after)


def qkv_kernel(count, *refs):
    slots, (shift, scale, qkv, normed, packed) = refs[:count], refs[count:]
    chunk, width = slots[0].shape[1:]
    for j in range(count):
        value = ln_parts(slots[j][0].astype(F32))[0] * (1.0 + scale[0]) + shift[0]
        normed[0, j] = value.astype(BF)
    rows = normed[0].reshape(count * chunk, width)
    packed[0] = matmul(rows, qkv[...]).astype(BF).reshape(count, chunk, packed.shape[3])


def qkv_forward(slots, group, per, shift, scale, qkv):
    count = len(slots)
    _, tok, width = slots[0].shape
    chunk = max(16, 256 // count)
    row = pl.BlockSpec((1, 1, width), lambda i, c: (i, 0, 0))
    cols = qkv.shape[1]
    return pl.pallas_call(
        partial(qkv_kernel, count),
        grid=(per, tok // chunk),
        in_specs=[pl.BlockSpec((1, chunk, width), lambda i, c: (group * per + i, c, 0))] * count
        + [row, row, pl.BlockSpec((width, cols), lambda i, c: (0, 0))],
        out_specs=[
            pl.BlockSpec((1, count, chunk, width), lambda i, c: (i, 0, c, 0)),
            pl.BlockSpec((1, count, chunk, cols), lambda i, c: (i, 0, c, 0)),
        ],
        out_shape=[
            jax.ShapeDtypeStruct((per, count, tok, width), BF),
            jax.ShapeDtypeStruct((per, count, tok, cols), BF),
        ],
        compiler_params=pltpu.CompilerParams(vmem_limit_bytes=VMEM_LIMIT),
        name="qkv_forward",
    )(*slots, shift, scale, qkv)


def mlp_kernel(count, *refs):
    inputs, grads = refs[:count], refs[count : 2 * count]
    gate, fc1, bias, fc2, x_all, g_all, activated, d_hidden, d_norm, d_bias = refs[2 * count :]
    chunk, width = inputs[0].shape[1:]
    hid = fc1.shape[1]
    for j in range(count):
        x_all[0, j] = inputs[j][0]
        g_all[0, j] = (gate[0] * grads[j][0].astype(F32)).astype(BF)
    x = x_all[0].reshape(count * chunk, width)
    g = g_all[0].reshape(count * chunk, width)
    hidden = matmul(x, fc1[...]) + bias[...]
    square = hidden * hidden
    tanh = jnp.tanh(GELU_C * (hidden + GELU_A * hidden * square))
    half = 0.5 * (1.0 + tanh)
    activated[0] = (hidden * half).astype(BF).reshape(count, chunk, hid)
    slope = half + (0.5 * GELU_C) * hidden * (1.0 - tanh * tanh) * (1.0 + 3.0 * GELU_A * square)
    d_h = (matmul_nt(g, fc2[...]) * slope).astype(BF)
    d_hidden[0] = d_h.reshape(count, chunk, hid)
    d_norm[0] = matmul_nt(d_h, fc1[...]).astype(BF).reshape(count, chunk, width)

    @pl.when((pl.program_id(0) == 0) & (pl.program_id(1) == 0))
    def _():
        d_bias[...] = jnp.zeros_like(d_bias)

    d_bias[...] += jnp.sum(d_h.astype(F32), axis=0, keepdims=True)


def mlp(inputs, grads, group, gate, fc1, bias, fc2):
    count = len(inputs)
    per, tok, width = inputs[0].shape
    hid = fc1.shape[1]
    chunk = max(16, 256 // count)
    slot = pl.BlockSpec((1, chunk, width), lambda i, c: (i, c, 0))
    late = pl.BlockSpec((1, chunk, width), lambda i, c: (group * per + i, c, 0))

    def whole(rows, cols):
        return pl.BlockSpec((rows, cols), lambda i, c: (0, 0))

    wide = pl.BlockSpec((1, count, chunk, width), lambda i, c: (i, 0, c, 0))
    inner = pl.BlockSpec((1, count, chunk, hid), lambda i, c: (i, 0, c, 0))
    shape_wide = jax.ShapeDtypeStruct((per, count, tok, width), BF)
    shape_inner = jax.ShapeDtypeStruct((per, count, tok, hid), BF)
    return pl.pallas_call(
        partial(mlp_kernel, count),
        grid=(per, tok // chunk),
        in_specs=[slot] * count
        + [late] * count
        + [pl.BlockSpec((1, 1, width), lambda i, c: (i, 0, 0))]
        + [whole(width, hid), whole(1, hid), whole(hid, width)],
        out_specs=[wide, wide, inner, inner, wide, whole(1, hid)],
        out_shape=[shape_wide, shape_wide, shape_inner, shape_inner, shape_wide]
        + [jax.ShapeDtypeStruct((1, hid), F32)],
        compiler_params=pltpu.CompilerParams(vmem_limit_bytes=VMEM_LIMIT),
        name="mlp",
    )(*inputs, *grads, gate, fc1, bias, fc2)


def mlp_out_kernel(activated, fc2, after, out):
    count, chunk, hid = activated.shape[1:]
    rows = activated[0].reshape(count * chunk, hid)
    out[0] = matmul(rows, fc2[...]).astype(BF).reshape(count, chunk, out.shape[3])


def mlp_out_terms(activated, fc2, after):
    per, count, tok, hid = activated.shape
    width = fc2.shape[1]
    chunk = max(16, 256 // count)
    return pl.pallas_call(
        mlp_out_kernel,
        grid=(per, tok // chunk),
        in_specs=[
            pl.BlockSpec((1, count, chunk, hid), lambda i, c: (i, 0, c, 0)),
            pl.BlockSpec((hid, width), lambda i, c: (0, 0)),
            pl.BlockSpec(memory_space=pl.ANY),
        ],
        out_specs=pl.BlockSpec((1, count, chunk, width), lambda i, c: (i, 0, c, 0)),
        out_shape=jax.ShapeDtypeStruct((per, count, tok, width), BF),
        compiler_params=pltpu.CompilerParams(vmem_limit_bytes=VMEM_LIMIT),
        name="mlp_out_terms",
    )(activated, fc2, after)


def resid_grad_kernel(count, *refs):
    d_norm, resid_mid, attn_out, cotangent, scale, gate, proj, after = refs[:8]
    d_resid, d_attn, d_shift, d_scale, d_gate = refs[8:13]
    d_attended = refs[13:]
    normed, inv_std = ln_parts(resid_mid[0])
    grad = d_norm[0]
    total = cotangent[0].astype(F32) + ln_backward(grad * (1.0 + scale[0]), normed, inv_std)
    d_resid[0] = total
    d_a = (gate[0] * total).astype(BF)
    d_attn[0] = d_a
    back = matmul_nt(d_a, proj[...]).astype(BF)
    cols = back.shape[1] // count
    for j in range(count):
        d_attended[j][0] = back[:, j * cols : (j + 1) * cols]

    @pl.when(pl.program_id(1) == 0)
    def _():
        d_shift[...] = jnp.zeros_like(d_shift)
        d_scale[...] = jnp.zeros_like(d_scale)
        d_gate[...] = jnp.zeros_like(d_gate)

    d_shift[0] += jnp.sum(grad, axis=0, keepdims=True)
    d_scale[0] += jnp.sum(grad * normed, axis=0, keepdims=True)
    d_gate[0] += jnp.sum(total * attn_out[0], axis=0, keepdims=True)


def resid_grad(d_norm, resid_mid, attn_out, cotangent, group, scale, gate, proj, after, count):
    per, tok, width = d_norm.shape
    chunk = min(tok, 128)
    block = pl.BlockSpec((1, chunk, width), lambda i, c: (i, c, 0))
    row = pl.BlockSpec((1, 1, width), lambda i, c: (i, 0, 0))
    part = pl.BlockSpec((1, chunk, width // count), lambda i, c: (i, c, 0))
    row_shape = jax.ShapeDtypeStruct((per, 1, width), F32)
    return pl.pallas_call(
        partial(resid_grad_kernel, count),
        grid=(per, tok // chunk),
        in_specs=[
            block,
            block,
            block,
            pl.BlockSpec((1, chunk, width), lambda i, c: (group * per + i, c, 0)),
            row,
            row,
            pl.BlockSpec((width, width), lambda i, c: (0, 0)),
            pl.BlockSpec(memory_space=pl.ANY),
        ],
        out_specs=[block, block, row, row, row] + [part] * count,
        out_shape=[
            jax.ShapeDtypeStruct((per, tok, width), F32),
            jax.ShapeDtypeStruct((per, tok, width), BF),
            row_shape,
            row_shape,
            row_shape,
        ]
        + [jax.ShapeDtypeStruct((per, tok, width // count), BF)] * count,
        compiler_params=pltpu.CompilerParams(vmem_limit_bytes=VMEM_LIMIT),
        name="resid_grad",
    )(d_norm, resid_mid, attn_out, cotangent, scale, gate, proj, after)


def pack_kernel(first, second, after, out):
    rows = first.shape[1]
    out[0, :rows] = first[0]
    out[0, rows:] = second[0]


def pack(first, second, after):
    count, rows, width = first.shape
    more = second.shape[1]
    return pl.pallas_call(
        pack_kernel,
        grid=(count,),
        in_specs=[
            pl.BlockSpec((1, rows, width), lambda i: (i, 0, 0)),
            pl.BlockSpec((1, more, width), lambda i: (i, 0, 0)),
            pl.BlockSpec(memory_space=pl.ANY),
        ],
        out_specs=pl.BlockSpec((1, rows + more, width), lambda i: (i, 0, 0)),
        out_shape=jax.ShapeDtypeStruct((count, rows + more, width), first.dtype),
        compiler_params=pltpu.CompilerParams(vmem_limit_bytes=VMEM_LIMIT),
        name="pack",
    )(first, second, after)


def pack_last_kernel(proj_terms, qkv_terms, after, out):
    half = proj_terms.shape[2] // 2
    folded = jnp.concatenate([proj_terms[0, :, :half], proj_terms[0, :, half:]], axis=0)
    out[0] = jnp.concatenate([folded, qkv_terms[0].astype(F32)], axis=1).astype(BF)


def pack_last(proj_terms, qkv_terms, after):
    count, half, width = proj_terms.shape
    _, rows, cols = qkv_terms.shape
    return pl.pallas_call(
        pack_last_kernel,
        grid=(count,),
        in_specs=[
            pl.BlockSpec((1, half, width), lambda i: (i, 0, 0)),
            pl.BlockSpec((1, rows, cols), lambda i: (i, 0, 0)),
            pl.BlockSpec(memory_space=pl.ANY),
        ],
        out_specs=pl.BlockSpec((1, rows, width // 2 + cols), lambda i: (i, 0, 0)),
        out_shape=jax.ShapeDtypeStruct((count, rows, width // 2 + cols), BF),
        compiler_params=pltpu.CompilerParams(vmem_limit_bytes=VMEM_LIMIT),
        name="pack_last",
    )(proj_terms, qkv_terms, after)


def unpack_kernel(joined, after, *parts):
    start = 0
    for part in parts:
        part[0] = joined[0, start : start + part.shape[1]]
        start += part.shape[1]


def unpack(joined, after, row_counts):
    count, rows, width = joined.shape
    return pl.pallas_call(
        unpack_kernel,
        grid=(count,),
        in_specs=[
            pl.BlockSpec((1, rows, width), lambda i: (i, 0, 0)),
            pl.BlockSpec(memory_space=pl.ANY),
        ],
        out_specs=[pl.BlockSpec((1, n, width), lambda i: (i, 0, 0)) for n in row_counts],
        out_shape=[jax.ShapeDtypeStruct((count, n, width), joined.dtype) for n in row_counts],
        compiler_params=pltpu.CompilerParams(vmem_limit_bytes=VMEM_LIMIT),
        name="unpack",
    )(joined, after)


def token_grad_kernel(per, d_first, e_first, d_resid, e_resid, tokens, scale, after, *outs):
    grad_tokens, d_shift, d_scale = outs
    early = pl.program_id(0) < per
    grad = jnp.where(early, d_first[0], e_first[0])
    normed, inv_std = ln_parts(tokens[0].astype(F32))
    grad_tokens[0] = jnp.where(early, d_resid[0], e_resid[0]) + ln_backward(
        grad * (1.0 + scale[0]), normed, inv_std
    )

    @pl.when(pl.program_id(1) == 0)
    def _():
        d_shift[...] = jnp.zeros_like(d_shift)
        d_scale[...] = jnp.zeros_like(d_scale)

    d_shift[0] += jnp.sum(grad, axis=0, keepdims=True)
    d_scale[0] += jnp.sum(grad * normed, axis=0, keepdims=True)


def token_grad(d_first, d_resid, tokens, scale, after):
    lat, tok, width = tokens.shape
    per = lat // 2
    chunk = min(tok, 128)
    early = pl.BlockSpec((1, chunk, width), lambda i, c: (jnp.minimum(i, per - 1), c, 0))
    late = pl.BlockSpec((1, chunk, width), lambda i, c: (jnp.maximum(i, per) - per, c, 0))
    block = pl.BlockSpec((1, chunk, width), lambda i, c: (i, c, 0))
    row = pl.BlockSpec((1, 1, width), lambda i, c: (i, 0, 0))
    row_shape = jax.ShapeDtypeStruct((lat, 1, width), F32)
    return pl.pallas_call(
        partial(token_grad_kernel, per),
        grid=(lat, tok // chunk),
        in_specs=[early, late, early, late, block, row, pl.BlockSpec(memory_space=pl.ANY)],
        out_specs=[block, row, row],
        out_shape=[jax.ShapeDtypeStruct((lat, tok, width), F32), row_shape, row_shape],
        compiler_params=pltpu.CompilerParams(vmem_limit_bytes=VMEM_LIMIT),
        name="token_grad",
    )(*d_first, *d_resid, tokens, scale, after)


def place_last_kernel(rows, owners, received, out_qkv, out_proj):
    cols = received.shape[2]
    half = rows // 2
    for i in range(3):
        out_qkv[:, i * cols : (i + 1) * cols] = received[owners[i], :rows].astype(F32)
    for core in range(2):
        total = received[core, rows:].astype(F32)
        for j in range(core + 2, received.shape[0], 2):
            total = total + received[j, rows:].astype(F32)
        out_proj[core * half : (core + 1) * half] = total


def place_last(received, rows, seq):
    count, _, cols = received.shape
    owners = (3 * seq + jnp.arange(3, dtype=jnp.int32)) % count
    vmem = pl.BlockSpec(memory_space=pltpu.VMEM)
    return pl.pallas_call(
        partial(place_last_kernel, rows),
        in_specs=[pl.BlockSpec(memory_space=pltpu.SMEM), vmem],
        out_specs=[vmem, vmem],
        out_shape=[
            jax.ShapeDtypeStruct((rows, 3 * cols), F32),
            jax.ShapeDtypeStruct((rows, cols), F32),
        ],
        compiler_params=pltpu.CompilerParams(vmem_limit_bytes=VMEM_LIMIT),
        name="place_last",
    )(owners, received)


def on_device(tokens, conditioning, w_mod, b_mod, w_qkv, w_proj, w_fc1, b_fc1, w_fc2, cotangent):
    lat, tok, width = tokens.shape
    seq_n = lax.axis_size("seq")
    dp_n = lax.axis_size("dp")
    seq = lax.axis_index("seq")
    dp = lax.axis_index("dp")
    core = seq % 2
    heads_here = HEADS // seq_n
    cols = heads_here * HEAD_DIM
    seq_len = tok * seq_n
    rows = w_qkv.shape[0]
    hid_here = w_fc2.shape[0] // seq_n
    hid = hid_here * dp_n
    groups = 2
    per = lat // groups
    own = per * tok

    cond_silu, silu_back = jax.vjp(jax.nn.silu, conditioning)
    cond_act = cond_silu.astype(BF)
    bias_here = lax.dynamic_slice(b_fc1, (seq * hid_here,), (hid_here,))
    small = jnp.concatenate([cond_act.reshape(lat * width), bias_here])
    small = dp_exchange(jnp.broadcast_to(small[None], (dp_n, lat * width + hid_here)))
    cond_all = small[:, : lat * width].reshape(dp_n * lat, width)
    fc1_bias = small[:, lat * width :].reshape(hid).astype(F32)
    cond_rows = lax.dynamic_slice(cond_all, (0, dp * rows), (dp_n * lat, rows))
    mod_terms = matmul(cond_rows, w_mod)
    piece = b_mod.shape[0]
    mod_terms = lax.dynamic_update_slice(
        mod_terms,
        lax.dynamic_slice(mod_terms, (0, dp * piece), (dp_n * lat, piece))
        + b_mod.astype(F32)[None],
        (0, dp * piece),
    )
    modulation = jnp.sum(dp_exchange(mod_terms.reshape(dp_n, lat, 6 * width)), axis=0)

    tok_slots = seq_gather(tokens)
    cot_slots = seq_gather(cotangent)

    qkv_here = jnp.concatenate(
        [lax.dynamic_slice(w_qkv, (0, t * width + seq * cols), (rows, cols)) for t in range(3)],
        axis=1,
    )
    qkv = dp_gather(qkv_here, lambda d: d).reshape(width, 3 * cols)
    half = rows // 2
    fc1_here = jnp.concatenate(
        [
            lax.dynamic_slice(w_fc1, (0, (d * seq_n + seq) * hid_here), (rows, hid_here))
            for d in range(dp_n)
        ],
        axis=1,
    )
    fc2_here = lax.dynamic_slice(w_fc2, (seq * hid_here, 0), (hid_here, width))
    proj_here = lax.dynamic_slice(w_proj, (core * half, 0), (half, width))
    together = hid == width
    proj_mine = lax.all_gather(proj_here, "dp", axis=0)
    if together:
        joined = lax.all_gather(jnp.concatenate([fc1_here, fc2_here]), "dp", axis=0)
    else:
        fc1 = lax.all_gather(fc1_here, "dp", axis=0, tiled=True)
        fc2 = lax.all_gather(fc2_here, "dp", axis=0, tiled=True)

    def part(g):
        return slice(g * per, (g + 1) * per)

    shift_attn, scale_attn, gate_attn, shift_mlp, scale_mlp, gate_mlp = [
        [modulation[part(g), None, i * width : (i + 1) * width] for g in range(groups)]
        for i in range(6)
    ]
    token_values = [tokens[part(g)].astype(F32) for g in range(groups)]
    normed_all, packed, mixed, log_sums, attended = [], [], [], [], []
    for g in range(groups):
        normed, rows_packed = qkv_forward(tok_slots, g, per, shift_attn[g], scale_attn[g], qkv)
        normed_all.append(normed.reshape(per * seq_len, width))
        packed.append(rows_packed.reshape(per, seq_len, 3 * cols))
        out, log_sum = attention(
            packed[g], mixed + cot_slots[-1:] if g else [], heads_here
        )
        mixed.append(out)
        log_sums.append(log_sum)
        out = out.reshape(per, seq_n, tok, cols)
        attended.append(
            jnp.concatenate(seq_exchange([out[:, j] for j in range(seq_n)]), axis=2).reshape(
                own, width
            )
        )

    proj_other = hop(proj_mine, "seq", 1)
    proj = jnp.where(
        core == 0,
        jnp.stack([proj_mine, proj_other], axis=1),
        jnp.stack([proj_other, proj_mine], axis=1),
    ).reshape(seq_n, cols, width)

    def by_place(blocks):
        return jnp.concatenate(
            [lax.dynamic_index_in_dim(blocks, seq ^ j, 0, keepdims=False) for j in range(seq_n)]
        )

    proj = by_place(proj)

    attn_out, resid_mid, normed_mlp, upstream = [], [], [], []
    for g in range(groups):
        attn_out.append(matmul(attended[g], proj).reshape(per, tok, width))
        resid_mid.append(token_values[g] + gate_attn[g] * attn_out[g])
        normed_mlp.append(
            (ln_parts(resid_mid[g])[0] * (1.0 + scale_mlp[g]) + shift_mlp[g]).astype(BF)
        )
        upstream.append(cotangent[part(g)].astype(F32))
    if together:
        fc1, fc2 = unpack(joined, normed_mlp[0], [rows, hid_here])
        fc1, fc2 = fc1.reshape(width, hid), fc2.reshape(hid, width)

    grad_fc1 = grad_fc2 = grad_bias1 = 0.0
    d_norm, activated = [], []
    for g in range(groups):
        x_all, d_mlp, active, d_hidden, terms, d_bias = mlp(
            seq_gather(normed_mlp[g]), cot_slots, g, gate_mlp[g], fc1, fc1_bias[None], fc2
        )
        d_norm.append(seq_reduce([terms[:, j].astype(F32) for j in range(seq_n)]))
        activated.append(active)
        flat = per * seq_len
        grad_fc2 = grad_fc2 + matmul_tn(active.reshape(flat, hid), d_mlp.reshape(flat, width))
        grad_fc1 = grad_fc1 + matmul_tn(x_all.reshape(flat, width), d_hidden.reshape(flat, hid))
        grad_bias1 = grad_bias1 + d_bias[0]
    grad_fc1 = grad_fc1.astype(BF).reshape(dp_n, rows, hid)
    grad_fc2 = grad_fc2.astype(BF).reshape(dp_n, hid_here, width)
    if together:
        grad_fc = pack(grad_fc1, grad_fc2, grad_bias1)
        sum_fc = lax.psum_scatter(grad_fc, "dp", scatter_dimension=0)
        sum_fc1, sum_fc2 = sum_fc[:rows], sum_fc[rows:]
    else:
        grad_fc = grad_fc1
        sum_fc1 = lax.psum_scatter(grad_fc1, "dp", scatter_dimension=0)
        sum_fc = sum_fc2 = lax.psum_scatter(grad_fc2, "dp", scatter_dimension=0)

    def stacked(terms):
        return jnp.concatenate(terms)

    d_shift_mlp, d_scale_mlp, d_gate_attn, d_resid, d_attn, d_attended = ([] for _ in range(6))
    d_mixed = []
    for g in range(groups):
        outs = resid_grad(
            d_norm[g], resid_mid[g], attn_out[g], cotangent, g, scale_mlp[g], gate_attn[g], proj,
            grad_fc, seq_n,
        )
        d_resid.append(outs[0])
        d_attn.append(outs[1].reshape(own, width))
        d_shift_mlp.append(outs[2][:, 0])
        d_scale_mlp.append(outs[3][:, 0])
        d_gate_attn.append(outs[4][:, 0])
        d_attended.append(outs[5])
        d_mixed.append(jnp.concatenate(seq_exchange(outs[5:]), axis=1))
    mlp_terms, mlp_near = [], []
    for g in range(groups):
        terms = mlp_out_terms(activated[g], fc2, d_attended[-1])
        mlp_terms.append(terms)
        mlp_near.append(seq_near([terms[:, j].astype(F32) for j in range(seq_n)]))
    grad_proj = by_place(
        matmul_tn(stacked(attended), stacked(d_attn)).astype(BF).reshape(seq_n, cols, width)
    ).reshape(dp_n, 2, half, width)
    proj_sent = hop(
        lax.dynamic_index_in_dim(grad_proj, 1 - core, axis=1, keepdims=False), "seq", 1
    )
    proj_terms = lax.dynamic_index_in_dim(grad_proj, core, axis=1, keepdims=False).astype(F32)
    proj_terms = proj_terms + proj_sent.astype(F32)

    d_packed, d_first, first_terms = [], [], []
    for g in range(groups):
        grads, terms = attention_grad(
            packed[g], mixed[g], log_sums[g], d_mixed[g], qkv,
            first_terms + [near[1] for near in mlp_near] if g else [d_attended[-1]] + mlp_terms,
            heads_here,
        )
        d_packed.append(grads.reshape(per * seq_len, 3 * cols))
        first_terms.append(terms)
        terms = terms.reshape(per, seq_n, tok, width)
        d_first.append(seq_reduce([terms[:, j].astype(F32) for j in range(seq_n)]))
    mlp_out = [seq_far(*near) for near in mlp_near]
    output = jnp.concatenate(
        [(resid_mid[g] + gate_mlp[g] * mlp_out[g]).astype(BF) for g in range(groups)]
    )
    d_gate_mlp = stacked([jnp.sum(upstream[g] * mlp_out[g], axis=1) for g in range(groups)])
    grad_qkv = matmul_tn(stacked(normed_all), stacked(d_packed)).astype(BF)
    last = pack_last(proj_terms, grad_qkv.reshape(dp_n, rows, 3 * cols), sum_fc)
    sum_last = lax.psum_scatter(last, "dp", scatter_dimension=0)
    sum_proj, sum_qkv = sum_last[:, : width // 2], sum_last[:, width // 2 :]
    grad_tokens, d_shift_attn, d_scale_attn = token_grad(
        d_first, d_resid, tokens, modulation[:, None, width : 2 * width], last
    )

    mod_part = jnp.concatenate(
        [d_shift_attn[:, 0], d_scale_attn[:, 0], stacked(d_gate_attn)]
        + [stacked(d_shift_mlp), stacked(d_scale_mlp), d_gate_mlp],
        axis=1,
    )
    bit = 1
    while bit < seq_n:
        mod_part = mod_part + hop(mod_part, "seq", bit)
        bit *= 2
    d_mod = dp_exchange(jnp.broadcast_to(mod_part.astype(BF)[None], (dp_n, lat, 6 * width)))
    d_mod = d_mod.reshape(dp_n * lat, 6 * width)
    share = 6 * width // (dp_n * seq_n)
    mod_cols = lax.dynamic_slice(d_mod, (0, (dp * seq_n + seq) * share), (dp_n * lat, share))
    grad_wmod = matmul_tn(cond_all, mod_cols)
    grad_bmod = jnp.sum(mod_cols.astype(F32), axis=0)
    back = jnp.concatenate(
        [
            matmul_nt(d_mod, w_mod).reshape(dp_n, lat * rows),
            grad_bias1.reshape(dp_n, hid_here),
        ],
        axis=1,
    )
    back = dp_exchange(back)
    d_cond = back[:, : lat * rows].reshape(dp_n, lat, rows)
    (grad_cond,) = silu_back(d_cond.transpose(1, 0, 2).reshape(lat, width))
    bias_out = jnp.sum(back[:, lat * rows :], axis=0)

    def to_owner(blocks):
        return lax.all_to_all(blocks, "seq", 0, 0, tiled=True).astype(F32)

    share = width // seq_n
    fc2_blocks = sum_fc2.reshape(hid_here, seq_n, share).transpose(1, 0, 2)
    fc1_blocks = sum_fc1.reshape(rows, seq_n, hid // seq_n).transpose(1, 0, 2)
    if together:
        received = to_owner(jnp.concatenate([fc1_blocks, fc2_blocks], axis=1))
        out_fc1, out_fc2 = received[:, :rows], received[:, rows:]
    else:
        out_fc1, out_fc2 = to_owner(fc1_blocks), to_owner(fc2_blocks)
    out_fc2 = out_fc2.reshape(seq_n * hid_here, share)
    out_fc1 = out_fc1.reshape(seq_n, rows, dp_n // seq_n, hid_here).transpose(1, 2, 0, 3)
    out_fc1 = out_fc1.reshape(rows, hid)
    proj_blocks = sum_proj.reshape(2, half, seq_n // 2, share).transpose(0, 2, 1, 3)
    proj_blocks = proj_blocks.reshape(seq_n, half, share)
    qkv_thirds = sum_qkv.reshape(rows, 3, cols).transpose(1, 0, 2)
    qkv_blocks = jnp.stack(
        [
            lax.dynamic_index_in_dim(
                qkv_thirds, jnp.minimum((3 * to - seq + seq_n - 1) // seq_n, 2), 0, keepdims=False
            )
            for to in range(seq_n)
        ]
    )
    received = lax.all_to_all(
        jnp.concatenate([qkv_blocks, proj_blocks], axis=1), "seq", 0, 0, tiled=True
    )
    out_qkv, out_proj = place_last(received, rows, seq)
    return (
        output,
        grad_tokens,
        grad_cond,
        grad_wmod,
        grad_bmod,
        out_qkv,
        out_proj,
        out_fc1,
        bias_out,
        out_fc2,
    )


def solution(mesh):
    placed = (
        P("dp", "seq", None),
        P("dp", None),
        P("dp", None),
        P("dp"),
        P("dp", None),
        P("dp", None),
        P("dp", None),
        P("dp"),
        P("dp", None),
        P("dp", "seq", None),
    )
    return jax.shard_map(
        on_device,
        mesh=mesh,
        in_specs=placed,
        out_specs=(
            P("dp", "seq", None),
            P("dp", "seq", None),
            P("dp", None),
            P(None, ("dp", "seq")),
            P(("dp", "seq")),
            P("dp", "seq"),
            P("dp", "seq"),
            P("dp", "seq"),
            P(("dp", "seq")),
            P("dp", "seq"),
        ),
        check_vma=False,
    )
```

```python
import math
from functools import partial

import jax
import jax.numpy as jnp
from jax import lax
from jax.experimental import pallas as pl
from jax.experimental.pallas import tpu as pltpu
from jax.sharding import PartitionSpec as P

HEADS = 16
HEAD_DIM = 72
BF = jnp.bfloat16
F32 = jnp.float32
GELU_C = 0.7978845608028654
GELU_A = 0.044715
VMEM_LIMIT = 60 * 2**20
EXP2_SCALE = HEAD_DIM ** (-0.5) * math.log2(math.e)


def hop(value, axis, bits):
    count = lax.axis_size(axis)
    return lax.ppermute(value, axis, [(i, i ^ bits) for i in range(count)])


def matmul(left, right):
    return jnp.dot(left, right, preferred_element_type=F32)


def matmul_nt(left, right):
    return lax.dot_general(left, right, (((1,), (1,)), ((), ())), preferred_element_type=F32)


def matmul_tn(left, right):
    return lax.dot_general(left, right, (((0,), (0,)), ((), ())), preferred_element_type=F32)


def ln_parts(values):
    row_mean = jnp.mean(values, axis=-1, keepdims=True)
    centred = values - row_mean
    row_var = jnp.mean(centred * centred, axis=-1, keepdims=True)
    inv_std = lax.rsqrt(row_var + 1e-06)
    return centred * inv_std, inv_std


def ln_backward(grad, normed, inv_std):
    mean_grad = jnp.mean(grad, axis=-1, keepdims=True)
    mean_inner = jnp.mean(grad * normed, axis=-1, keepdims=True)
    return (grad - mean_grad - normed * mean_inner) * inv_std


def seq_gather(mine):
    slots = {0: mine}
    bit = lax.axis_size("seq") // 2
    while bit:
        for j in list(slots):
            slots[j | bit] = hop(slots[j], "seq", bit)
        bit //= 2
    return [slots[j] for j in range(len(slots))]


def seq_step(slots, bit):
    kept = {j: v for j, v in slots.items() if not j & bit}
    for j in slots:
        if j & bit:
            kept[j ^ bit] = kept[j ^ bit] + hop(slots[j].astype(BF), "seq", bit).astype(F32)
    return kept


def seq_near(slots):
    slots = dict(enumerate(slots))
    bit = 1
    while len(slots) > 2:
        slots = seq_step(slots, bit)
        bit *= 2
    return slots[0], slots[bit].astype(BF)


def seq_far(kept, sent):
    return kept + hop(sent, "seq", lax.axis_size("seq") // 2).astype(F32)


def seq_reduce(slots):
    return seq_far(*seq_near(slots))


def seq_exchange(blocks):
    return [blocks[0]] + [hop(blocks[j], "seq", j) for j in range(1, len(blocks))]


def dp_exchange(value):
    return lax.all_to_all(value, "dp", 0, 0, tiled=True)


def dp_gather(mine, place):
    count = lax.axis_size("dp")
    index = lax.axis_index("dp")
    slots = {0: mine}
    for j in range(2, count, 2):
        slots[j] = hop(mine, "dp", j)
    for j in range(0, count, 2):
        slots[j + 1] = hop(slots[j], "dp", 1)
    whole = jnp.zeros((count,) + mine.shape, mine.dtype)
    for j in range(count):
        whole = lax.dynamic_update_index_in_dim(whole, slots[j], place(index ^ j), 0)
    return whole


def dp_scatter(terms, place):
    count = lax.axis_size("dp")
    index = lax.axis_index("dp")

    def block(j):
        return lax.dynamic_index_in_dim(terms, place(index ^ j), 0, keepdims=False)

    half = {}
    for j in list(range(2, count, 2)) + [0]:
        half[j] = block(j).astype(F32) + hop(block(j + 1), "dp", 1).astype(F32)
    total = half[0]
    for j in range(2, count, 2):
        total = total + hop(half[j].astype(BF), "dp", j).astype(F32)
    return total


def attend_kernel(heads, block, packed, *refs):
    mixed, log_sum, mixed_t = refs[-3:]
    seq_len = packed.shape[1]
    cols = heads * HEAD_DIM
    for h in range(heads):
        at = h * HEAD_DIM
        keys = packed[0, :, cols + at : cols + at + HEAD_DIM]
        values_t = packed[0, :, 2 * cols + at : 2 * cols + at + HEAD_DIM].astype(F32).T.astype(BF)
        for start in range(0, seq_len, block):
            queries = packed[0, start : start + block, at : at + HEAD_DIM]
            scores = matmul_nt(keys, queries)
            top = jnp.max(scores, axis=0, keepdims=True)
            exponent = jnp.exp2((scores - top) * EXP2_SCALE)
            total = jnp.sum(exponent, axis=0, keepdims=True)
            part = matmul(values_t, exponent.astype(BF)) / total
            mixed_t[at : at + HEAD_DIM, start : start + block] = part
            log_sum[0, h : h + 1, start : start + block] = top * EXP2_SCALE + jnp.log2(total)
    mixed[0] = mixed_t[...].T.astype(BF)


def attend_grad_kernel(heads, block, packed, mixed, log_sum, d_mixed, qkv, *refs):
    d_packed, terms, d_queries_t = refs[-3:]
    seq_len = packed.shape[1]
    cols = heads * HEAD_DIM
    inv_root = HEAD_DIM ** (-0.5)
    for h in range(heads):
        at = h * HEAD_DIM
        keys = packed[0, :, cols + at : cols + at + HEAD_DIM]
        values = packed[0, :, 2 * cols + at : 2 * cols + at + HEAD_DIM]
        keys_t = keys.astype(F32).T.astype(BF)
        d_keys = d_values = None
        for start in range(0, seq_len, block):
            queries = packed[0, start : start + block, at : at + HEAD_DIM]
            grads = d_mixed[0, start : start + block, at : at + HEAD_DIM]
            outs = mixed[0, start : start + block, at : at + HEAD_DIM]
            inner = jnp.sum(grads.astype(F32) * outs.astype(F32), axis=1, keepdims=True)
            inner = jnp.broadcast_to(inner, (block, 128)).T[0:1]
            scores = matmul_nt(keys, queries)
            probs = jnp.exp2(scores * EXP2_SCALE - log_sum[0, h : h + 1, start : start + block])
            d_probs = matmul_nt(values, grads)
            d_scores = (probs * (d_probs - inner)).astype(BF)
            d_v = matmul(probs.astype(BF), grads)
            d_k = matmul(d_scores, queries)
            d_values = d_v if d_values is None else d_values + d_v
            d_keys = d_k if d_keys is None else d_keys + d_k
            d_queries_t[at : at + HEAD_DIM, start : start + block] = matmul(keys_t, d_scores) * inv_root
        d_packed[0, :, cols + at : cols + at + HEAD_DIM] = (d_keys * inv_root).astype(BF)
        d_packed[0, :, 2 * cols + at : 2 * cols + at + HEAD_DIM] = d_values.astype(BF)
    d_packed[0, :, 0:cols] = d_queries_t[...].T.astype(BF)
    for start in range(0, seq_len, block):
        rows = d_packed[0, start : start + block]
        terms[0, start : start + block] = matmul_nt(rows, qkv[...]).astype(BF)


def row_spec(*shape):
    return pl.BlockSpec((1,) + shape, lambda i: (i, 0, 0))


def attention(packed, after, heads, block=1024):
    lat, seq_len, _ = packed.shape
    cols = heads * HEAD_DIM
    return pl.pallas_call(
        partial(attend_kernel, heads, block),
        grid=(lat,),
        in_specs=[row_spec(seq_len, 3 * cols)] + [pl.BlockSpec(memory_space=pl.ANY)] * len(after),
        out_specs=[row_spec(seq_len, cols), row_spec(heads, seq_len)],
        out_shape=[
            jax.ShapeDtypeStruct((lat, seq_len, cols), BF),
            jax.ShapeDtypeStruct((lat, heads, seq_len), F32),
        ],
        scratch_shapes=[pltpu.VMEM((cols, seq_len), F32)],
        compiler_params=pltpu.CompilerParams(vmem_limit_bytes=VMEM_LIMIT),
        name="attend",
    )(packed, *after)


def attention_grad(packed, mixed, log_sum, d_mixed, qkv, after, heads, block=512):
    lat, seq_len, _ = packed.shape
    cols = heads * HEAD_DIM
    return pl.pallas_call(
        partial(attend_grad_kernel, heads, block),
        grid=(lat,),
        in_specs=[
            row_spec(seq_len, 3 * cols),
            row_spec(seq_len, cols),
            row_spec(heads, seq_len),
            row_spec(seq_len, cols),
            pl.BlockSpec(qkv.shape, lambda i: (0, 0)),
        ]
        + [pl.BlockSpec(memory_space=pl.ANY)] * len(after),
        out_specs=[row_spec(seq_len, 3 * cols), row_spec(seq_len, qkv.shape[0])],
        out_shape=[
            jax.ShapeDtypeStruct((lat, seq_len, 3 * cols), BF),
            jax.ShapeDtypeStruct((lat, seq_len, qkv.shape[0]), BF),
        ],
        scratch_shapes=[pltpu.VMEM((cols, seq_len), F32)],
        compiler_params=pltpu.CompilerParams(vmem_limit_bytes=VMEM_LIMIT),
        name="attend_grad",
    )(packed, mixed, log_sum, d_mixed, qkv, *after)


def qkv_kernel(count, *refs):
    slots, (shift, scale, qkv, normed, packed) = refs[:count], refs[count:]
    chunk, width = slots[0].shape[1:]
    for j in range(count):
        value = ln_parts(slots[j][0].astype(F32))[0] * (1.0 + scale[0]) + shift[0]
        normed[0, j] = value.astype(BF)
    rows = normed[0].reshape(count * chunk, width)
    packed[0] = matmul(rows, qkv[...]).astype(BF).reshape(count, chunk, packed.shape[3])


def qkv_forward(slots, group, per, shift, scale, qkv):
    count = len(slots)
    _, tok, width = slots[0].shape
    chunk = max(16, 256 // count)
    row = pl.BlockSpec((1, 1, width), lambda i, c: (i, 0, 0))
    cols = qkv.shape[1]
    return pl.pallas_call(
        partial(qkv_kernel, count),
        grid=(per, tok // chunk),
        in_specs=[pl.BlockSpec((1, chunk, width), lambda i, c: (group * per + i, c, 0))] * count
        + [row, row, pl.BlockSpec((width, cols), lambda i, c: (0, 0))],
        out_specs=[
            pl.BlockSpec((1, count, chunk, width), lambda i, c: (i, 0, c, 0)),
            pl.BlockSpec((1, count, chunk, cols), lambda i, c: (i, 0, c, 0)),
        ],
        out_shape=[
            jax.ShapeDtypeStruct((per, count, tok, width), BF),
            jax.ShapeDtypeStruct((per, count, tok, cols), BF),
        ],
        compiler_params=pltpu.CompilerParams(vmem_limit_bytes=VMEM_LIMIT),
        name="qkv_forward",
    )(*slots, shift, scale, qkv)


def mlp_kernel(count, *refs):
    inputs, grads = refs[:count], refs[count : 2 * count]
    gate, fc1, bias, fc2 = refs[2 * count : 2 * count + 4]
    x_all, g_all, activated, d_hidden, d_norm, d_bias = refs[-6:]
    chunk, width = inputs[0].shape[1:]
    hid = bias.shape[1]
    fc1 = fc1[...].reshape(width, hid)
    fc2 = fc2[...].reshape(hid, width)
    for j in range(count):
        x_all[0, j] = inputs[j][0]
        g_all[0, j] = (gate[0] * grads[j][0].astype(F32)).astype(BF)
    x = x_all[0].reshape(count * chunk, width)
    g = g_all[0].reshape(count * chunk, width)
    hidden = matmul(x, fc1) + bias[...]
    square = hidden * hidden
    tanh = jnp.tanh(GELU_C * (hidden + GELU_A * hidden * square))
    half = 0.5 * (1.0 + tanh)
    activated[0] = (hidden * half).astype(BF).reshape(count, chunk, hid)
    slope = half + (0.5 * GELU_C) * hidden * (1.0 - tanh * tanh) * (1.0 + 3.0 * GELU_A * square)
    d_h = (matmul_nt(g, fc2) * slope).astype(BF)
    d_hidden[0] = d_h.reshape(count, chunk, hid)
    d_norm[0] = matmul_nt(d_h, fc1).astype(BF).reshape(count, chunk, width)

    @pl.when((pl.program_id(0) == 0) & (pl.program_id(1) == 0))
    def _():
        d_bias[...] = jnp.zeros_like(d_bias)

    d_bias[...] += jnp.sum(d_h.astype(F32), axis=0, keepdims=True)


def stored_spec(stored):
    array, rows, index = stored
    return pl.BlockSpec((array.shape[0], rows, array.shape[2]), lambda i, c: (0, index, 0))


def mlp(inputs, grads, group, gate, fc1, bias, fc2, after):
    count = len(inputs)
    per, tok, width = inputs[0].shape
    hid = bias.shape[1]
    chunk = max(16, 256 // count)
    slot = pl.BlockSpec((1, chunk, width), lambda i, c: (i, c, 0))
    late = pl.BlockSpec((1, chunk, width), lambda i, c: (group * per + i, c, 0))

    def whole(rows, cols):
        return pl.BlockSpec((rows, cols), lambda i, c: (0, 0))

    wide = pl.BlockSpec((1, count, chunk, width), lambda i, c: (i, 0, c, 0))
    inner = pl.BlockSpec((1, count, chunk, hid), lambda i, c: (i, 0, c, 0))
    shape_wide = jax.ShapeDtypeStruct((per, count, tok, width), BF)
    shape_inner = jax.ShapeDtypeStruct((per, count, tok, hid), BF)
    return pl.pallas_call(
        partial(mlp_kernel, count),
        grid=(per, tok // chunk),
        in_specs=[slot] * count
        + [late] * count
        + [pl.BlockSpec((1, 1, width), lambda i, c: (i, 0, 0))]
        + [stored_spec(fc1), whole(1, hid), stored_spec(fc2)]
        + [pl.BlockSpec(memory_space=pl.ANY)] * len(after),
        out_specs=[wide, wide, inner, inner, wide, whole(1, hid)],
        out_shape=[shape_wide, shape_wide, shape_inner, shape_inner, shape_wide]
        + [jax.ShapeDtypeStruct((1, hid), F32)],
        compiler_params=pltpu.CompilerParams(vmem_limit_bytes=VMEM_LIMIT),
        name="mlp",
    )(*inputs, *grads, gate, fc1[0], bias, fc2[0], *after)


def mlp_out_kernel(activated, fc2, after, out):
    count, chunk, hid = activated.shape[1:]
    rows = activated[0].reshape(count * chunk, hid)
    weight = fc2[...].reshape(hid, out.shape[3])
    out[0] = matmul(rows, weight).astype(BF).reshape(count, chunk, out.shape[3])


def mlp_out_terms(activated, fc2, after):
    per, count, tok, hid = activated.shape
    width = fc2[0].shape[2]
    chunk = max(16, 256 // count)
    return pl.pallas_call(
        mlp_out_kernel,
        grid=(per, tok // chunk),
        in_specs=[
            pl.BlockSpec((1, count, chunk, hid), lambda i, c: (i, 0, c, 0)),
            stored_spec(fc2),
            pl.BlockSpec(memory_space=pl.ANY),
        ],
        out_specs=pl.BlockSpec((1, count, chunk, width), lambda i, c: (i, 0, c, 0)),
        out_shape=jax.ShapeDtypeStruct((per, count, tok, width), BF),
        compiler_params=pltpu.CompilerParams(vmem_limit_bytes=VMEM_LIMIT),
        name="mlp_out_terms",
    )(activated, fc2[0], after)


def resid_grad_kernel(count, *refs):
    d_norm, resid_mid, attn_out, cotangent, scale, gate, proj, after = refs[:8]
    d_resid, d_attn, d_shift, d_scale, d_gate = refs[8:13]
    d_attended = refs[13:]
    normed, inv_std = ln_parts(resid_mid[0])
    grad = d_norm[0]
    total = cotangent[0].astype(F32) + ln_backward(grad * (1.0 + scale[0]), normed, inv_std)
    d_resid[0] = total
    d_a = (gate[0] * total).astype(BF)
    d_attn[0] = d_a
    back = matmul_nt(d_a, proj[...]).astype(BF)
    cols = back.shape[1] // count
    for j in range(count):
        d_attended[j][0] = back[:, j * cols : (j + 1) * cols]

    @pl.when(pl.program_id(1) == 0)
    def _():
        d_shift[...] = jnp.zeros_like(d_shift)
        d_scale[...] = jnp.zeros_like(d_scale)
        d_gate[...] = jnp.zeros_like(d_gate)

    d_shift[0] += jnp.sum(grad, axis=0, keepdims=True)
    d_scale[0] += jnp.sum(grad * normed, axis=0, keepdims=True)
    d_gate[0] += jnp.sum(total * attn_out[0], axis=0, keepdims=True)


def resid_grad(d_norm, resid_mid, attn_out, cotangent, group, scale, gate, proj, after, count):
    per, tok, width = d_norm.shape
    chunk = min(tok, 128)
    block = pl.BlockSpec((1, chunk, width), lambda i, c: (i, c, 0))
    row = pl.BlockSpec((1, 1, width), lambda i, c: (i, 0, 0))
    part = pl.BlockSpec((1, chunk, width // count), lambda i, c: (i, c, 0))
    row_shape = jax.ShapeDtypeStruct((per, 1, width), F32)
    return pl.pallas_call(
        partial(resid_grad_kernel, count),
        grid=(per, tok // chunk),
        in_specs=[
            block,
            block,
            block,
            pl.BlockSpec((1, chunk, width), lambda i, c: (group * per + i, c, 0)),
            row,
            row,
            pl.BlockSpec((width, width), lambda i, c: (0, 0)),
            pl.BlockSpec(memory_space=pl.ANY),
        ],
        out_specs=[block, block, row, row, row] + [part] * count,
        out_shape=[
            jax.ShapeDtypeStruct((per, tok, width), F32),
            jax.ShapeDtypeStruct((per, tok, width), BF),
            row_shape,
            row_shape,
            row_shape,
        ]
        + [jax.ShapeDtypeStruct((per, tok, width // count), BF)] * count,
        compiler_params=pltpu.CompilerParams(vmem_limit_bytes=VMEM_LIMIT),
        name="resid_grad",
    )(d_norm, resid_mid, attn_out, cotangent, scale, gate, proj, after)


def pack_kernel(first, second, after, out):
    rows = first.shape[1]
    out[0, :rows] = first[0]
    out[0, rows:] = second[0]


def pack(first, second, after):
    count, rows, width = first.shape
    more = second.shape[1]
    return pl.pallas_call(
        pack_kernel,
        grid=(count,),
        in_specs=[
            pl.BlockSpec((1, rows, width), lambda i: (i, 0, 0)),
            pl.BlockSpec((1, more, width), lambda i: (i, 0, 0)),
            pl.BlockSpec(memory_space=pl.ANY),
        ],
        out_specs=pl.BlockSpec((1, rows + more, width), lambda i: (i, 0, 0)),
        out_shape=jax.ShapeDtypeStruct((count, rows + more, width), first.dtype),
        compiler_params=pltpu.CompilerParams(vmem_limit_bytes=VMEM_LIMIT),
        name="pack",
    )(first, second, after)


def pack_last_kernel(proj_terms, qkv_terms, after, out):
    half = proj_terms.shape[2] // 2
    cols = qkv_terms.shape[2]
    folded = jnp.concatenate([proj_terms[0, :, :half], proj_terms[0, :, half:]], axis=0)
    out[0, :, :cols] = qkv_terms[0]
    out[0, :, cols:] = folded.astype(BF)


def pack_last(proj_terms, qkv_terms, after):
    count, half, width = proj_terms.shape
    _, rows, cols = qkv_terms.shape
    return pl.pallas_call(
        pack_last_kernel,
        grid=(count,),
        in_specs=[
            pl.BlockSpec((1, half, width), lambda i: (i, 0, 0)),
            pl.BlockSpec((1, rows, cols), lambda i: (i, 0, 0)),
            pl.BlockSpec(memory_space=pl.ANY),
        ],
        out_specs=pl.BlockSpec((1, rows, width // 2 + cols), lambda i: (i, 0, 0)),
        out_shape=jax.ShapeDtypeStruct((count, rows, width // 2 + cols), BF),
        compiler_params=pltpu.CompilerParams(vmem_limit_bytes=VMEM_LIMIT),
        name="pack_last",
    )(proj_terms, qkv_terms, after)


def token_grad_kernel(per, d_first, e_first, d_resid, e_resid, tokens, scale, after, *outs):
    grad_tokens, d_shift, d_scale = outs
    early = pl.program_id(0) < per
    grad = jnp.where(early, d_first[0], e_first[0])
    normed, inv_std = ln_parts(tokens[0].astype(F32))
    grad_tokens[0] = jnp.where(early, d_resid[0], e_resid[0]) + ln_backward(
        grad * (1.0 + scale[0]), normed, inv_std
    )

    @pl.when(pl.program_id(1) == 0)
    def _():
        d_shift[...] = jnp.zeros_like(d_shift)
        d_scale[...] = jnp.zeros_like(d_scale)

    d_shift[0] += jnp.sum(grad, axis=0, keepdims=True)
    d_scale[0] += jnp.sum(grad * normed, axis=0, keepdims=True)


def token_grad(d_first, d_resid, tokens, scale, after):
    lat, tok, width = tokens.shape
    per = lat // 2
    chunk = min(tok, 128)
    early = pl.BlockSpec((1, chunk, width), lambda i, c: (jnp.minimum(i, per - 1), c, 0))
    late = pl.BlockSpec((1, chunk, width), lambda i, c: (jnp.maximum(i, per) - per, c, 0))
    block = pl.BlockSpec((1, chunk, width), lambda i, c: (i, c, 0))
    row = pl.BlockSpec((1, 1, width), lambda i, c: (i, 0, 0))
    row_shape = jax.ShapeDtypeStruct((lat, 1, width), F32)
    return pl.pallas_call(
        partial(token_grad_kernel, per),
        grid=(lat, tok // chunk),
        in_specs=[early, late, early, late, block, row, pl.BlockSpec(memory_space=pl.ANY)],
        out_specs=[block, row, row],
        out_shape=[jax.ShapeDtypeStruct((lat, tok, width), F32), row_shape, row_shape],
        compiler_params=pltpu.CompilerParams(vmem_limit_bytes=VMEM_LIMIT),
        name="token_grad",
    )(*d_first, *d_resid, tokens, scale, after)


def place_last_kernel(rows, owners, received, out_qkv, out_proj):
    cols = received.shape[2]
    half = rows // 2
    for i in range(3):
        out_qkv[:, i * cols : (i + 1) * cols] = received[owners[i], :rows].astype(F32)
    for core in range(2):
        total = received[core, rows:].astype(F32)
        for j in range(core + 2, received.shape[0], 2):
            total = total + received[j, rows:].astype(F32)
        out_proj[core * half : (core + 1) * half] = total


def place_last(received, rows, seq):
    count, _, cols = received.shape
    owners = (3 * seq + jnp.arange(3, dtype=jnp.int32)) % count
    vmem = pl.BlockSpec(memory_space=pltpu.VMEM)
    return pl.pallas_call(
        partial(place_last_kernel, rows),
        in_specs=[pl.BlockSpec(memory_space=pltpu.SMEM), vmem],
        out_specs=[vmem, vmem],
        out_shape=[
            jax.ShapeDtypeStruct((rows, 3 * cols), F32),
            jax.ShapeDtypeStruct((rows, cols), F32),
        ],
        compiler_params=pltpu.CompilerParams(vmem_limit_bytes=VMEM_LIMIT),
        name="place_last",
    )(owners, received)


def on_device(tokens, conditioning, w_mod, b_mod, w_qkv, w_proj, w_fc1, b_fc1, w_fc2, cotangent):
    lat, tok, width = tokens.shape
    seq_n = lax.axis_size("seq")
    dp_n = lax.axis_size("dp")
    seq = lax.axis_index("seq")
    dp = lax.axis_index("dp")
    core = seq % 2
    heads_here = HEADS // seq_n
    cols = heads_here * HEAD_DIM
    seq_len = tok * seq_n
    rows = w_qkv.shape[0]
    hid_here = w_fc2.shape[0] // seq_n
    hid = hid_here * dp_n
    groups = 2
    per = lat // groups
    own = per * tok

    cond_silu, silu_back = jax.vjp(jax.nn.silu, conditioning)
    cond_act = cond_silu.astype(BF)
    bias_here = lax.dynamic_slice(b_fc1, (seq * hid_here,), (hid_here,))
    small = jnp.concatenate([cond_act.reshape(lat * width), bias_here])
    small = dp_exchange(jnp.broadcast_to(small[None], (dp_n, lat * width + hid_here)))
    cond_all = small[:, : lat * width].reshape(dp_n * lat, width)
    fc1_bias = small[:, lat * width :].reshape(hid).astype(F32)
    cond_rows = lax.dynamic_slice(cond_all, (0, dp * rows), (dp_n * lat, rows))
    mod_terms = matmul(cond_rows, w_mod)
    piece = b_mod.shape[0]
    mod_terms = lax.dynamic_update_slice(
        mod_terms,
        lax.dynamic_slice(mod_terms, (0, dp * piece), (dp_n * lat, piece))
        + b_mod.astype(F32)[None],
        (0, dp * piece),
    )
    modulation = jnp.sum(dp_exchange(mod_terms.reshape(dp_n, lat, 6 * width)), axis=0)

    tok_slots = seq_gather(tokens)
    cot_slots = seq_gather(cotangent)

    qkv_here = jnp.concatenate(
        [lax.dynamic_slice(w_qkv, (0, t * width + seq * cols), (rows, cols)) for t in range(3)],
        axis=1,
    )
    qkv = dp_gather(qkv_here, lambda d: d).reshape(width, 3 * cols)
    half = rows // 2
    fc1_here = jnp.concatenate(
        [
            lax.dynamic_slice(w_fc1, (0, (d * seq_n + seq) * hid_here), (rows, hid_here))
            for d in range(dp_n)
        ],
        axis=1,
    )
    fc2_here = lax.dynamic_slice(w_fc2, (seq * hid_here, 0), (hid_here, width))
    proj_here = lax.dynamic_slice(w_proj, (core * half, 0), (half, width))
    together = hid == width
    proj_mine = lax.all_gather(proj_here, "dp", axis=0)
    if together:
        joined = lax.all_gather(jnp.concatenate([fc1_here, fc2_here]), "dp", axis=0)
        fc1, fc2 = (joined, rows, 0), (joined, hid_here, 1)
    else:
        fc1 = (lax.all_gather(fc1_here, "dp", axis=0, tiled=True)[None], width, 0)
        fc2 = (lax.all_gather(fc2_here, "dp", axis=0, tiled=True)[None], hid, 0)

    def part(g):
        return slice(g * per, (g + 1) * per)

    shift_attn, scale_attn, gate_attn, shift_mlp, scale_mlp, gate_mlp = [
        [modulation[part(g), None, i * width : (i + 1) * width] for g in range(groups)]
        for i in range(6)
    ]
    token_values = [tokens[part(g)].astype(F32) for g in range(groups)]
    proj_other = hop(proj_mine, "seq", 1)
    proj = jnp.where(
        core == 0,
        jnp.stack([proj_mine, proj_other], axis=1),
        jnp.stack([proj_other, proj_mine], axis=1),
    ).reshape(seq_n, cols, width)

    def by_place(blocks):
        return jnp.concatenate(
            [lax.dynamic_index_in_dim(blocks, seq ^ j, 0, keepdims=False) for j in range(seq_n)]
        )

    proj = by_place(proj)

    normed_all, packed, mixed, log_sums, attended = [], [], [], [], []
    attn_out, resid_mid, normed_mlp, upstream = [], [], [], []
    for g in range(groups):
        normed, rows_packed = qkv_forward(tok_slots, g, per, shift_attn[g], scale_attn[g], qkv)
        normed_all.append(normed.reshape(per * seq_len, width))
        packed.append(rows_packed.reshape(per, seq_len, 3 * cols))
        out, log_sum = attention(
            packed[g], normed_mlp + cot_slots[-1:] if g else [], heads_here
        )
        mixed.append(out)
        log_sums.append(log_sum)
        out = out.reshape(per, seq_n, tok, cols)
        attended.append(
            jnp.concatenate(seq_exchange([out[:, j] for j in range(seq_n)]), axis=2).reshape(
                own, width
            )
        )
        attn_out.append(matmul(attended[g], proj).reshape(per, tok, width))
        resid_mid.append(token_values[g] + gate_attn[g] * attn_out[g])
        normed_mlp.append(
            (ln_parts(resid_mid[g])[0] * (1.0 + scale_mlp[g]) + shift_mlp[g]).astype(BF)
        )
        upstream.append(cotangent[part(g)].astype(F32))

    grad_fc1 = grad_fc2 = grad_bias1 = 0.0
    d_near, activated = [], []
    for g in range(groups):
        x_all, d_mlp, active, d_hidden, terms, d_bias = mlp(
            seq_gather(normed_mlp[g]), cot_slots, g, gate_mlp[g], fc1, fc1_bias[None], fc2,
            [near[1] for near in d_near],
        )
        d_near.append(seq_near([terms[:, j].astype(F32) for j in range(seq_n)]))
        activated.append(active)
        flat = per * seq_len
        grad_fc2 = grad_fc2 + matmul_tn(active.reshape(flat, hid), d_mlp.reshape(flat, width))
        grad_fc1 = grad_fc1 + matmul_tn(x_all.reshape(flat, width), d_hidden.reshape(flat, hid))
        grad_bias1 = grad_bias1 + d_bias[0]
    grad_fc1 = grad_fc1.astype(BF).reshape(dp_n, rows, hid)
    grad_fc2 = grad_fc2.astype(BF).reshape(dp_n, hid_here, width)
    if together:
        grad_fc = pack(grad_fc1, grad_fc2, d_near[-1][1])
        sum_fc = lax.psum_scatter(grad_fc, "dp", scatter_dimension=0)
        sum_fc1, sum_fc2 = sum_fc[:rows], sum_fc[rows:]
    else:
        grad_fc = grad_fc1
        sum_fc1 = lax.psum_scatter(grad_fc1, "dp", scatter_dimension=0)
        sum_fc = sum_fc2 = lax.psum_scatter(grad_fc2, "dp", scatter_dimension=0)

    def stacked(terms):
        return jnp.concatenate(terms)

    d_shift_mlp, d_scale_mlp, d_gate_attn, d_resid, d_attn, d_attended = ([] for _ in range(6))
    d_mixed = []
    for g in range(groups):
        outs = resid_grad(
            seq_far(*d_near[g]), resid_mid[g], attn_out[g], cotangent, g, scale_mlp[g],
            gate_attn[g], proj, d_attended[0] if g else grad_fc, seq_n,
        )
        d_resid.append(outs[0])
        d_attn.append(outs[1].reshape(own, width))
        d_shift_mlp.append(outs[2][:, 0])
        d_scale_mlp.append(outs[3][:, 0])
        d_gate_attn.append(outs[4][:, 0])
        d_attended.append(outs[5])
        d_mixed.append(jnp.concatenate(seq_exchange(outs[5:]), axis=1))
    mlp_terms, mlp_near = [], []
    for g in range(groups):
        terms = mlp_out_terms(activated[g], fc2, d_attended[-1])
        mlp_terms.append(terms)
        mlp_near.append(seq_near([terms[:, j].astype(F32) for j in range(seq_n)]))
    grad_proj = by_place(
        matmul_tn(stacked(attended), stacked(d_attn)).astype(BF).reshape(seq_n, cols, width)
    ).reshape(dp_n, 2, half, width)
    proj_sent = hop(
        lax.dynamic_index_in_dim(grad_proj, 1 - core, axis=1, keepdims=False), "seq", 1
    )
    proj_terms = lax.dynamic_index_in_dim(grad_proj, core, axis=1, keepdims=False).astype(F32)
    proj_terms = proj_terms + proj_sent.astype(F32)

    d_packed, d_first, first_terms = [], [], []
    for g in range(groups):
        grads, terms = attention_grad(
            packed[g], mixed[g], log_sums[g], d_mixed[g], qkv,
            first_terms + [near[1] for near in mlp_near] if g else [d_attended[-1]] + mlp_terms,
            heads_here,
        )
        d_packed.append(grads.reshape(per * seq_len, 3 * cols))
        first_terms.append(terms)
        terms = terms.reshape(per, seq_n, tok, width)
        d_first.append(seq_reduce([terms[:, j].astype(F32) for j in range(seq_n)]))
    mlp_out = [seq_far(*near) for near in mlp_near]
    output = jnp.concatenate(
        [(resid_mid[g] + gate_mlp[g] * mlp_out[g]).astype(BF) for g in range(groups)]
    )
    d_gate_mlp = stacked([jnp.sum(upstream[g] * mlp_out[g], axis=1) for g in range(groups)])
    grad_qkv = matmul_tn(stacked(normed_all), stacked(d_packed)).astype(BF)
    last = pack_last(proj_terms, grad_qkv.reshape(dp_n, rows, 3 * cols), sum_fc)
    sum_last = lax.psum_scatter(last, "dp", scatter_dimension=0)
    sum_qkv, sum_proj = sum_last[:, : 3 * cols], sum_last[:, 3 * cols :]
    grad_tokens, d_shift_attn, d_scale_attn = token_grad(
        d_first, d_resid, tokens, modulation[:, None, width : 2 * width], last
    )

    mod_part = jnp.concatenate(
        [d_shift_attn[:, 0], d_scale_attn[:, 0], stacked(d_gate_attn)]
        + [stacked(d_shift_mlp), stacked(d_scale_mlp), d_gate_mlp],
        axis=1,
    )
    bit = 1
    while bit < seq_n:
        mod_part = mod_part + hop(mod_part, "seq", bit)
        bit *= 2
    d_mod = dp_exchange(jnp.broadcast_to(mod_part.astype(BF)[None], (dp_n, lat, 6 * width)))
    d_mod = d_mod.reshape(dp_n * lat, 6 * width)
    share = 6 * width // (dp_n * seq_n)
    mod_cols = lax.dynamic_slice(d_mod, (0, (dp * seq_n + seq) * share), (dp_n * lat, share))
    grad_wmod = matmul_tn(cond_all, mod_cols)
    grad_bmod = jnp.sum(mod_cols.astype(F32), axis=0)
    back = jnp.concatenate(
        [
            matmul_nt(d_mod, w_mod).reshape(dp_n, lat * rows),
            grad_bias1.reshape(dp_n, hid_here),
        ],
        axis=1,
    )
    back = dp_exchange(back)
    d_cond = back[:, : lat * rows].reshape(dp_n, lat, rows)
    (grad_cond,) = silu_back(d_cond.transpose(1, 0, 2).reshape(lat, width))
    bias_out = jnp.sum(back[:, lat * rows :], axis=0)

    def to_owner(blocks):
        return lax.all_to_all(blocks, "seq", 0, 0, tiled=True).astype(F32)

    share = width // seq_n
    fc2_blocks = sum_fc2.reshape(hid_here, seq_n, share).transpose(1, 0, 2)
    fc1_blocks = sum_fc1.reshape(rows, seq_n, hid // seq_n).transpose(1, 0, 2)
    if together:
        received = to_owner(jnp.concatenate([fc1_blocks, fc2_blocks], axis=1))
        out_fc1, out_fc2 = received[:, :rows], received[:, rows:]
    else:
        out_fc1, out_fc2 = to_owner(fc1_blocks), to_owner(fc2_blocks)
    out_fc2 = out_fc2.reshape(seq_n * hid_here, share)
    out_fc1 = out_fc1.reshape(seq_n, rows, dp_n // seq_n, hid_here).transpose(1, 2, 0, 3)
    out_fc1 = out_fc1.reshape(rows, hid)
    proj_blocks = sum_proj.reshape(2, half, seq_n // 2, share).transpose(0, 2, 1, 3)
    proj_blocks = proj_blocks.reshape(seq_n, half, share)
    qkv_thirds = sum_qkv.reshape(rows, 3, cols).transpose(1, 0, 2)
    qkv_blocks = jnp.stack(
        [
            lax.dynamic_index_in_dim(
                qkv_thirds, jnp.minimum((3 * to - seq + seq_n - 1) // seq_n, 2), 0, keepdims=False
            )
            for to in range(seq_n)
        ]
    )
    received = lax.all_to_all(
        jnp.concatenate([qkv_blocks, proj_blocks], axis=1), "seq", 0, 0, tiled=True
    )
    out_qkv, out_proj = place_last(received, rows, seq)
    return (
        output,
        grad_tokens,
        grad_cond,
        grad_wmod,
        grad_bmod,
        out_qkv,
        out_proj,
        out_fc1,
        bias_out,
        out_fc2,
    )


def solution(mesh):
    placed = (
        P("dp", "seq", None),
        P("dp", None),
        P("dp", None),
        P("dp"),
        P("dp", None),
        P("dp", None),
        P("dp", None),
        P("dp"),
        P("dp", None),
        P("dp", "seq", None),
    )
    return jax.shard_map(
        on_device,
        mesh=mesh,
        in_specs=placed,
        out_specs=(
            P("dp", "seq", None),
            P("dp", "seq", None),
            P("dp", None),
            P(None, ("dp", "seq")),
            P(("dp", "seq")),
            P("dp", "seq"),
            P("dp", "seq"),
            P("dp", "seq"),
            P(("dp", "seq")),
            P("dp", "seq"),
        ),
        check_vma=False,
    )
```

```python
import math
from functools import partial

import jax
import jax.numpy as jnp
from jax import lax
from jax.experimental import pallas as pl
from jax.experimental.pallas import tpu as pltpu
from jax.sharding import PartitionSpec as P

HEADS = 16
HEAD_DIM = 72
BF = jnp.bfloat16
F32 = jnp.float32
GELU_C = 0.7978845608028654
GELU_A = 0.044715
VMEM_LIMIT = 60 * 2**20
EXP2_SCALE = HEAD_DIM ** (-0.5) * math.log2(math.e)


def hop(value, axis, bits):
    count = lax.axis_size(axis)
    return lax.ppermute(value, axis, [(i, i ^ bits) for i in range(count)])


def matmul(left, right):
    return jnp.dot(left, right, preferred_element_type=F32)


def matmul_nt(left, right):
    return lax.dot_general(left, right, (((1,), (1,)), ((), ())), preferred_element_type=F32)


def matmul_tn(left, right):
    return lax.dot_general(left, right, (((0,), (0,)), ((), ())), preferred_element_type=F32)


def ln_parts(values):
    row_mean = jnp.mean(values, axis=-1, keepdims=True)
    centred = values - row_mean
    row_var = jnp.mean(centred * centred, axis=-1, keepdims=True)
    inv_std = lax.rsqrt(row_var + 1e-06)
    return centred * inv_std, inv_std


def ln_backward(grad, normed, inv_std):
    mean_grad = jnp.mean(grad, axis=-1, keepdims=True)
    mean_inner = jnp.mean(grad * normed, axis=-1, keepdims=True)
    return (grad - mean_grad - normed * mean_inner) * inv_std


def seq_gather(mine):
    slots = {0: mine}
    bit = lax.axis_size("seq") // 2
    while bit:
        for j in list(slots):
            slots[j | bit] = hop(slots[j], "seq", bit)
        bit //= 2
    return [slots[j] for j in range(len(slots))]


def seq_step(slots, bit):
    kept = {j: v for j, v in slots.items() if not j & bit}
    for j in slots:
        if j & bit:
            kept[j ^ bit] = kept[j ^ bit] + hop(slots[j].astype(BF), "seq", bit).astype(F32)
    return kept


def seq_near(slots):
    slots = dict(enumerate(slots))
    bit = 1
    while len(slots) > 2:
        slots = seq_step(slots, bit)
        bit *= 2
    return slots[0], slots[bit].astype(BF)


def far_hop(sent):
    return hop(sent, "seq", lax.axis_size("seq") // 2)


def seq_far(kept, sent):
    return kept + far_hop(sent).astype(F32)


def seq_exchange(blocks):
    return [blocks[0]] + [hop(blocks[j], "seq", j) for j in range(1, len(blocks))]


def dp_exchange(value):
    return lax.all_to_all(value, "dp", 0, 0, tiled=True)


def dp_gather(mine, place):
    count = lax.axis_size("dp")
    index = lax.axis_index("dp")
    slots = {0: mine}
    for j in range(2, count, 2):
        slots[j] = hop(mine, "dp", j)
    for j in range(0, count, 2):
        slots[j + 1] = hop(slots[j], "dp", 1)
    whole = jnp.zeros((count,) + mine.shape, mine.dtype)
    for j in range(count):
        whole = lax.dynamic_update_index_in_dim(whole, slots[j], place(index ^ j), 0)
    return whole


def dp_scatter(terms, place):
    count = lax.axis_size("dp")
    index = lax.axis_index("dp")

    def block(j):
        return lax.dynamic_index_in_dim(terms, place(index ^ j), 0, keepdims=False)

    half = {}
    for j in list(range(2, count, 2)) + [0]:
        half[j] = block(j).astype(F32) + hop(block(j + 1), "dp", 1).astype(F32)
    total = half[0]
    for j in range(2, count, 2):
        total = total + hop(half[j].astype(BF), "dp", j).astype(F32)
    return total


def attend_kernel(heads, block, packed, *refs):
    mixed, log_sum, mixed_t = refs[-3:]
    seq_len = packed.shape[1]
    cols = heads * HEAD_DIM
    for h in range(heads):
        at = h * HEAD_DIM
        keys = packed[0, :, cols + at : cols + at + HEAD_DIM]
        values_t = packed[0, :, 2 * cols + at : 2 * cols + at + HEAD_DIM].astype(F32).T.astype(BF)
        for start in range(0, seq_len, block):
            queries = packed[0, start : start + block, at : at + HEAD_DIM]
            scores = matmul_nt(keys, queries)
            top = jnp.max(scores, axis=0, keepdims=True)
            exponent = jnp.exp2((scores - top) * EXP2_SCALE)
            total = jnp.sum(exponent, axis=0, keepdims=True)
            part = matmul(values_t, exponent.astype(BF)) / total
            mixed_t[at : at + HEAD_DIM, start : start + block] = part
            log_sum[0, h : h + 1, start : start + block] = top * EXP2_SCALE + jnp.log2(total)
    mixed[0] = mixed_t[...].T.astype(BF)


def attend_grad_kernel(heads, block, count, packed, mixed, log_sum, qkv, *refs):
    d_packed, terms, d_queries_t, d_mixed = refs[-4:]
    tok = refs[0].shape[1]
    for j in range(count):
        d_mixed[0, j * tok : (j + 1) * tok] = refs[j][0]
    seq_len = packed.shape[1]
    cols = heads * HEAD_DIM
    inv_root = HEAD_DIM ** (-0.5)
    for h in range(heads):
        at = h * HEAD_DIM
        keys = packed[0, :, cols + at : cols + at + HEAD_DIM]
        values = packed[0, :, 2 * cols + at : 2 * cols + at + HEAD_DIM]
        keys_t = keys.astype(F32).T.astype(BF)
        d_keys = d_values = None
        for start in range(0, seq_len, block):
            queries = packed[0, start : start + block, at : at + HEAD_DIM]
            grads = d_mixed[0, start : start + block, at : at + HEAD_DIM]
            outs = mixed[0, start : start + block, at : at + HEAD_DIM]
            inner = jnp.sum(grads.astype(F32) * outs.astype(F32), axis=1, keepdims=True)
            inner = jnp.broadcast_to(inner, (block, 128)).T[0:1]
            scores = matmul_nt(keys, queries)
            probs = jnp.exp2(scores * EXP2_SCALE - log_sum[0, h : h + 1, start : start + block])
            d_probs = matmul_nt(values, grads)
            d_scores = (probs * (d_probs - inner)).astype(BF)
            d_v = matmul(probs.astype(BF), grads)
            d_k = matmul(d_scores, queries)
            d_values = d_v if d_values is None else d_values + d_v
            d_keys = d_k if d_keys is None else d_keys + d_k
            d_queries_t[at : at + HEAD_DIM, start : start + block] = matmul(keys_t, d_scores) * inv_root
        d_packed[0, :, cols + at : cols + at + HEAD_DIM] = (d_keys * inv_root).astype(BF)
        d_packed[0, :, 2 * cols + at : 2 * cols + at + HEAD_DIM] = d_values.astype(BF)
    d_packed[0, :, 0:cols] = d_queries_t[...].T.astype(BF)
    for start in range(0, seq_len, block):
        rows = d_packed[0, start : start + block]
        terms[0, start : start + block] = matmul_nt(rows, qkv[...]).astype(BF)


def row_spec(*shape):
    return pl.BlockSpec((1,) + shape, lambda i: (i, 0, 0))


def attention(packed, after, heads, block=1024):
    lat, seq_len, _ = packed.shape
    cols = heads * HEAD_DIM
    return pl.pallas_call(
        partial(attend_kernel, heads, block),
        grid=(lat,),
        in_specs=[row_spec(seq_len, 3 * cols)] + [pl.BlockSpec(memory_space=pl.ANY)] * len(after),
        out_specs=[row_spec(seq_len, cols), row_spec(heads, seq_len)],
        out_shape=[
            jax.ShapeDtypeStruct((lat, seq_len, cols), BF),
            jax.ShapeDtypeStruct((lat, heads, seq_len), F32),
        ],
        scratch_shapes=[pltpu.VMEM((cols, seq_len), F32)],
        compiler_params=pltpu.CompilerParams(vmem_limit_bytes=VMEM_LIMIT),
        name="attend",
    )(packed, *after)


def attention_grad(packed, mixed, log_sum, d_mixed, qkv, after, heads, block=512):
    lat, seq_len, _ = packed.shape
    cols = heads * HEAD_DIM
    return pl.pallas_call(
        partial(attend_grad_kernel, heads, block, len(d_mixed)),
        grid=(lat,),
        in_specs=[
            row_spec(seq_len, 3 * cols),
            row_spec(seq_len, cols),
            row_spec(heads, seq_len),
            pl.BlockSpec(qkv.shape, lambda i: (0, 0)),
        ]
        + [row_spec(seq_len // len(d_mixed), cols)] * len(d_mixed)
        + [pl.BlockSpec(memory_space=pl.ANY)] * len(after),
        out_specs=[row_spec(seq_len, 3 * cols), row_spec(seq_len, qkv.shape[0])],
        out_shape=[
            jax.ShapeDtypeStruct((lat, seq_len, 3 * cols), BF),
            jax.ShapeDtypeStruct((lat, seq_len, qkv.shape[0]), BF),
        ],
        scratch_shapes=[pltpu.VMEM((cols, seq_len), F32), pltpu.VMEM((1, seq_len, cols), BF)],
        compiler_params=pltpu.CompilerParams(vmem_limit_bytes=VMEM_LIMIT),
        name="attend_grad",
    )(packed, mixed, log_sum, qkv, *d_mixed, *after)


def qkv_kernel(count, *refs):
    slots, (shift, scale, qkv, normed, packed) = refs[:count], refs[count:]
    chunk, width = slots[0].shape[1:]
    for j in range(count):
        value = ln_parts(slots[j][0].astype(F32))[0] * (1.0 + scale[0]) + shift[0]
        normed[0, j] = value.astype(BF)
    rows = normed[0].reshape(count * chunk, width)
    packed[0] = matmul(rows, qkv[...]).astype(BF).reshape(count, chunk, packed.shape[3])


def qkv_forward(slots, group, per, shift, scale, qkv):
    count = len(slots)
    _, tok, width = slots[0].shape
    chunk = max(16, 256 // count)
    row = pl.BlockSpec((1, 1, width), lambda i, c: (i, 0, 0))
    cols = qkv.shape[1]
    return pl.pallas_call(
        partial(qkv_kernel, count),
        grid=(per, tok // chunk),
        in_specs=[pl.BlockSpec((1, chunk, width), lambda i, c: (group * per + i, c, 0))] * count
        + [row, row, pl.BlockSpec((width, cols), lambda i, c: (0, 0))],
        out_specs=[
            pl.BlockSpec((1, count, chunk, width), lambda i, c: (i, 0, c, 0)),
            pl.BlockSpec((1, count, chunk, cols), lambda i, c: (i, 0, c, 0)),
        ],
        out_shape=[
            jax.ShapeDtypeStruct((per, count, tok, width), BF),
            jax.ShapeDtypeStruct((per, count, tok, cols), BF),
        ],
        compiler_params=pltpu.CompilerParams(vmem_limit_bytes=VMEM_LIMIT),
        name="qkv_forward",
    )(*slots, shift, scale, qkv)


def mlp_kernel(count, *refs):
    inputs, grads = refs[:count], refs[count : 2 * count]
    gate, fc1, bias, fc2 = refs[2 * count : 2 * count + 4]
    x_all, g_all, activated, d_hidden, d_norm, d_bias = refs[-6:]
    chunk, width = inputs[0].shape[1:]
    hid = bias.shape[1]
    fc1 = fc1[...].reshape(width, hid)
    fc2 = fc2[...].reshape(hid, width)
    for j in range(count):
        x_all[0, j] = inputs[j][0]
        g_all[0, j] = (gate[0] * grads[j][0].astype(F32)).astype(BF)
    x = x_all[0].reshape(count * chunk, width)
    g = g_all[0].reshape(count * chunk, width)
    hidden = matmul(x, fc1) + bias[...]
    square = hidden * hidden
    tanh = jnp.tanh(GELU_C * (hidden + GELU_A * hidden * square))
    half = 0.5 * (1.0 + tanh)
    activated[0] = (hidden * half).astype(BF).reshape(count, chunk, hid)
    slope = half + (0.5 * GELU_C) * hidden * (1.0 - tanh * tanh) * (1.0 + 3.0 * GELU_A * square)
    d_h = (matmul_nt(g, fc2) * slope).astype(BF)
    d_hidden[0] = d_h.reshape(count, chunk, hid)
    d_norm[0] = matmul_nt(d_h, fc1).astype(BF).reshape(count, chunk, width)

    @pl.when((pl.program_id(0) == 0) & (pl.program_id(1) == 0))
    def _():
        d_bias[...] = jnp.zeros_like(d_bias)

    d_bias[...] += jnp.sum(d_h.astype(F32), axis=0, keepdims=True)


def stored_spec(stored):
    array, rows, index = stored
    return pl.BlockSpec((array.shape[0], rows, array.shape[2]), lambda i, c: (0, index, 0))


def mlp(inputs, grads, group, gate, fc1, bias, fc2, after):
    count = len(inputs)
    per, tok, width = inputs[0].shape
    hid = bias.shape[1]
    chunk = max(16, 256 // count)
    slot = pl.BlockSpec((1, chunk, width), lambda i, c: (i, c, 0))
    late = pl.BlockSpec((1, chunk, width), lambda i, c: (group * per + i, c, 0))

    def whole(rows, cols):
        return pl.BlockSpec((rows, cols), lambda i, c: (0, 0))

    wide = pl.BlockSpec((1, count, chunk, width), lambda i, c: (i, 0, c, 0))
    inner = pl.BlockSpec((1, count, chunk, hid), lambda i, c: (i, 0, c, 0))
    shape_wide = jax.ShapeDtypeStruct((per, count, tok, width), BF)
    shape_inner = jax.ShapeDtypeStruct((per, count, tok, hid), BF)
    return pl.pallas_call(
        partial(mlp_kernel, count),
        grid=(per, tok // chunk),
        in_specs=[slot] * count
        + [late] * count
        + [pl.BlockSpec((1, 1, width), lambda i, c: (i, 0, 0))]
        + [stored_spec(fc1), whole(1, hid), stored_spec(fc2)]
        + [pl.BlockSpec(memory_space=pl.ANY)] * len(after),
        out_specs=[wide, wide, inner, inner, wide, whole(1, hid)],
        out_shape=[shape_wide, shape_wide, shape_inner, shape_inner, shape_wide]
        + [jax.ShapeDtypeStruct((1, hid), F32)],
        compiler_params=pltpu.CompilerParams(vmem_limit_bytes=VMEM_LIMIT),
        name="mlp",
    )(*inputs, *grads, gate, fc1[0], bias, fc2[0], *after)


def mlp_out_kernel(activated, fc2, after, out):
    count, chunk, hid = activated.shape[1:]
    rows = activated[0].reshape(count * chunk, hid)
    weight = fc2[...].reshape(hid, out.shape[3])
    out[0] = matmul(rows, weight).astype(BF).reshape(count, chunk, out.shape[3])


def mlp_out_terms(activated, fc2, after):
    per, count, tok, hid = activated.shape
    width = fc2[0].shape[2]
    chunk = max(16, 256 // count)
    return pl.pallas_call(
        mlp_out_kernel,
        grid=(per, tok // chunk),
        in_specs=[
            pl.BlockSpec((1, count, chunk, hid), lambda i, c: (i, 0, c, 0)),
            stored_spec(fc2),
            pl.BlockSpec(memory_space=pl.ANY),
        ],
        out_specs=pl.BlockSpec((1, count, chunk, width), lambda i, c: (i, 0, c, 0)),
        out_shape=jax.ShapeDtypeStruct((per, count, tok, width), BF),
        compiler_params=pltpu.CompilerParams(vmem_limit_bytes=VMEM_LIMIT),
        name="mlp_out_terms",
    )(activated, fc2[0], after)


def resid_grad_kernel(count, *refs):
    d_norm, resid_mid, attn_out, cotangent, scale, gate, proj, after = refs[:8]
    d_resid, d_attn, d_shift, d_scale, d_gate = refs[8:13]
    d_attended = refs[13:]
    normed, inv_std = ln_parts(resid_mid[0])
    grad = d_norm[0]
    total = cotangent[0].astype(F32) + ln_backward(grad * (1.0 + scale[0]), normed, inv_std)
    d_resid[0] = total
    d_a = (gate[0] * total).astype(BF)
    d_attn[0] = d_a
    back = matmul_nt(d_a, proj[...]).astype(BF)
    cols = back.shape[1] // count
    for j in range(count):
        d_attended[j][0] = back[:, j * cols : (j + 1) * cols]

    @pl.when(pl.program_id(1) == 0)
    def _():
        d_shift[...] = jnp.zeros_like(d_shift)
        d_scale[...] = jnp.zeros_like(d_scale)
        d_gate[...] = jnp.zeros_like(d_gate)

    d_shift[0] += jnp.sum(grad, axis=0, keepdims=True)
    d_scale[0] += jnp.sum(grad * normed, axis=0, keepdims=True)
    d_gate[0] += jnp.sum(total * attn_out[0], axis=0, keepdims=True)


def resid_grad(d_norm, resid_mid, attn_out, cotangent, group, scale, gate, proj, after, count):
    per, tok, width = d_norm.shape
    chunk = min(tok, 128)
    block = pl.BlockSpec((1, chunk, width), lambda i, c: (i, c, 0))
    row = pl.BlockSpec((1, 1, width), lambda i, c: (i, 0, 0))
    part = pl.BlockSpec((1, chunk, width // count), lambda i, c: (i, c, 0))
    row_shape = jax.ShapeDtypeStruct((per, 1, width), F32)
    return pl.pallas_call(
        partial(resid_grad_kernel, count),
        grid=(per, tok // chunk),
        in_specs=[
            block,
            block,
            block,
            pl.BlockSpec((1, chunk, width), lambda i, c: (group * per + i, c, 0)),
            row,
            row,
            pl.BlockSpec((width, width), lambda i, c: (0, 0)),
            pl.BlockSpec(memory_space=pl.ANY),
        ],
        out_specs=[block, block, row, row, row] + [part] * count,
        out_shape=[
            jax.ShapeDtypeStruct((per, tok, width), F32),
            jax.ShapeDtypeStruct((per, tok, width), BF),
            row_shape,
            row_shape,
            row_shape,
        ]
        + [jax.ShapeDtypeStruct((per, tok, width // count), BF)] * count,
        compiler_params=pltpu.CompilerParams(vmem_limit_bytes=VMEM_LIMIT),
        name="resid_grad",
    )(d_norm, resid_mid, attn_out, cotangent, scale, gate, proj, after)


def pack_kernel(first, second, after, out):
    rows = first.shape[1]
    out[0, :rows] = first[0]
    out[0, rows:] = second[0]


def pack(first, second, after):
    count, rows, width = first.shape
    more = second.shape[1]
    return pl.pallas_call(
        pack_kernel,
        grid=(count,),
        in_specs=[
            pl.BlockSpec((1, rows, width), lambda i: (i, 0, 0)),
            pl.BlockSpec((1, more, width), lambda i: (i, 0, 0)),
            pl.BlockSpec(memory_space=pl.ANY),
        ],
        out_specs=pl.BlockSpec((1, rows + more, width), lambda i: (i, 0, 0)),
        out_shape=jax.ShapeDtypeStruct((count, rows + more, width), first.dtype),
        compiler_params=pltpu.CompilerParams(vmem_limit_bytes=VMEM_LIMIT),
        name="pack",
    )(first, second, after)


def pack_last_kernel(proj_terms, qkv_terms, after, out):
    half = proj_terms.shape[2] // 2
    cols = qkv_terms.shape[2]
    folded = jnp.concatenate([proj_terms[0, :, :half], proj_terms[0, :, half:]], axis=0)
    out[0, :, :cols] = qkv_terms[0]
    out[0, :, cols:] = folded.astype(BF)


def pack_last(proj_terms, qkv_terms, after):
    count, half, width = proj_terms.shape
    _, rows, cols = qkv_terms.shape
    return pl.pallas_call(
        pack_last_kernel,
        grid=(count,),
        in_specs=[
            pl.BlockSpec((1, half, width), lambda i: (i, 0, 0)),
            pl.BlockSpec((1, rows, cols), lambda i: (i, 0, 0)),
            pl.BlockSpec(memory_space=pl.ANY),
        ],
        out_specs=pl.BlockSpec((1, rows, width // 2 + cols), lambda i: (i, 0, 0)),
        out_shape=jax.ShapeDtypeStruct((count, rows, width // 2 + cols), BF),
        compiler_params=pltpu.CompilerParams(vmem_limit_bytes=VMEM_LIMIT),
        name="pack_last",
    )(proj_terms, qkv_terms, after)


def token_grad_kernel(per, *refs):
    pairs, (tokens, cotangent, scale, gate) = refs[:12], refs[12:16]
    output, grad_tokens, d_shift, d_scale, d_gate = refs[-5:]
    early = pl.program_id(0) < per

    def pick(i):
        return jnp.where(early, pairs[2 * i][0].astype(F32), pairs[2 * i + 1][0].astype(F32))

    grad = pick(0) + pick(1)
    normed, inv_std = ln_parts(tokens[0].astype(F32))
    grad_tokens[0] = pick(2) + ln_backward(grad * (1.0 + scale[0]), normed, inv_std)
    mlp_out = pick(3) + pick(4)
    output[0] = (pick(5) + gate[0] * mlp_out).astype(BF)

    @pl.when(pl.program_id(1) == 0)
    def _():
        d_shift[...] = jnp.zeros_like(d_shift)
        d_scale[...] = jnp.zeros_like(d_scale)
        d_gate[...] = jnp.zeros_like(d_gate)

    d_shift[0] += jnp.sum(grad, axis=0, keepdims=True)
    d_scale[0] += jnp.sum(grad * normed, axis=0, keepdims=True)
    d_gate[0] += jnp.sum(cotangent[0].astype(F32) * mlp_out, axis=0, keepdims=True)


def token_grad(pairs, tokens, cotangent, scale, gate, after):
    lat, tok, width = tokens.shape
    per = lat // 2
    chunk = min(tok, 128)
    early = pl.BlockSpec((1, chunk, width), lambda i, c: (jnp.minimum(i, per - 1), c, 0))
    late = pl.BlockSpec((1, chunk, width), lambda i, c: (jnp.maximum(i, per) - per, c, 0))
    block = pl.BlockSpec((1, chunk, width), lambda i, c: (i, c, 0))
    row = pl.BlockSpec((1, 1, width), lambda i, c: (i, 0, 0))
    row_shape = jax.ShapeDtypeStruct((lat, 1, width), F32)
    return pl.pallas_call(
        partial(token_grad_kernel, per),
        grid=(lat, tok // chunk),
        in_specs=[early, late] * 6 + [block, block, row, row, pl.BlockSpec(memory_space=pl.ANY)],
        out_specs=[block, block, row, row, row],
        out_shape=[
            jax.ShapeDtypeStruct((lat, tok, width), BF),
            jax.ShapeDtypeStruct((lat, tok, width), F32),
            row_shape,
            row_shape,
            row_shape,
        ],
        compiler_params=pltpu.CompilerParams(vmem_limit_bytes=VMEM_LIMIT),
        name="token_grad",
    )(*[v for pair in pairs for v in pair], tokens, cotangent, scale, gate, after)


def place_last_kernel(rows, owners, received, out_qkv, out_proj):
    cols = received.shape[2]
    half = rows // 2
    for i in range(3):
        out_qkv[:, i * cols : (i + 1) * cols] = received[owners[i], :rows].astype(F32)
    for core in range(2):
        total = received[core, rows:].astype(F32)
        for j in range(core + 2, received.shape[0], 2):
            total = total + received[j, rows:].astype(F32)
        out_proj[core * half : (core + 1) * half] = total


def place_last(received, rows, seq):
    count, _, cols = received.shape
    owners = (3 * seq + jnp.arange(3, dtype=jnp.int32)) % count
    vmem = pl.BlockSpec(memory_space=pltpu.VMEM)
    return pl.pallas_call(
        partial(place_last_kernel, rows),
        in_specs=[pl.BlockSpec(memory_space=pltpu.SMEM), vmem],
        out_specs=[vmem, vmem],
        out_shape=[
            jax.ShapeDtypeStruct((rows, 3 * cols), F32),
            jax.ShapeDtypeStruct((rows, cols), F32),
        ],
        compiler_params=pltpu.CompilerParams(vmem_limit_bytes=VMEM_LIMIT),
        name="place_last",
    )(owners, received)


def on_device(tokens, conditioning, w_mod, b_mod, w_qkv, w_proj, w_fc1, b_fc1, w_fc2, cotangent):
    lat, tok, width = tokens.shape
    seq_n = lax.axis_size("seq")
    dp_n = lax.axis_size("dp")
    seq = lax.axis_index("seq")
    dp = lax.axis_index("dp")
    core = seq % 2
    heads_here = HEADS // seq_n
    cols = heads_here * HEAD_DIM
    seq_len = tok * seq_n
    rows = w_qkv.shape[0]
    hid_here = w_fc2.shape[0] // seq_n
    hid = hid_here * dp_n
    groups = 2
    per = lat // groups
    own = per * tok

    cond_silu, silu_back = jax.vjp(jax.nn.silu, conditioning)
    cond_act = cond_silu.astype(BF)
    bias_here = lax.dynamic_slice(b_fc1, (seq * hid_here,), (hid_here,))
    small = jnp.concatenate([cond_act.reshape(lat * width), bias_here])
    small = dp_exchange(jnp.broadcast_to(small[None], (dp_n, lat * width + hid_here)))
    cond_all = small[:, : lat * width].reshape(dp_n * lat, width)
    fc1_bias = small[:, lat * width :].reshape(hid).astype(F32)
    cond_rows = lax.dynamic_slice(cond_all, (0, dp * rows), (dp_n * lat, rows))
    mod_terms = matmul(cond_rows, w_mod)
    piece = b_mod.shape[0]
    mod_terms = lax.dynamic_update_slice(
        mod_terms,
        lax.dynamic_slice(mod_terms, (0, dp * piece), (dp_n * lat, piece))
        + b_mod.astype(F32)[None],
        (0, dp * piece),
    )
    modulation = jnp.sum(dp_exchange(mod_terms.reshape(dp_n, lat, 6 * width)), axis=0)

    tok_slots = seq_gather(tokens)
    cot_slots = seq_gather(cotangent)

    qkv_here = jnp.concatenate(
        [lax.dynamic_slice(w_qkv, (0, t * width + seq * cols), (rows, cols)) for t in range(3)],
        axis=1,
    )
    qkv = dp_gather(qkv_here, lambda d: d).reshape(width, 3 * cols)
    half = rows // 2
    fc1_here = jnp.concatenate(
        [
            lax.dynamic_slice(w_fc1, (0, (d * seq_n + seq) * hid_here), (rows, hid_here))
            for d in range(dp_n)
        ],
        axis=1,
    )
    fc2_here = lax.dynamic_slice(w_fc2, (seq * hid_here, 0), (hid_here, width))
    proj_here = lax.dynamic_slice(w_proj, (core * half, 0), (half, width))
    together = hid == width
    proj_mine = lax.all_gather(proj_here, "dp", axis=0)
    if together:
        joined = lax.all_gather(jnp.concatenate([fc1_here, fc2_here]), "dp", axis=0)
        fc1, fc2 = (joined, rows, 0), (joined, hid_here, 1)
    else:
        fc1 = (lax.all_gather(fc1_here, "dp", axis=0, tiled=True)[None], width, 0)
        fc2 = (lax.all_gather(fc2_here, "dp", axis=0, tiled=True)[None], hid, 0)

    def part(g):
        return slice(g * per, (g + 1) * per)

    shift_attn, scale_attn, gate_attn, shift_mlp, scale_mlp, gate_mlp = [
        [modulation[part(g), None, i * width : (i + 1) * width] for g in range(groups)]
        for i in range(6)
    ]
    token_values = [tokens[part(g)].astype(F32) for g in range(groups)]
    proj_other = hop(proj_mine, "seq", 1)
    proj = jnp.where(
        core == 0,
        jnp.stack([proj_mine, proj_other], axis=1),
        jnp.stack([proj_other, proj_mine], axis=1),
    ).reshape(seq_n, cols, width)

    def by_place(blocks):
        return jnp.concatenate(
            [lax.dynamic_index_in_dim(blocks, seq ^ j, 0, keepdims=False) for j in range(seq_n)]
        )

    proj = by_place(proj)

    normed_all, packed, mixed, log_sums, attended = [], [], [], [], []
    attn_out, resid_mid, normed_mlp = [], [], []
    for g in range(groups):
        normed, rows_packed = qkv_forward(tok_slots, g, per, shift_attn[g], scale_attn[g], qkv)
        normed_all.append(normed.reshape(per * seq_len, width))
        packed.append(rows_packed.reshape(per, seq_len, 3 * cols))
        out, log_sum = attention(
            packed[g], normed_mlp + cot_slots[-1:] if g else [], heads_here
        )
        mixed.append(out)
        log_sums.append(log_sum)
        out = out.reshape(per, seq_n, tok, cols)
        attended.append(
            jnp.concatenate(seq_exchange([out[:, j] for j in range(seq_n)]), axis=2).reshape(
                own, width
            )
        )
        attn_out.append(matmul(attended[g], proj).reshape(per, tok, width))
        resid_mid.append(token_values[g] + gate_attn[g] * attn_out[g])
        normed_mlp.append(
            (ln_parts(resid_mid[g])[0] * (1.0 + scale_mlp[g]) + shift_mlp[g]).astype(BF)
        )

    grad_fc1 = grad_fc2 = grad_bias1 = 0.0
    d_near, activated = [], []
    for g in range(groups):
        x_all, d_mlp, active, d_hidden, terms, d_bias = mlp(
            seq_gather(normed_mlp[g]), cot_slots, g, gate_mlp[g], fc1, fc1_bias[None], fc2,
            [near[1] for near in d_near],
        )
        d_near.append(seq_near([terms[:, j].astype(F32) for j in range(seq_n)]))
        activated.append(active)
        flat = per * seq_len
        grad_fc2 = grad_fc2 + matmul_tn(active.reshape(flat, hid), d_mlp.reshape(flat, width))
        grad_fc1 = grad_fc1 + matmul_tn(x_all.reshape(flat, width), d_hidden.reshape(flat, hid))
        grad_bias1 = grad_bias1 + d_bias[0]
    grad_fc1 = grad_fc1.astype(BF).reshape(dp_n, rows, hid)
    grad_fc2 = grad_fc2.astype(BF).reshape(dp_n, hid_here, width)
    if together:
        grad_fc = pack(grad_fc1, grad_fc2, d_near[-1][1])
        sum_fc = lax.psum_scatter(grad_fc, "dp", scatter_dimension=0)
        sum_fc1, sum_fc2 = sum_fc[:rows], sum_fc[rows:]
    else:
        grad_fc = grad_fc1
        sum_fc1 = lax.psum_scatter(grad_fc1, "dp", scatter_dimension=0)
        sum_fc = sum_fc2 = lax.psum_scatter(grad_fc2, "dp", scatter_dimension=0)

    def stacked(terms):
        return jnp.concatenate(terms)

    d_shift_mlp, d_scale_mlp, d_gate_attn, d_resid, d_attn, d_attended = ([] for _ in range(6))
    d_mixed = []
    for g in range(groups):
        outs = resid_grad(
            seq_far(*d_near[g]), resid_mid[g], attn_out[g], cotangent, g, scale_mlp[g],
            gate_attn[g], proj, d_attended[0] if g else grad_fc, seq_n,
        )
        d_resid.append(outs[0])
        d_attn.append(outs[1].reshape(own, width))
        d_shift_mlp.append(outs[2][:, 0])
        d_scale_mlp.append(outs[3][:, 0])
        d_gate_attn.append(outs[4][:, 0])
        d_attended.append(outs[5])
        d_mixed.append(seq_exchange(outs[5:]))
    mlp_terms, mlp_near = [], []
    for g in range(groups):
        terms = mlp_out_terms(activated[g], fc2, d_attended[-1])
        mlp_terms.append(terms)
        mlp_near.append(seq_near([terms[:, j].astype(F32) for j in range(seq_n)]))
    grad_proj = by_place(
        matmul_tn(stacked(attended), stacked(d_attn)).astype(BF).reshape(seq_n, cols, width)
    ).reshape(dp_n, 2, half, width)
    proj_sent = hop(
        lax.dynamic_index_in_dim(grad_proj, 1 - core, axis=1, keepdims=False), "seq", 1
    )
    proj_terms = lax.dynamic_index_in_dim(grad_proj, core, axis=1, keepdims=False).astype(F32)
    proj_terms = proj_terms + proj_sent.astype(F32)

    d_packed, d_first, first_terms = [], [], []
    for g in range(groups):
        grads, terms = attention_grad(
            packed[g], mixed[g], log_sums[g], d_mixed[g], qkv,
            first_terms + [near[1] for near in mlp_near] + [proj_terms]
            if g
            else [d_attended[-1]] + mlp_terms,
            heads_here,
        )
        d_packed.append(grads.reshape(per * seq_len, 3 * cols))
        first_terms.append(terms)
        terms = terms.reshape(per, seq_n, tok, width)
        d_first.append(seq_near([terms[:, j].astype(F32) for j in range(seq_n)]))
    grad_qkv = matmul_tn(stacked(normed_all), stacked(d_packed)).astype(BF)
    last = pack_last(proj_terms, grad_qkv.reshape(dp_n, rows, 3 * cols), sum_fc)
    sum_last = lax.psum_scatter(last, "dp", scatter_dimension=0)
    sum_qkv, sum_proj = sum_last[:, : 3 * cols], sum_last[:, 3 * cols :]
    pairs = [
        [near[0] for near in d_first],
        [far_hop(near[1]) for near in d_first],
        d_resid,
        [near[0] for near in mlp_near],
        [far_hop(near[1]) for near in mlp_near],
        resid_mid,
    ]
    output, grad_tokens, d_shift_attn, d_scale_attn, d_gate_mlp = token_grad(
        pairs, tokens, cotangent, modulation[:, None, width : 2 * width],
        modulation[:, None, 5 * width :], last,
    )

    mod_part = jnp.concatenate(
        [d_shift_attn[:, 0], d_scale_attn[:, 0], stacked(d_gate_attn)]
        + [stacked(d_shift_mlp), stacked(d_scale_mlp), d_gate_mlp[:, 0]],
        axis=1,
    )
    bit = 1
    while bit < seq_n:
        mod_part = mod_part + hop(mod_part, "seq", bit)
        bit *= 2
    d_mod = dp_exchange(jnp.broadcast_to(mod_part.astype(BF)[None], (dp_n, lat, 6 * width)))
    d_mod = d_mod.reshape(dp_n * lat, 6 * width)
    share = 6 * width // (dp_n * seq_n)
    mod_cols = lax.dynamic_slice(d_mod, (0, (dp * seq_n + seq) * share), (dp_n * lat, share))
    grad_wmod = matmul_tn(cond_all, mod_cols)
    grad_bmod = jnp.sum(mod_cols.astype(F32), axis=0)
    back = jnp.concatenate(
        [
            matmul_nt(d_mod, w_mod).reshape(dp_n, lat * rows),
            grad_bias1.reshape(dp_n, hid_here),
        ],
        axis=1,
    )
    back = dp_exchange(back)
    d_cond = back[:, : lat * rows].reshape(dp_n, lat, rows)
    (grad_cond,) = silu_back(d_cond.transpose(1, 0, 2).reshape(lat, width))
    bias_out = jnp.sum(back[:, lat * rows :], axis=0)

    def to_owner(blocks):
        return lax.all_to_all(blocks, "seq", 0, 0, tiled=True).astype(F32)

    share = width // seq_n
    fc2_blocks = sum_fc2.reshape(hid_here, seq_n, share).transpose(1, 0, 2)
    fc1_blocks = sum_fc1.reshape(rows, seq_n, hid // seq_n).transpose(1, 0, 2)
    if together:
        received = to_owner(jnp.concatenate([fc1_blocks, fc2_blocks], axis=1))
        out_fc1, out_fc2 = received[:, :rows], received[:, rows:]
    else:
        out_fc1, out_fc2 = to_owner(fc1_blocks), to_owner(fc2_blocks)
    out_fc2 = out_fc2.reshape(seq_n * hid_here, share)
    out_fc1 = out_fc1.reshape(seq_n, rows, dp_n // seq_n, hid_here).transpose(1, 2, 0, 3)
    out_fc1 = out_fc1.reshape(rows, hid)
    proj_blocks = sum_proj.reshape(2, half, seq_n // 2, share).transpose(0, 2, 1, 3)
    proj_blocks = proj_blocks.reshape(seq_n, half, share)
    qkv_thirds = sum_qkv.reshape(rows, 3, cols).transpose(1, 0, 2)
    qkv_blocks = jnp.stack(
        [
            lax.dynamic_index_in_dim(
                qkv_thirds, jnp.minimum((3 * to - seq + seq_n - 1) // seq_n, 2), 0, keepdims=False
            )
            for to in range(seq_n)
        ]
    )
    received = lax.all_to_all(
        jnp.concatenate([qkv_blocks, proj_blocks], axis=1), "seq", 0, 0, tiled=True
    )
    out_qkv, out_proj = place_last(received, rows, seq)
    return (
        output,
        grad_tokens,
        grad_cond,
        grad_wmod,
        grad_bmod,
        out_qkv,
        out_proj,
        out_fc1,
        bias_out,
        out_fc2,
    )


def solution(mesh):
    placed = (
        P("dp", "seq", None),
        P("dp", None),
        P("dp", None),
        P("dp"),
        P("dp", None),
        P("dp", None),
        P("dp", None),
        P("dp"),
        P("dp", None),
        P("dp", "seq", None),
    )
    return jax.shard_map(
        on_device,
        mesh=mesh,
        in_specs=placed,
        out_specs=(
            P("dp", "seq", None),
            P("dp", "seq", None),
            P("dp", None),
            P(None, ("dp", "seq")),
            P(("dp", "seq")),
            P("dp", "seq"),
            P("dp", "seq"),
            P("dp", "seq"),
            P(("dp", "seq")),
            P("dp", "seq"),
        ),
        check_vma=False,
    )
```
